128 devices in a mesh: section: 2 (over y_lo), tensor: 2 (over y_hi), wide: 32 (over x, z, core).
Axes of the slice: x: 4, y: 4 (y_hi: 2, y_lo: 2; y = y_hi * 2 + y_lo), z: 4, core: 2. Of those that a mesh axis runs over, the one named last changes fastest.
Arguments:
- x_in: bfloat16 [2, 4096, 1024], P(None, ('tensor', 'wide')), may hold values from -6 to 6
- out_cot: bfloat16 [2, 4096, 1024], P(None, ('tensor', 'wide')), may hold values from -6 to 6
- image_ids: int32 [2, 4096], replicated, may hold values from 0 to 2, as said below
- w_qkv: bfloat16 [2, 1024, 3, 1024], P('section', 'wide', None, 'tensor'), may hold values from -1 to 1, as said below
- w_out: bfloat16 [2, 1024, 1024], P('section', ('tensor', 'wide')), may hold values from -0.5 to 0.5
- w_fc1: bfloat16 [2, 1024, 4096], P('section', 'wide', 'tensor'), may hold values from -0.1875 to 0.1875
- w_fc2: bfloat16 [2, 4096, 1024], P('section', ('tensor', 'wide')), may hold values from -0.09375 to 0.09375
- gains: bfloat16 [2, 2, 1024], P('section', None, 'wide'), may hold values from 0.5 to 1.5
- shifts: bfloat16 [2, 4, 1024], P('section', None, 'wide'), may hold values from -1.5 to 1.5
- layer_scales: bfloat16 [2, 2, 1024], P('section', None, 'wide'), may hold values from 0.5 to 1.5
- qv_bias: bfloat16 [2, 2, 1024], P('section', None, ('tensor', 'wide')), may hold values from -1.5 to 1.5
- fc1_bias: bfloat16 [2, 4096], P('section', ('tensor', 'wide')), may hold values from -1.5 to 1.5
Outputs:
- section_outputs: bfloat16 [2, 2, 4096, 1024], P('section', None, ('tensor', 'wide'))
- input_grads: float32 [2, 2, 4096, 1024], P('section', None, ('tensor', 'wide'))
- g_w_qkv: float32 [2, 1024, 3, 1024], P('section', 'wide', None, 'tensor')
- g_w_out: float32 [2, 1024, 1024], P('section', ('tensor', 'wide'))
- g_w_fc1: float32 [2, 1024, 4096], P('section', 'wide', 'tensor')
- g_w_fc2: float32 [2, 4096, 1024], P('section', ('tensor', 'wide'))
- g_gains: float32 [2, 2, 1024], P('section', None, 'wide')
- g_shifts: float32 [2, 4, 1024], P('section', None, 'wide')
- g_layer_scales: float32 [2, 2, 1024], P('section', None, 'wide')
- g_qv_bias: float32 [2, 2, 1024], P('section', None, ('tensor', 'wide'))
- g_fc1_bias: float32 [2, 4096], P('section', ('tensor', 'wide'))
The draws below stay inside these ranges and needn't reach their ends.
Inputs may be any that keep to these rules, and one draw needn't show every extreme that they name: `image_ids`: each micro-batch packs three images in order: image 0 ends and image 2 begins at boundaries that lie within 4096/12 tokens of 4096/3 and of 2 * 4096/3; image 1 lies between. `w_qkv`: projection weights of order 1024^-0.5.
All inputs are finite; a program needn't handle non-finite values.
Results may differ from the reference program's by a relative error of at most 0.035.
Values may be sent and summed in bfloat16 or wider, within the bound.
No kernel may reach another device: no remote copies, remote signals or barrier semaphores. Data moves between devices by JAX's collectives and lax.ppermute only.
A program may use at most 192 MiB of HBM per device.

```python
import math
import jax
import jax.numpy as jnp
from jax import lax

D = 1024
HEADS = 16
HEAD = 64
FF = 4096
MICRO = 2
MBTOK = 4096


def draw_image_ids(key, part):
    key = jax.random.fold_in(key, 11)
    first_key, last_key = jax.random.split(key)
    jitter = MBTOK // 12
    first_ends = MBTOK // 3 + jax.random.randint(first_key, (MICRO, 1), -jitter, jitter + 1)
    last_starts = 2 * MBTOK // 3 + jax.random.randint(last_key, (MICRO, 1), -jitter, jitter + 1)
    places = jnp.arange(MBTOK, dtype=jnp.int32)[None, :]
    return (places >= first_ends).astype(jnp.int32) + (places >= last_starts).astype(jnp.int32)


def draw_w_qkv(key, part):
    key = jax.random.fold_in(key, 23)
    shape = (2, D, 3, D)
    base = jnp.clip(jax.random.normal(key, shape, jnp.float32), -4.0, 4.0)
    factors = jnp.array([1.4142135, 1.4142135, 1.0], jnp.float32)
    return (base * factors[None, None, :, None] * D ** (-0.5)).astype(jnp.bfloat16)


def shard_levels(key, shape, pieces, least, top_value):
    def one(axis_at, parts):
        steps = jax.random.uniform(jax.random.fold_in(jax.random.fold_in(key, 6), axis_at), (parts,), jnp.float32, least / len(pieces), top_value / len(pieces))
        return jnp.repeat(jnp.exp(steps), shape[axis_at] // parts).reshape((-1,) + (1,) * (len(shape) - axis_at - 1))

    factor_of = one(*pieces[0])
    for cut in pieces[1:]:
        factor_of = factor_of * one(*cut)
    return factor_of


def gaussian(own_key, dims, deviation, limit, cuts=(), kind=jnp.bfloat16):
    drawn = jax.random.normal(own_key, dims, jnp.float32) * deviation
    if len(cuts) > 0:
        drawn = shard_levels(own_key, dims, cuts, -0.22, 0.18) * drawn
    return jnp.clip(drawn, min=-limit, max=limit).astype(kind)


def setup_inputs(seed: int = 0) -> dict:
    splits = jax.random.split(jax.random.key(seed), 13)
    x_in = gaussian(splits[0], (MICRO, MBTOK, D), 1.0, 6.0, ((1, 64),))
    out_cot = gaussian(splits[1], (MICRO, MBTOK, D), 1.0, 6.0, ((1, 64),))
    image_ids = draw_image_ids(jax.random.fold_in(splits[12], 71), 0)
    w_qkv = draw_w_qkv(jax.random.fold_in(splits[12], 71), 0)
    w_out = gaussian(splits[4], (2, D, D), (D // 8) ** -0.5, 0.5, ((0, 2), (1, 64)))
    w_fc1 = gaussian(splits[5], (2, D, FF), D ** -0.5, 0.1875, ((0, 2), (1, 32), (2, 2)))
    w_fc2 = gaussian(splits[6], (2, FF, D), FF ** -0.5, 0.09375, ((0, 2), (1, 64)))
    gains = jnp.clip(1.0 + 0.1 * jax.random.normal(splits[7], (2, 2, D), jnp.float32), 0.5, 1.5).astype(jnp.bfloat16)
    shifts = gaussian(splits[8], (2, 4, D), 0.3, 1.5, ((0, 2), (2, 32)))
    layer_scales = jnp.clip(jnp.exp(math.log(1.5) - 1.0986123 * jax.random.uniform(splits[9], (2, 2, D), jnp.float32) ** shard_levels(splits[9], (2, 2, D), ((0, 2), (2, 32)), -0.2, 0.2)), 0.5, 1.5).astype(jnp.bfloat16)
    qv_bias = gaussian(splits[10], (2, 2, D), 0.3, 1.5, ((0, 2), (2, 64)))
    fc1_bias = gaussian(splits[11], (2, FF), 0.3, 1.5, ((0, 2), (1, 64)))
    return {"x_in": x_in, "out_cot": out_cot, "image_ids": image_ids, "w_qkv": w_qkv, "w_out": w_out, "w_fc1": w_fc1, "w_fc2": w_fc2, "gains": gains, "shifts": shifts, "layer_scales": layer_scales, "qv_bias": qv_bias, "fc1_bias": fc1_bias}


EPS = 1e-06
NEG_FILL = -1e+30
ROOT_HALF = 0.7071067811865476
HIGHEST = lax.Precision.HIGHEST

@jax.custom_vjp
def low(v):
    return lax.optimization_barrier(v.astype(jnp.bfloat16)).astype(jnp.float32)

@jax.custom_vjp
def low_back(v):
    return v

def low_keep(v):
    return (low(v), None)

def low_pass(kept, grad):
    return (grad,)

def back_keep(v):
    return (v, None)

def back_low(kept, grad):
    return (low(grad),)
low.defvjp(low_keep, low_pass)
low_back.defvjp(back_keep, back_low)

def matmul_high(left, right):
    return jnp.dot(left, right, preferred_element_type=jnp.float32, precision=HIGHEST)

def layer_norm(rows_in, gain_row, shift_row):
    centre = lax.optimization_barrier(jnp.mean(rows_in, axis=-1, keepdims=True))
    centred = rows_in - centre
    spread = lax.optimization_barrier(jnp.mean(centred * centred, axis=-1, keepdims=True))
    return centred * lax.rsqrt(spread + EPS) * gain_row + shift_row

def gelu_exact(pre_act):
    return 0.5 * pre_act * (1.0 + lax.erf(pre_act * ROOT_HALF))

def attention(queries, key_rows, value_rows, seg_ids):
    tokens_all = queries.shape[0]
    block_rows = min(512, tokens_all)
    score_scale = HEAD ** (-0.5)
    query_blocks = queries.reshape(tokens_all // block_rows, block_rows, HEADS, HEAD)
    id_blocks = seg_ids.reshape(tokens_all // block_rows, block_rows)

    def one_block(block_pair):
        query_part, id_part = block_pair
        scores = low_back(jnp.einsum('qhd,khd->hqk', query_part, key_rows, precision=HIGHEST) * score_scale)
        same_image = id_part[:, None] == seg_ids[None, :]
        masked = jnp.where(same_image[None], scores, NEG_FILL)
        highest = lax.optimization_barrier(jnp.max(masked, axis=-1, keepdims=True))
        expo_vals = jnp.exp(masked - highest)
        probability = expo_vals / lax.optimization_barrier(jnp.sum(expo_vals, axis=-1, keepdims=True))
        return jnp.einsum('hqk,khd->qhd', low(probability), value_rows, precision=HIGHEST)
    mixture = lax.map(jax.checkpoint(one_block), (query_blocks, id_blocks))
    return mixture.reshape(tokens_all, HEADS * HEAD)

def block_layer(rows_in, seg_ids, wqkv_one, wout_one, wone_one, wtwo_one, gain_rows, shift_rows, scale_rows, qv_rows, fc1_row):
    tokens_all = rows_in.shape[0]
    normed = low(layer_norm(rows_in, gain_rows[0], shift_rows[0]))
    queries = low(low_back(matmul_high(normed, wqkv_one[:, 0]) + qv_rows[0]))
    key_rows = low(low_back(matmul_high(normed, wqkv_one[:, 1])))
    value_rows = low(low_back(matmul_high(normed, wqkv_one[:, 2]) + qv_rows[1]))
    head_shape = (tokens_all, HEADS, HEAD)
    mixture = attention(queries.reshape(head_shape), key_rows.reshape(head_shape), value_rows.reshape(head_shape), seg_ids)
    mixture = low(low_back(mixture))
    middle = rows_in + scale_rows[0] * (low_back(matmul_high(mixture, wout_one)) + shift_rows[1])
    second = low(layer_norm(middle, gain_rows[1], shift_rows[2]))
    hidden_pre = low_back(matmul_high(second, wone_one) + fc1_row)
    hidden = low(gelu_exact(hidden_pre))
    return middle + scale_rows[1] * (low_back(matmul_high(hidden, wtwo_one)) + shift_rows[3])

def reference(x_in, out_cot, image_ids, w_qkv, w_out, w_fc1, w_fc2, gains, shifts, layer_scales, qv_bias, fc1_bias):
    floats = tuple((array_in.astype(jnp.float32) for array_in in (x_in, w_qkv, w_out, w_fc1, w_fc2, gains, shifts, layer_scales, qv_bias, fc1_bias)))
    probe = jnp.zeros(x_in.shape, jnp.float32)

    def forward_pass(x_rows, probe_rows, wqkv_all, wout_all, wone_all, wtwo_all, gain_all, shift_all, scale_all, qv_all, fc1_all):
        firsts = []
        seconds = []
        for micro_idx in range(MICRO):
            seg_ids = image_ids[micro_idx]
            first_out = block_layer(x_rows[micro_idx], seg_ids, wqkv_all[0], wout_all[0], wone_all[0], wtwo_all[0], gain_all[0], shift_all[0], scale_all[0], qv_all[0], fc1_all[0])
            second_in = low_back(low(first_out)) + probe_rows[micro_idx]
            second_out = block_layer(second_in, seg_ids, wqkv_all[1], wout_all[1], wone_all[1], wtwo_all[1], gain_all[1], shift_all[1], scale_all[1], qv_all[1], fc1_all[1])
            firsts.append(first_out)
            seconds.append(second_out)
        return (jnp.stack(seconds), jnp.stack(firsts))
    finals, pullback, firsts = jax.vjp(forward_pass, floats[0], probe, *floats[1:], has_aux=True)
    grads = pullback(out_cot.astype(jnp.float32))
    section_outputs = jnp.stack([firsts, finals]).astype(jnp.bfloat16)
    input_grads = jnp.stack([grads[0], grads[1]])
    return (section_outputs, input_grads, grads[2], grads[3], grads[4], grads[5], grads[6], grads[7], grads[8], grads[9], grads[10])
```

```python
import jax
import jax.numpy as jnp
from jax import lax
from jax.experimental import pallas as pl
from jax.experimental.pallas import tpu as pltpu
from jax.sharding import PartitionSpec as P

HEAD = 64
EPS = 1e-06
NEG_FILL = -1e30
ROOT_HALF = 0.7071067811865476
INV_ROOT_TAU = 0.3989422804014327
SCALE = HEAD ** (-0.5)
BF = jnp.bfloat16
F32 = jnp.float32
MIB = 1024 * 1024

ROWS = 64
BOTH = 128
WIDE = 32
HEADS_DEV = 8
QUARTERS = 4
HALF_W = 512
MODEL = 1024
HIDDEN = 2048
SEND_ROWS = 144
BLOCKS_Q = 4
CHUNKS = 8


def params(limit=56):
    return pltpu.CompilerParams(vmem_limit_bytes=limit * MIB)


def cost(flops, moved):
    return pl.CostEstimate(flops=int(flops), bytes_accessed=int(moved), transcendentals=0)


def whole(shape):
    count = len(shape)
    return pl.BlockSpec(shape, lambda *g: (0,) * count)


def swap(block, axis):
    return lax.ppermute(block, axis, [(0, 1), (1, 0)])


def nt(left, right):
    return lax.dot_general(left, right, (((1,), (1,)), ((), ())), preferred_element_type=F32)


def tn(left, right):
    return lax.dot_general(left, right, (((0,), (0,)), ((), ())), preferred_element_type=F32)


def nn(left, right):
    return jnp.dot(left, right, preferred_element_type=F32)


def low_lanes(shape):
    return lax.broadcasted_iota(jnp.int32, shape, len(shape) - 1) < HEAD


def turn(tile):
    return pltpu.roll(tile, HEAD, 1)


def pack_heads(tile, out_ref, pair, row0):
    rolled = turn(tile)
    for quarter in range(QUARTERS):
        first = slice(quarter * 32, quarter * 32 + 16)
        second = slice(quarter * 32 + 16, quarter * 32 + 32)
        mask = low_lanes((16, 128))
        even = jnp.where(mask, tile[first], rolled[second])
        odd = jnp.where(mask, rolled[first], tile[second])
        out_ref[(2 * pair) * QUARTERS + quarter, row0 : row0 + 16, :] = even.astype(BF)
        out_ref[(2 * pair + 1) * QUARTERS + quarter, row0 : row0 + 16, :] = odd.astype(BF)


def unpack_heads(in_ref, row0):
    mask = low_lanes((16, 128))
    columns = []
    for pair in range(HEADS_DEV // 2):
        pieces = []
        for quarter in range(QUARTERS):
            even = in_ref[(2 * pair) * QUARTERS + quarter, row0 : row0 + 16, :].astype(F32)
            odd = in_ref[(2 * pair + 1) * QUARTERS + quarter, row0 : row0 + 16, :].astype(F32)
            pieces.append(jnp.where(mask, even, turn(odd)))
            pieces.append(jnp.where(mask, turn(even), odd))
        columns.append(jnp.concatenate(pieces, axis=0))
    return jnp.concatenate(columns, axis=1)


def qkv_kernel(own_ref, other_ref, weight_ref, bias_ref, out_ref):
    rows = jnp.concatenate([own_ref[...], other_ref[...]], axis=0)

    def project(which):
        weight = weight_ref[:, which * 32 : which * 32 + 32, :].reshape(MODEL, HALF_W)
        return nn(rows, weight)

    queries = project(0) + bias_ref[0:1, :]
    keys = project(1)
    values = project(2) + bias_ref[1:2, :]
    mask = low_lanes((BOTH, 128))
    for pair in range(HEADS_DEV // 2):
        columns = slice(pair * 128, pair * 128 + 128)
        key_tile, value_tile, query_tile = keys[:, columns], values[:, columns], queries[:, columns]
        even = jnp.where(mask, key_tile, turn(value_tile)).astype(BF)
        odd = jnp.where(mask, turn(key_tile), value_tile).astype(BF)
        for quarter in range(QUARTERS):
            out_ref[(2 * pair) * QUARTERS + quarter, 0:BOTH, :] = even
            out_ref[(2 * pair + 1) * QUARTERS + quarter, 0:BOTH, :] = odd
        pack_heads(query_tile, out_ref, pair, BOTH)


def qkv_call(own, other, weight, bias):
    return pl.pallas_call(
        qkv_kernel,
        grid=(1,),
        in_specs=[whole((ROWS, MODEL)), whole((ROWS, MODEL)), whole((WIDE, 96, HALF_W)), whole((2, HALF_W))],
        out_specs=whole((WIDE, SEND_ROWS, 128)),
        out_shape=jax.ShapeDtypeStruct((WIDE, SEND_ROWS, 128), BF),
        compiler_params=params(),
        cost_estimate=cost(2 * BOTH * MODEL * 1536, 5e6),
    )(own, other, weight, bias)


def query_tiles(packed):
    mask = low_lanes((128, 128))
    return jnp.concatenate(
        [jnp.where(mask, packed, 0.0), jnp.where(mask, turn(packed), 0.0)], axis=0
    )


def key_chunk(recv_ref, chunk):
    half, group = chunk // 4, chunk % 4
    block = recv_ref[group * 8 : group * 8 + 8, half * ROWS : half * ROWS + ROWS, :]
    return block.reshape(512, 128)


def lane_tiles(fn, block):
    return fn(fn(block[:, 0:128], block[:, 128:256]), fn(block[:, 256:384], block[:, 384:512]))


def attend_kernel(
    flag_ref, recv_ref, key_id_ref, query_id_ref, out_ref, keep_ref, lse_ref,
    score_ref, top_ref, total_ref, acc_ref,
):
    at = pl.program_id(0)
    packed = recv_ref[pl.ds(at * 8, 8), BOTH : BOTH + 16, :].astype(F32).reshape(128, 128)
    queries = (query_tiles(packed) * SCALE).astype(BF)
    query_ids = query_id_ref[0]
    top_ref[...] = jnp.full((256, 128), NEG_FILL, F32)
    total_ref[...] = jnp.zeros((256, 128), F32)
    acc_ref[...] = jnp.zeros((256, 128), F32)
    for chunk in range(CHUNKS):

        @pl.when(flag_ref[at, chunk] != 0)
        def _():
            scores = nt(queries, key_chunk(recv_ref, chunk))
            scores = jnp.where(query_ids == key_id_ref[chunk], scores, NEG_FILL)
            score_ref[chunk] = scores
            top_ref[...] = jnp.maximum(top_ref[...], lane_tiles(jnp.maximum, scores))

    top = jnp.max(top_ref[...], axis=1, keepdims=True)
    for chunk in range(CHUNKS):

        @pl.when(flag_ref[at, chunk] != 0)
        def _():
            expo = jnp.exp(score_ref[chunk] - top)
            total_ref[...] += lane_tiles(jnp.add, expo)
            acc_ref[...] += nn(expo.astype(BF), key_chunk(recv_ref, chunk))

    total = jnp.sum(total_ref[...], axis=1, keepdims=True)
    mixture = acc_ref[...] / total
    lse_ref[...] = top + jnp.log(total)
    mask = low_lanes((128, 128))
    joined = jnp.where(mask, turn(mixture[:128]), mixture[128:]).reshape(8, 16, 128)
    keep_ref[...] = joined
    out_ref[...] = joined.astype(BF)


def attend_call(flags, recv, key_ids, query_ids):
    return pl.pallas_call(
        attend_kernel,
        grid_spec=pltpu.PrefetchScalarGridSpec(
            num_scalar_prefetch=1,
            grid=(BLOCKS_Q,),
            in_specs=[
                pl.BlockSpec((WIDE, SEND_ROWS, 128), lambda i, f: (0, 0, 0)),
                pl.BlockSpec((CHUNKS, 1, 512), lambda i, f: (0, 0, 0)),
                pl.BlockSpec((1, 256, 1), lambda i, f: (i, 0, 0)),
            ],
            out_specs=[
                pl.BlockSpec((8, 16, 128), lambda i, f: (i, 0, 0)),
                pl.BlockSpec((8, 16, 128), lambda i, f: (i, 0, 0)),
                pl.BlockSpec((256, 1), lambda i, f: (i, 0)),
            ],
            scratch_shapes=[
                pltpu.VMEM((CHUNKS, 256, 512), F32),
                pltpu.VMEM((256, 128), F32),
                pltpu.VMEM((256, 128), F32),
                pltpu.VMEM((256, 128), F32),
            ],
        ),
        out_shape=[
            jax.ShapeDtypeStruct((WIDE, 16, 128), BF),
            jax.ShapeDtypeStruct((WIDE, 16, 128), F32),
            jax.ShapeDtypeStruct((1024, 1), F32),
        ],
        compiler_params=params(),
        cost_estimate=cost(4 * 1024 * 4096 * 256, 2e6),
    )(flags, recv, key_ids, query_ids)


def attend_back_kernel(
    flag_ref, recv_ref, grad_ref, keep_ref, lse_ref, key_id_ref, query_id_ref, out_ref,
    key_grad_ref, query_grad_ref,
):
    at = pl.program_id(0)

    @pl.when(at == 0)
    def _():
        key_grad_ref[...] = jnp.zeros((WIDE, BOTH, 128), F32)

    mask = low_lanes((128, 128))
    packed = recv_ref[pl.ds(at * 8, 8), BOTH : BOTH + 16, :].astype(F32).reshape(128, 128)
    queries = (query_tiles(packed) * SCALE).astype(BF)
    grads = grad_ref[...].astype(F32).reshape(128, 128)
    grad_tile = jnp.concatenate(
        [jnp.where(mask, 0.0, turn(grads)), jnp.where(mask, 0.0, grads)], axis=0
    ).astype(BF)
    product = grads * keep_ref[...].reshape(128, 128)
    delta = jnp.concatenate(
        [
            jnp.sum(jnp.where(mask, product, 0.0), axis=1, keepdims=True),
            jnp.sum(jnp.where(mask, 0.0, product), axis=1, keepdims=True),
        ],
        axis=0,
    )
    lse = lse_ref[...]
    query_ids = query_id_ref[0]
    both = jnp.concatenate([queries, grad_tile], axis=0)
    query_grad_ref[...] = jnp.zeros((256, 128), F32)
    for chunk in range(CHUNKS):

        @pl.when(flag_ref[at, chunk] != 0)
        def _():
            half, group = chunk // 4, chunk % 4
            keys = key_chunk(recv_ref, chunk)
            scores = nt(queries, keys)
            scores = jnp.where(query_ids == key_id_ref[chunk], scores, NEG_FILL)
            chance = jnp.exp(scores - lse)
            grad_scores = (chance * (nt(grad_tile, keys) - delta)).astype(BF)
            query_grad_ref[...] += nn(grad_scores, keys)
            stacked = jnp.concatenate([grad_scores, chance.astype(BF)], axis=0)
            key_grad_ref[group * 8 : group * 8 + 8, half * ROWS : half * ROWS + ROWS, :] += tn(
                stacked, both
            ).reshape(8, ROWS, 128)

    query_grad = query_grad_ref[...] * SCALE
    joined = jnp.where(mask, query_grad[:128], turn(query_grad[128:]))
    out_ref[pl.ds(at * 8, 8), BOTH : BOTH + 16, :] = joined.astype(BF).reshape(8, 16, 128)

    @pl.when(at == BLOCKS_Q - 1)
    def _():
        out_ref[:, 0:BOTH, :] = key_grad_ref[...].astype(BF)


def attend_back_call(flags, recv, grads, keep, lse, key_ids, query_ids):
    return pl.pallas_call(
        attend_back_kernel,
        grid_spec=pltpu.PrefetchScalarGridSpec(
            num_scalar_prefetch=1,
            grid=(BLOCKS_Q,),
            in_specs=[
                pl.BlockSpec((WIDE, SEND_ROWS, 128), lambda i, f: (0, 0, 0)),
                pl.BlockSpec((8, 16, 128), lambda i, f: (i, 0, 0)),
                pl.BlockSpec((8, 16, 128), lambda i, f: (i, 0, 0)),
                pl.BlockSpec((256, 1), lambda i, f: (i, 0)),
                pl.BlockSpec((CHUNKS, 1, 512), lambda i, f: (0, 0, 0)),
                pl.BlockSpec((1, 256, 1), lambda i, f: (i, 0, 0)),
            ],
            out_specs=pl.BlockSpec((WIDE, SEND_ROWS, 128), lambda i, f: (0, 0, 0)),
            scratch_shapes=[
                pltpu.VMEM((WIDE, BOTH, 128), F32),
                pltpu.VMEM((256, 128), F32),
            ],
        ),
        out_shape=jax.ShapeDtypeStruct((WIDE, SEND_ROWS, 128), BF),
        compiler_params=params(),
        cost_estimate=cost(10 * 1024 * 4096 * 256, 3e6),
    )(flags, recv, grads, keep, lse, key_ids, query_ids)


def out_kernel(recv_ref, weight_ref, mixture_ref, own_ref, other_ref):
    mixture = unpack_heads(recv_ref, 0).astype(BF)
    mixture_ref[...] = mixture
    result = nn(mixture, weight_ref[...].reshape(HALF_W, MODEL))
    own_ref[...] = result[:ROWS]
    other_ref[...] = result[ROWS:].astype(BF)


def out_call(recv, weights):
    return pl.pallas_call(
        out_kernel,
        grid=(1,),
        in_specs=[whole((WIDE, 16, 128)), pl.BlockSpec((WIDE, 16, MODEL), lambda i: (0, 8, 0))],
        out_specs=[whole((BOTH, HALF_W)), whole((ROWS, MODEL)), whole((ROWS, MODEL))],
        out_shape=[
            jax.ShapeDtypeStruct((BOTH, HALF_W), BF),
            jax.ShapeDtypeStruct((ROWS, MODEL), F32),
            jax.ShapeDtypeStruct((ROWS, MODEL), BF),
        ],
        compiler_params=params(),
        cost_estimate=cost(2 * BOTH * HALF_W * MODEL, 2e6),
    )(recv, weights)


def mlp_kernel(own_ref, other_ref, bias_ref, one_ref, two_ref, pre_ref, act_ref, own_out, other_out, acc_ref):
    at = pl.program_id(0)
    rows = jnp.concatenate([own_ref[...], other_ref[...]], axis=0)
    pre = nn(rows, one_ref[...].reshape(MODEL, MODEL)) + bias_ref[...]
    act = (0.5 * pre * (1.0 + lax.erf(pre * ROOT_HALF))).astype(BF)
    pre_ref[...] = pre
    act_ref[...] = act
    part = nn(act, two_ref[...].reshape(MODEL, MODEL))

    @pl.when(at == 0)
    def _():
        acc_ref[...] = part

    @pl.when(at == 1)
    def _():
        result = acc_ref[...] + part
        own_out[...] = result[:ROWS]
        other_out[...] = result[ROWS:].astype(BF)


def mlp_call(own, other, bias, weights):
    return pl.pallas_call(
        mlp_kernel,
        grid=(2,),
        in_specs=[
            whole((ROWS, MODEL)),
            whole((ROWS, MODEL)),
            pl.BlockSpec((1, MODEL), lambda j: (0, j)),
            pl.BlockSpec((WIDE, 32, MODEL), lambda j: (0, 2 + j, 0)),
            pl.BlockSpec((16, 64, MODEL), lambda j: (j, 0, 0)),
        ],
        out_specs=[
            pl.BlockSpec((BOTH, MODEL), lambda j: (0, j)),
            pl.BlockSpec((BOTH, MODEL), lambda j: (0, j)),
            whole((ROWS, MODEL)),
            whole((ROWS, MODEL)),
        ],
        out_shape=[
            jax.ShapeDtypeStruct((BOTH, HIDDEN), F32),
            jax.ShapeDtypeStruct((BOTH, HIDDEN), BF),
            jax.ShapeDtypeStruct((ROWS, MODEL), F32),
            jax.ShapeDtypeStruct((ROWS, MODEL), BF),
        ],
        scratch_shapes=[pltpu.VMEM((BOTH, MODEL), F32)],
        compiler_params=params(),
        cost_estimate=cost(4 * BOTH * HIDDEN * MODEL, 10e6),
    )(own, other, bias, weights, weights)


def mlp_back_kernel(
    own_ref, other_ref, c_own_ref, c_other_ref, pre_ref, act_ref, one_ref, two_ref,
    grad_ref, bias_ref, own_out, other_out, acc_ref,
):
    at = pl.program_id(0)
    rows = jnp.concatenate([own_ref[...], other_ref[...]], axis=0)
    normed = jnp.concatenate([c_own_ref[...], c_other_ref[...]], axis=0)
    pre = pre_ref[...]
    slope = 0.5 * (1.0 + lax.erf(pre * ROOT_HALF)) + pre * jnp.exp(-0.5 * pre * pre) * INV_ROOT_TAU
    grad_pre = (nt(rows, two_ref[...].reshape(MODEL, MODEL)) * slope).astype(BF)
    bias_ref[...] = jnp.sum(grad_pre.astype(F32), axis=0, keepdims=True)
    part = nt(grad_pre, one_ref[...].reshape(MODEL, MODEL))
    grad_two = tn(act_ref[...], rows).astype(BF).reshape(16, 64, MODEL)
    grad_one = tn(normed, grad_pre).astype(BF).reshape(WIDE, 32, MODEL)

    @pl.when(at == 0)
    def _():
        acc_ref[...] = part
        grad_ref[0:16, 0:64, :] = grad_two
        grad_ref[:, 64:96, :] = grad_one

    @pl.when(at == 1)
    def _():
        result = acc_ref[...] + part
        own_out[...] = result[:ROWS]
        other_out[...] = result[ROWS:].astype(BF)
        grad_ref[16:32, 0:64, :] = grad_two
        grad_ref[:, 96:128, :] = grad_one


def mlp_back_call(own, other, c_own, c_other, pre, act, weights):
    return pl.pallas_call(
        mlp_back_kernel,
        grid=(2,),
        in_specs=[
            whole((ROWS, MODEL)),
            whole((ROWS, MODEL)),
            whole((ROWS, MODEL)),
            whole((ROWS, MODEL)),
            pl.BlockSpec((BOTH, MODEL), lambda j: (0, j)),
            pl.BlockSpec((BOTH, MODEL), lambda j: (0, j)),
            pl.BlockSpec((WIDE, 32, MODEL), lambda j: (0, 2 + j, 0)),
            pl.BlockSpec((16, 64, MODEL), lambda j: (j, 0, 0)),
        ],
        out_specs=[
            whole((WIDE, 128, MODEL)),
            pl.BlockSpec((1, MODEL), lambda j: (0, j)),
            whole((ROWS, MODEL)),
            whole((ROWS, MODEL)),
        ],
        out_shape=[
            jax.ShapeDtypeStruct((WIDE, 128, MODEL), BF),
            jax.ShapeDtypeStruct((1, HIDDEN), F32),
            jax.ShapeDtypeStruct((ROWS, MODEL), F32),
            jax.ShapeDtypeStruct((ROWS, MODEL), BF),
        ],
        scratch_shapes=[pltpu.VMEM((BOTH, MODEL), F32)],
        compiler_params=params(),
        cost_estimate=cost(8 * BOTH * HIDDEN * MODEL, 20e6),
    )(own, other, c_own, c_other, pre, act, weights, weights)


def out_back_kernel(own_ref, other_ref, mixture_ref, weight_ref, send_ref, grad_ref):
    rows = jnp.concatenate([own_ref[...], other_ref[...]], axis=0)
    grad_mix = nt(rows, weight_ref[...].reshape(HALF_W, MODEL))
    for pair in range(HEADS_DEV // 2):
        pack_heads(grad_mix[:, pair * 128 : pair * 128 + 128], send_ref, pair, 0)
    grad_ref[...] = tn(mixture_ref[...], rows).astype(BF).reshape(WIDE, 16, MODEL)


def out_back_call(own, other, mixture, weights):
    return pl.pallas_call(
        out_back_kernel,
        grid=(1,),
        in_specs=[
            whole((ROWS, MODEL)),
            whole((ROWS, MODEL)),
            whole((BOTH, HALF_W)),
            pl.BlockSpec((WIDE, 16, MODEL), lambda i: (0, 8, 0)),
        ],
        out_specs=[whole((WIDE, 16, 128)), whole((WIDE, 16, MODEL))],
        out_shape=[
            jax.ShapeDtypeStruct((WIDE, 16, 128), BF),
            jax.ShapeDtypeStruct((WIDE, 16, MODEL), BF),
        ],
        compiler_params=params(),
        cost_estimate=cost(4 * BOTH * HALF_W * MODEL, 3e6),
    )(own, other, mixture, weights)


def qkv_back_kernel(recv_ref, own_ref, other_ref, weight_ref, grad_ref, bias_ref, own_out, other_out):
    rows = jnp.concatenate([own_ref[...], other_ref[...]], axis=0)
    grad_q = unpack_heads(recv_ref, BOTH).astype(BF)
    mask = low_lanes((BOTH, 128))
    key_columns, value_columns = [], []
    for pair in range(HEADS_DEV // 2):
        sums = []
        for head in (2 * pair, 2 * pair + 1):
            total = recv_ref[head * QUARTERS, 0:BOTH, :].astype(F32)
            for quarter in range(1, QUARTERS):
                total = total + recv_ref[head * QUARTERS + quarter, 0:BOTH, :].astype(F32)
            sums.append(total)
        key_columns.append(jnp.where(mask, sums[0], turn(sums[1])))
        value_columns.append(jnp.where(mask, turn(sums[0]), sums[1]))
    grad_k = jnp.concatenate(key_columns, axis=1).astype(BF)
    grad_v = jnp.concatenate(value_columns, axis=1).astype(BF)
    bias_ref[0:1, :] = jnp.sum(grad_q.astype(F32), axis=0, keepdims=True)
    bias_ref[1:2, :] = jnp.sum(grad_v.astype(F32), axis=0, keepdims=True)

    def weight(which):
        return weight_ref[:, which * 32 : which * 32 + 32, :].reshape(MODEL, HALF_W)

    result = nt(grad_q, weight(0)) + nt(grad_k, weight(1)) + nt(grad_v, weight(2))
    own_out[...] = result[:ROWS]
    other_out[...] = result[ROWS:].astype(BF)
    grad_ref[:, 0:32, 0:HALF_W] = tn(rows, grad_q).astype(BF).reshape(WIDE, 32, HALF_W)
    grad_ref[:, 0:32, HALF_W:MODEL] = tn(rows, grad_k).astype(BF).reshape(WIDE, 32, HALF_W)
    value_part = tn(rows, grad_v).astype(BF).reshape(WIDE, 32, HALF_W)
    grad_ref[:, 32:48, 0:HALF_W] = value_part[:, 0:16]
    grad_ref[:, 32:48, HALF_W:MODEL] = value_part[:, 16:32]


def qkv_back_call(recv, own, other, weight):
    return pl.pallas_call(
        qkv_back_kernel,
        grid=(1,),
        in_specs=[
            whole((WIDE, SEND_ROWS, 128)),
            whole((ROWS, MODEL)),
            whole((ROWS, MODEL)),
            whole((WIDE, 96, HALF_W)),
        ],
        out_specs=[
            whole((WIDE, 48, MODEL)),
            whole((2, HALF_W)),
            whole((ROWS, MODEL)),
            whole((ROWS, MODEL)),
        ],
        out_shape=[
            jax.ShapeDtypeStruct((WIDE, 48, MODEL), BF),
            jax.ShapeDtypeStruct((2, HALF_W), F32),
            jax.ShapeDtypeStruct((ROWS, MODEL), F32),
            jax.ShapeDtypeStruct((ROWS, MODEL), BF),
        ],
        compiler_params=params(),
        cost_estimate=cost(12 * BOTH * HALF_W * MODEL, 8e6),
    )(recv, own, other, weight)


def layer_norm(rows_in, gain_row, shift_row):
    centre = jnp.mean(rows_in, axis=-1, keepdims=True)
    centred = rows_in - centre
    spread = jnp.mean(centred * centred, axis=-1, keepdims=True)
    rstd_rows = lax.rsqrt(spread + EPS)
    normal_rows = centred * rstd_rows
    return ((normal_rows * gain_row + shift_row).astype(BF), normal_rows, rstd_rows)


def norm_back(grad_rows, normal_rows, rstd_rows, gain_row):
    scaled = grad_rows * gain_row
    first_mean = jnp.mean(scaled, axis=-1, keepdims=True)
    second_mean = jnp.mean(scaled * normal_rows, axis=-1, keepdims=True)
    return rstd_rows * (scaled - first_mean - normal_rows * second_mean)


def all_to_all(block):
    return lax.all_to_all(block, "wide", 0, 0, tiled=True)


def layer_forward(layer_in, ids, weights, small):
    flags, key_ids, query_ids = ids
    qkv_weight, rest_weight = weights
    gain_rows, shift_rows, scale_rows, qv_rows, fc1_row = small
    a_own, hat_a, rstd_a = layer_norm(layer_in, gain_rows[0], shift_rows[0])
    a_other = swap(a_own, "tensor")
    sent = qkv_call(a_own, a_other, qkv_weight, qv_rows)
    recv = all_to_all(sent)
    mix_sent, mix_keep, lse = attend_call(flags, recv, key_ids, query_ids)
    mixture, proj_own, proj_other = out_call(all_to_all(mix_sent), rest_weight)
    branch_a = proj_own + swap(proj_other, "tensor").astype(F32) + shift_rows[1]
    middle = layer_in + scale_rows[0] * branch_a
    c_own, hat_c, rstd_c = layer_norm(middle, gain_rows[1], shift_rows[2])
    c_other = swap(c_own, "tensor")
    pre, act, mlp_own, mlp_other = mlp_call(c_own, c_other, fc1_row, rest_weight)
    branch_m = mlp_own + swap(mlp_other, "tensor").astype(F32) + shift_rows[3]
    layer_out = middle + scale_rows[1] * branch_m
    kept = (
        a_own, a_other, hat_a, rstd_a, recv, mix_keep, lse, mixture, branch_a,
        c_own, c_other, hat_c, rstd_c, pre, act, branch_m,
    )
    return layer_out, kept


def column_sum(rows):
    return jnp.sum(rows, axis=0)


def mlp_backward(grad_in, kept, weights, small):
    (a_own, a_other, hat_a, rstd_a, recv, mix_keep, lse, mixture, branch_a,
     c_own, c_other, hat_c, rstd_c, pre, act, branch_m) = kept
    gain_rows, shift_rows, scale_rows, qv_rows, fc1_row = small
    grad_m = grad_in * scale_rows[1]
    low_m = grad_m.astype(BF)
    grad_pack, fc1_grad, norm_own, norm_other = mlp_back_call(
        low_m, swap(low_m, "tensor"), c_own, c_other, pre, act, weights[1]
    )
    grad_norm = norm_own + swap(norm_other, "tensor").astype(F32)
    grad_mid = grad_in + norm_back(grad_norm, hat_c, rstd_c, gain_rows[1])
    vectors = (
        column_sum(grad_norm * hat_c),
        column_sum(grad_norm),
        column_sum(grad_m),
        column_sum(grad_in * branch_m),
    )
    return grad_mid, grad_pack, fc1_grad, vectors


def attn_backward(grad_mid, kept, ids, weights, small):
    (a_own, a_other, hat_a, rstd_a, recv, mix_keep, lse, mixture, branch_a,
     c_own, c_other, hat_c, rstd_c, pre, act, branch_m) = kept
    flags, key_ids, query_ids = ids
    gain_rows, shift_rows, scale_rows, qv_rows, fc1_row = small
    grad_a = grad_mid * scale_rows[0]
    low_a = grad_a.astype(BF)
    mix_grad, out_pack = out_back_call(low_a, swap(low_a, "tensor"), mixture, weights[1])
    back = attend_back_call(flags, recv, all_to_all(mix_grad), mix_keep, lse, key_ids, query_ids)
    qkv_pack, qv_grad, norm_own, norm_other = qkv_back_call(
        all_to_all(back), a_own, a_other, weights[0]
    )
    grad_norm = norm_own + swap(norm_other, "tensor").astype(F32)
    grad_x = grad_mid + norm_back(grad_norm, hat_a, rstd_a, gain_rows[0])
    vectors = (
        column_sum(grad_norm * hat_a),
        column_sum(grad_norm),
        column_sum(grad_a),
        column_sum(grad_mid * branch_a),
    )
    return grad_x, qkv_pack, out_pack, qv_grad, vectors


def body(
    x_in, out_cot, image_ids, w_qkv, w_out, w_fc1, w_fc2, gains, shifts, layer_scales, qv_bias, fc1_bias
):
    section = lax.axis_index("section")
    tensor = lax.axis_index("tensor")
    wide = lax.axis_index("wide")
    is_first = section == 0

    def one(array):
        return lax.dynamic_index_in_dim(array, section, 0, keepdims=False)

    flat_small = jnp.concatenate(
        [
            gains.reshape(-1),
            shifts.reshape(-1),
            layer_scales.reshape(-1),
            qv_bias.reshape(-1),
            fc1_bias.reshape(-1),
            jnp.zeros((160,), BF),
        ]
    )
    small_block = jnp.concatenate(
        [flat_small.reshape(1, HALF_W), jnp.zeros((15, HALF_W), BF)], axis=0
    )
    pack_a = jnp.concatenate(
        [jnp.transpose(w_qkv[0], (1, 0, 2)).reshape(96, HALF_W), small_block], axis=0
    )
    pack_b = jnp.concatenate(
        [w_fc2[0], w_fc1[0][:, :MODEL], w_fc1[0][:, MODEL:], w_out[0]], axis=0
    )
    other_a = swap(pack_a, "section")
    other_b = swap(pack_b, "section")

    def gather(block):
        return lax.all_gather(block, "wide", axis=0, tiled=False)

    a_layers = (
        gather(jnp.where(is_first, pack_a, other_a)),
        gather(jnp.where(is_first, other_a, pack_a)),
    )
    b_layers = (
        gather(jnp.where(is_first, pack_b, other_b)),
        gather(jnp.where(is_first, other_b, pack_b)),
    )

    def small_rows(gathered):
        block = gathered[:, 96, :].astype(F32)

        def pick(start, count, width):
            part = block[:, start : start + count * width].reshape(WIDE, count, width)
            return jnp.transpose(part, (1, 0, 2)).reshape(count, WIDE * width)

        return (pick(0, 2, 32), pick(64, 4, 32), pick(192, 2, 32), pick(256, 2, 16), pick(288, 1, 64))

    small = tuple(small_rows(block) for block in a_layers)
    weights = tuple((a_layers[layer], b_layers[layer]) for layer in range(2))

    id_grid = one(image_ids).reshape(2, WIDE, ROWS)
    sorted_ids = jnp.where(tensor == 0, id_grid, id_grid[::-1])
    key_ids = sorted_ids.reshape(CHUNKS, 1, 512)
    quarter = lax.rem(wide, QUARTERS)
    half_ids = lax.dynamic_index_in_dim(sorted_ids, quarter // 2, 0, keepdims=False)
    quarter_ids = lax.dynamic_slice_in_dim(half_ids, lax.rem(quarter, 2) * 32, 32, 1)
    query_ids = jnp.transpose(quarter_ids.reshape(BLOCKS_Q, 8, 2, 16), (0, 2, 1, 3)).reshape(
        BLOCKS_Q, 256, 1
    )
    key_low, key_high = jnp.min(key_ids[:, 0], axis=1), jnp.max(key_ids[:, 0], axis=1)
    query_low, query_high = jnp.min(query_ids[..., 0], axis=1), jnp.max(query_ids[..., 0], axis=1)
    flags = (
        (query_low[:, None] <= key_high[None]) & (query_high[:, None] >= key_low[None])
    ).astype(jnp.int32)
    ids = (flags, key_ids, query_ids)

    rows = one(x_in).astype(F32)
    kept, outs = [], []
    for layer in range(2):
        layer_out, saved = layer_forward(rows, ids, weights[layer], small[layer])
        outs.append(layer_out.astype(BF))
        kept.append(saved)
        rows = outs[-1].astype(F32)

    def rs(pack):
        count = pack.shape[1]
        return lax.psum_scatter(
            pack.reshape(WIDE * count, MODEL), "wide", scatter_dimension=0, tiled=True
        )

    def small_shards(pairs):
        parts = [
            jnp.transpose(vector.reshape(count, WIDE, -1), (1, 0, 2)).reshape(WIDE, -1)
            for vector, count in pairs
        ]
        return jnp.concatenate(parts, axis=1).astype(BF)

    def padded(shards, count):
        return jnp.pad(shards[:, None, :], ((0, 0), (0, count - 1), (0, MODEL - shards.shape[1])))

    grad = one(out_cot).astype(F32)
    grad_mid1, mlp_pack1, fc1_grad1, mlp_vec1 = mlp_backward(grad, kept[1], weights[1], small[1])
    sum_mlp1 = rs(mlp_pack1)
    grad_x1, qkv_pack1, out_pack1, qv_grad1, attn_vec1 = attn_backward(
        grad_mid1, kept[1], ids, weights[1], small[1]
    )
    grad = grad_x1.astype(BF).astype(F32)
    grad_mid0, mlp_pack0, fc1_grad0, mlp_vec0 = mlp_backward(grad, kept[0], weights[0], small[0])
    small1 = small_shards(
        [(jnp.stack(mlp_vec1 + attn_vec1), 8), (qv_grad1, 2), (fc1_grad1, 1)]
    )
    small0 = small_shards([(jnp.stack(mlp_vec0), 4), (fc1_grad0, 1)])
    grad_x0, qkv_pack0, out_pack0, qv_grad0, attn_vec0 = attn_backward(
        grad_mid0, kept[0], ids, weights[0], small[0]
    )
    middle_pack = jnp.concatenate(
        [
            mlp_pack0,
            qkv_pack1,
            out_pack1,
            out_pack0,
            padded(jnp.concatenate([small1, small0], axis=1), 16),
        ],
        axis=1,
    )
    sum_mid = rs(middle_pack)
    last_small = small_shards([(jnp.stack(attn_vec0), 4), (qv_grad0, 2)])
    last_pack = jnp.concatenate([qkv_pack0, padded(last_small, 8)], axis=1)
    last_recv = lax.all_to_all(last_pack, "wide", 0, 0, tiled=True)
    sum_last = jnp.sum(last_recv.astype(F32), axis=0).astype(BF)

    def to_owner(first, second):
        own = jnp.where(is_first, first, second)
        away = jnp.where(is_first, second, first)
        return own.astype(F32) + swap(away, "section").astype(F32)

    mlp_total = to_owner(sum_mid[0:128], sum_mlp1)
    out_total = to_owner(sum_mid[192:208], sum_mid[176:192])
    qkv_total = to_owner(sum_last[0:48], sum_mid[128:176])
    tiny = sum_mid[208]
    tiny1 = tiny[:352]
    tiny_mlp0 = tiny[352:544]
    tiny_attn0 = sum_last[48][:160]
    tiny0 = jnp.concatenate([tiny_mlp0[:128], tiny_attn0, tiny_mlp0[128:]])
    tiny_total = to_owner(tiny0[None], tiny1[None])[0]
    norm_part = tiny_total[:256].astype(BF)
    norm_total = (norm_part.astype(F32) + swap(norm_part, "tensor").astype(F32)).reshape(8, 32)
    g_gains = jnp.stack([norm_total[4], norm_total[0]])
    g_shifts = jnp.stack([norm_total[5], norm_total[6], norm_total[1], norm_total[2]])
    g_scales = jnp.stack([norm_total[7], norm_total[3]])
    g_qv = tiny_total[256:288].reshape(2, 16)
    g_fc1_bias = tiny_total[288:352]
    g_fc2 = mlp_total[0:64]
    g_fc1 = jnp.concatenate([mlp_total[64:96], mlp_total[96:128]], axis=1)
    pairs = qkv_total[0:32]
    value_grad = jnp.concatenate([qkv_total[32:48, :HALF_W], qkv_total[32:48, HALF_W:]], axis=0)
    g_qkv = jnp.stack([pairs[:, :HALF_W], pairs[:, HALF_W:], value_grad], axis=1)

    def by_micro(first, second):
        own = jnp.where(is_first, first, second)
        came = swap(jnp.where(is_first, second, first), "section")
        return jnp.stack([jnp.where(is_first, own, came), jnp.where(is_first, came, own)])

    return (
        by_micro(outs[0], outs[1])[None],
        by_micro(grad_x0, grad_x1)[None],
        g_qkv[None],
        out_total[None],
        g_fc1[None],
        g_fc2[None],
        g_gains[None],
        g_shifts[None],
        g_scales[None],
        g_qv[None],
        g_fc1_bias[None],
    )


def solution(mesh):
    in_specs = (
        P(None, ("tensor", "wide"), None),
        P(None, ("tensor", "wide"), None),
        P(),
        P("section", "wide", None, "tensor"),
        P("section", ("tensor", "wide"), None),
        P("section", "wide", "tensor"),
        P("section", ("tensor", "wide"), None),
        P("section", None, "wide"),
        P("section", None, "wide"),
        P("section", None, "wide"),
        P("section", None, ("tensor", "wide")),
        P("section", ("tensor", "wide")),
    )
    out_specs = (
        P("section", None, ("tensor", "wide"), None),
        P("section", None, ("tensor", "wide"), None),
        P("section", "wide", None, "tensor"),
        P("section", ("tensor", "wide"), None),
        P("section", "wide", "tensor"),
        P("section", ("tensor", "wide"), None),
        P("section", None, "wide"),
        P("section", None, "wide"),
        P("section", None, "wide"),
        P("section", None, ("tensor", "wide")),
        P("section", ("tensor", "wide")),
    )
    return jax.shard_map(body, mesh=mesh, in_specs=in_specs, out_specs=out_specs, check_vma=False)
```

```python
import jax
import jax.numpy as jnp
from jax import lax
from jax.experimental import pallas as pl
from jax.experimental.pallas import tpu as pltpu
from jax.sharding import PartitionSpec as P

HEAD = 64
EPS = 1e-06
NEG_FILL = -1e30
ROOT_HALF = 0.7071067811865476
INV_ROOT_TAU = 0.3989422804014327
SCALE = HEAD ** (-0.5)
BF = jnp.bfloat16
F32 = jnp.float32
MIB = 1024 * 1024

ROWS = 64
BOTH = 128
WIDE = 32
HEADS_DEV = 8
QUARTERS = 4
HALF_W = 512
MODEL = 1024
HIDDEN = 2048
SEND_ROWS = 144
BLOCKS_Q = 4
CHUNKS = 8


def params(limit=56):
    return pltpu.CompilerParams(vmem_limit_bytes=limit * MIB)


def cost(micros):
    return pl.CostEstimate(flops=int(micros * 1e9), bytes_accessed=100000, transcendentals=0)


def whole(shape):
    count = len(shape)
    return pl.BlockSpec(shape, lambda *g: (0,) * count)


def swap(block, axis):
    return lax.ppermute(block, axis, [(0, 1), (1, 0)])


def nt(left, right):
    return lax.dot_general(left, right, (((1,), (1,)), ((), ())), preferred_element_type=F32)


def tn(left, right):
    return lax.dot_general(left, right, (((0,), (0,)), ((), ())), preferred_element_type=F32)


def nn(left, right):
    return jnp.dot(left, right, preferred_element_type=F32)


def low_lanes(shape):
    return lax.broadcasted_iota(jnp.int32, shape, len(shape) - 1) < HEAD


def turn(tile):
    return pltpu.roll(tile, HEAD, 1)


def pack_heads(tile, out_ref, pair, row0):
    rolled = turn(tile)
    for quarter in range(QUARTERS):
        first = slice(quarter * 32, quarter * 32 + 16)
        second = slice(quarter * 32 + 16, quarter * 32 + 32)
        mask = low_lanes((16, 128))
        even = jnp.where(mask, tile[first], rolled[second])
        odd = jnp.where(mask, rolled[first], tile[second])
        out_ref[(2 * pair) * QUARTERS + quarter, row0 : row0 + 16, :] = even.astype(BF)
        out_ref[(2 * pair + 1) * QUARTERS + quarter, row0 : row0 + 16, :] = odd.astype(BF)


def unpack_heads(in_ref, row0):
    mask = low_lanes((16, 128))
    columns = []
    for pair in range(HEADS_DEV // 2):
        pieces = []
        for quarter in range(QUARTERS):
            even = in_ref[(2 * pair) * QUARTERS + quarter, row0 : row0 + 16, :].astype(F32)
            odd = in_ref[(2 * pair + 1) * QUARTERS + quarter, row0 : row0 + 16, :].astype(F32)
            pieces.append(jnp.where(mask, even, turn(odd)))
            pieces.append(jnp.where(mask, turn(even), odd))
        columns.append(jnp.concatenate(pieces, axis=0))
    return jnp.concatenate(columns, axis=1)


def norm_parts(rows_in):
    centre = jnp.mean(rows_in, axis=-1, keepdims=True)
    centred = rows_in - centre
    spread = jnp.mean(centred * centred, axis=-1, keepdims=True)
    rstd_rows = lax.rsqrt(spread + EPS)
    return centred * rstd_rows, rstd_rows


def norm_back(grad_rows, normal_rows, rstd_rows, gain_row):
    scaled = grad_rows * gain_row
    first_mean = jnp.mean(scaled, axis=-1, keepdims=True)
    second_mean = jnp.mean(scaled * normal_rows, axis=-1, keepdims=True)
    return rstd_rows * (scaled - first_mean - normal_rows * second_mean)


def joined(own_ref, recv_ref):
    recv = jnp.concatenate([recv_ref[ROWS:], recv_ref[:ROWS]], axis=0)
    return own_ref[...].astype(F32) + recv.astype(F32)


def column_sum(rows):
    return jnp.sum(rows[:ROWS], axis=0, keepdims=True) + jnp.sum(rows[ROWS:], axis=0, keepdims=True)


GAIN_A, GAIN_C, SHIFT_A, SHIFT_O, SHIFT_C, SHIFT_M, SCALE_A, SCALE_M = range(8)


def row_of(ref, at):
    return ref[at : at + 1, :]


def qkv_weight(ref, which):
    if which < 2:
        return ref[:, 0:32, which * HALF_W : which * HALF_W + HALF_W].reshape(MODEL, HALF_W)
    parts = [ref[:, 32:48, 0:HALF_W], ref[:, 32:48, HALF_W:MODEL]]
    return jnp.concatenate(parts, axis=1).reshape(MODEL, HALF_W)


def project_and_pack(rows, vec_ref, bias_ref, weight_ref, out_ref, rows_ref, normed_ref):
    rows_ref[...] = rows
    hat, _ = norm_parts(rows.astype(F32))
    normed = (hat * row_of(vec_ref, GAIN_A) + row_of(vec_ref, SHIFT_A)).astype(BF)
    normed_ref[...] = normed
    queries = nn(normed, qkv_weight(weight_ref, 0)) + bias_ref[0:1, :]
    keys = nn(normed, qkv_weight(weight_ref, 1))
    values = nn(normed, qkv_weight(weight_ref, 2)) + bias_ref[1:2, :]
    mask = low_lanes((BOTH, 128))
    for pair in range(HEADS_DEV // 2):
        columns = slice(pair * 128, pair * 128 + 128)
        key_tile, value_tile, query_tile = keys[:, columns], values[:, columns], queries[:, columns]
        even = jnp.where(mask, key_tile, turn(value_tile)).astype(BF)
        odd = jnp.where(mask, turn(key_tile), value_tile).astype(BF)
        for quarter in range(QUARTERS):
            out_ref[(2 * pair) * QUARTERS + quarter, 0:BOTH, :] = even
            out_ref[(2 * pair + 1) * QUARTERS + quarter, 0:BOTH, :] = odd
        pack_heads(query_tile, out_ref, pair, BOTH)


def qkv_first_kernel(own_ref, other_ref, vec_ref, bias_ref, weight_ref, out_ref, rows_ref, normed_ref):
    rows = jnp.concatenate([own_ref[...], other_ref[...]], axis=0)
    project_and_pack(rows, vec_ref, bias_ref, weight_ref, out_ref, rows_ref, normed_ref)


def qkv_next_kernel(
    middle_ref, mlp_own_ref, mlp_recv_ref, before_ref, vec_ref, bias_ref, weight_ref,
    out_ref, rows_ref, normed_ref,
):
    branch = joined(mlp_own_ref, mlp_recv_ref) + row_of(before_ref, SHIFT_M)
    rows = (middle_ref[...] + row_of(before_ref, SCALE_M) * branch).astype(BF)
    project_and_pack(rows, vec_ref, bias_ref, weight_ref, out_ref, rows_ref, normed_ref)


def qkv_block(index):
    return pl.BlockSpec((WIDE, 48, MODEL), lambda i: (0, index, 0))


def qkv_call(inputs, small, weight, block_at):
    vec, bias, _ = small
    first = len(inputs) == 2
    return pl.pallas_call(
        qkv_first_kernel if first else qkv_next_kernel,
        grid=(1,),
        in_specs=[whole(part.shape) for part in inputs]
        + [whole((8, MODEL)), whole((2, HALF_W)), qkv_block(block_at)],
        out_specs=[whole((WIDE, SEND_ROWS, 128)), whole((BOTH, MODEL)), whole((BOTH, MODEL))],
        out_shape=[
            jax.ShapeDtypeStruct((WIDE, SEND_ROWS, 128), BF),
            jax.ShapeDtypeStruct((BOTH, MODEL), BF),
            jax.ShapeDtypeStruct((BOTH, MODEL), BF),
        ],
        compiler_params=params(),
        cost_estimate=cost(5),
    )(*inputs, vec, bias, weight)


def query_tiles(packed):
    mask = low_lanes((128, 128))
    return jnp.concatenate(
        [jnp.where(mask, packed, 0.0), jnp.where(mask, turn(packed), 0.0)], axis=0
    )


def key_chunk(recv_ref, chunk):
    half, group = chunk // 4, chunk % 4
    block = recv_ref[group * 8 : group * 8 + 8, half * ROWS : half * ROWS + ROWS, :]
    return block.reshape(512, 128)


def lane_tiles(fn, block):
    return fn(fn(block[:, 0:128], block[:, 128:256]), fn(block[:, 256:384], block[:, 384:512]))


def attend_kernel(
    flag_ref, recv_ref, key_id_ref, query_id_ref, out_ref, keep_ref, lse_ref,
    score_ref, top_ref, total_ref, acc_ref,
):
    at = pl.program_id(0)
    packed = recv_ref[pl.ds(at * 8, 8), BOTH : BOTH + 16, :].astype(F32).reshape(128, 128)
    queries = (query_tiles(packed) * SCALE).astype(BF)
    query_ids = query_id_ref[0]
    top_ref[...] = jnp.full((256, 128), NEG_FILL, F32)
    total_ref[...] = jnp.zeros((256, 128), F32)
    acc_ref[...] = jnp.zeros((256, 128), F32)
    for chunk in range(CHUNKS):

        @pl.when(flag_ref[at, chunk] != 0)
        def _():
            scores = nt(queries, key_chunk(recv_ref, chunk))
            scores = jnp.where(query_ids == key_id_ref[chunk], scores, NEG_FILL)
            score_ref[chunk] = scores
            top_ref[...] = jnp.maximum(top_ref[...], lane_tiles(jnp.maximum, scores))

    top = jnp.max(top_ref[...], axis=1, keepdims=True)
    for chunk in range(CHUNKS):

        @pl.when(flag_ref[at, chunk] != 0)
        def _():
            expo = jnp.exp(score_ref[chunk] - top)
            total_ref[...] += lane_tiles(jnp.add, expo)
            acc_ref[...] += nn(expo.astype(BF), key_chunk(recv_ref, chunk))

    total = jnp.sum(total_ref[...], axis=1, keepdims=True)
    mixture = acc_ref[...] / total
    lse_ref[...] = top + jnp.log(total)
    mask = low_lanes((128, 128))
    joined = jnp.where(mask, turn(mixture[:128]), mixture[128:]).reshape(8, 16, 128)
    keep_ref[...] = joined
    out_ref[...] = joined.astype(BF)


def attend_call(flags, recv, key_ids, query_ids):
    return pl.pallas_call(
        attend_kernel,
        grid_spec=pltpu.PrefetchScalarGridSpec(
            num_scalar_prefetch=1,
            grid=(BLOCKS_Q,),
            in_specs=[
                pl.BlockSpec((WIDE, SEND_ROWS, 128), lambda i, f: (0, 0, 0)),
                pl.BlockSpec((CHUNKS, 1, 512), lambda i, f: (0, 0, 0)),
                pl.BlockSpec((1, 256, 1), lambda i, f: (i, 0, 0)),
            ],
            out_specs=[
                pl.BlockSpec((8, 16, 128), lambda i, f: (i, 0, 0)),
                pl.BlockSpec((8, 16, 128), lambda i, f: (i, 0, 0)),
                pl.BlockSpec((256, 1), lambda i, f: (i, 0)),
            ],
            scratch_shapes=[
                pltpu.VMEM((CHUNKS, 256, 512), F32),
                pltpu.VMEM((256, 128), F32),
                pltpu.VMEM((256, 128), F32),
                pltpu.VMEM((256, 128), F32),
            ],
        ),
        out_shape=[
            jax.ShapeDtypeStruct((WIDE, 16, 128), BF),
            jax.ShapeDtypeStruct((WIDE, 16, 128), F32),
            jax.ShapeDtypeStruct((1024, 1), F32),
        ],
        compiler_params=params(),
        cost_estimate=cost(12),
    )(flags, recv, key_ids, query_ids)


def attend_back_kernel(
    flag_ref, recv_ref, grad_ref, keep_ref, lse_ref, key_id_ref, query_id_ref, out_ref,
    key_grad_ref, query_grad_ref,
):
    at = pl.program_id(0)

    @pl.when(at == 0)
    def _():
        key_grad_ref[...] = jnp.zeros((WIDE, BOTH, 128), F32)

    mask = low_lanes((128, 128))
    packed = recv_ref[pl.ds(at * 8, 8), BOTH : BOTH + 16, :].astype(F32).reshape(128, 128)
    queries = (query_tiles(packed) * SCALE).astype(BF)
    grads = grad_ref[...].astype(F32).reshape(128, 128)
    grad_tile = jnp.concatenate(
        [jnp.where(mask, 0.0, turn(grads)), jnp.where(mask, 0.0, grads)], axis=0
    ).astype(BF)
    product = grads * keep_ref[...].reshape(128, 128)
    delta = jnp.concatenate(
        [
            jnp.sum(jnp.where(mask, product, 0.0), axis=1, keepdims=True),
            jnp.sum(jnp.where(mask, 0.0, product), axis=1, keepdims=True),
        ],
        axis=0,
    )
    lse = lse_ref[...]
    query_ids = query_id_ref[0]
    both = jnp.concatenate([queries, grad_tile], axis=0)
    query_grad_ref[...] = jnp.zeros((256, 128), F32)
    for chunk in range(CHUNKS):

        @pl.when(flag_ref[at, chunk] != 0)
        def _():
            half, group = chunk // 4, chunk % 4
            keys = key_chunk(recv_ref, chunk)
            scores = nt(queries, keys)
            scores = jnp.where(query_ids == key_id_ref[chunk], scores, NEG_FILL)
            chance = jnp.exp(scores - lse)
            grad_scores = (chance * (nt(grad_tile, keys) - delta)).astype(BF)
            query_grad_ref[...] += nn(grad_scores, keys)
            stacked = jnp.concatenate([grad_scores, chance.astype(BF)], axis=0)
            key_grad_ref[group * 8 : group * 8 + 8, half * ROWS : half * ROWS + ROWS, :] += tn(
                stacked, both
            ).reshape(8, ROWS, 128)

    query_grad = query_grad_ref[...] * SCALE
    joined = jnp.where(mask, query_grad[:128], turn(query_grad[128:]))
    out_ref[pl.ds(at * 8, 8), BOTH : BOTH + 16, :] = joined.astype(BF).reshape(8, 16, 128)

    @pl.when(at == BLOCKS_Q - 1)
    def _():
        out_ref[:, 0:BOTH, :] = key_grad_ref[...].astype(BF)


def attend_back_call(flags, recv, grads, keep, lse, key_ids, query_ids):
    return pl.pallas_call(
        attend_back_kernel,
        grid_spec=pltpu.PrefetchScalarGridSpec(
            num_scalar_prefetch=1,
            grid=(BLOCKS_Q,),
            in_specs=[
                pl.BlockSpec((WIDE, SEND_ROWS, 128), lambda i, f: (0, 0, 0)),
                pl.BlockSpec((8, 16, 128), lambda i, f: (i, 0, 0)),
                pl.BlockSpec((8, 16, 128), lambda i, f: (i, 0, 0)),
                pl.BlockSpec((256, 1), lambda i, f: (i, 0)),
                pl.BlockSpec((CHUNKS, 1, 512), lambda i, f: (0, 0, 0)),
                pl.BlockSpec((1, 256, 1), lambda i, f: (i, 0, 0)),
            ],
            out_specs=pl.BlockSpec((WIDE, SEND_ROWS, 128), lambda i, f: (0, 0, 0)),
            scratch_shapes=[
                pltpu.VMEM((WIDE, BOTH, 128), F32),
                pltpu.VMEM((256, 128), F32),
            ],
        ),
        out_shape=jax.ShapeDtypeStruct((WIDE, SEND_ROWS, 128), BF),
        compiler_params=params(),
        cost_estimate=cost(16),
    )(flags, recv, grads, keep, lse, key_ids, query_ids)


def out_kernel(recv_ref, weight_ref, mixture_ref, part_ref):
    mixture = unpack_heads(recv_ref, 0).astype(BF)
    mixture_ref[...] = mixture
    part_ref[...] = nn(mixture, weight_ref[...].reshape(HALF_W, MODEL)).astype(BF)


def out_call(recv, weights):
    return pl.pallas_call(
        out_kernel,
        grid=(1,),
        in_specs=[whole((WIDE, 16, 128)), pl.BlockSpec((WIDE, 16, MODEL), lambda i: (0, 8, 0))],
        out_specs=[whole((BOTH, HALF_W)), whole((BOTH, MODEL))],
        out_shape=[
            jax.ShapeDtypeStruct((BOTH, HALF_W), BF),
            jax.ShapeDtypeStruct((BOTH, MODEL), BF),
        ],
        compiler_params=params(),
        cost_estimate=cost(2.5),
    )(recv, weights)


def mlp_kernel(
    rows_ref, part_own_ref, part_recv_ref, vec_ref, bias_ref, one_ref, two_ref,
    middle_ref, normed_ref, pre_ref, act_ref, out_ref, acc_ref,
):
    at = pl.program_id(0)

    @pl.when(at == 0)
    def _():
        branch = joined(part_own_ref, part_recv_ref) + row_of(vec_ref, SHIFT_O)
        middle = rows_ref[...].astype(F32) + row_of(vec_ref, SCALE_A) * branch
        middle_ref[...] = middle
        hat, _ = norm_parts(middle)
        normed_ref[...] = (hat * row_of(vec_ref, GAIN_C) + row_of(vec_ref, SHIFT_C)).astype(BF)

    pre = nn(normed_ref[...], one_ref[...].reshape(MODEL, MODEL)) + bias_ref[...]
    act = (0.5 * pre * (1.0 + lax.erf(pre * ROOT_HALF))).astype(BF)
    pre_ref[...] = pre
    act_ref[...] = act
    part = nn(act, two_ref[...].reshape(MODEL, MODEL))

    @pl.when(at == 0)
    def _():
        acc_ref[...] = part

    @pl.when(at == 1)
    def _():
        out_ref[...] = (acc_ref[...] + part).astype(BF)


def mlp_call(rows, part_own, part_recv, small, weights):
    vec, _, bias = small
    return pl.pallas_call(
        mlp_kernel,
        grid=(2,),
        in_specs=[
            whole((BOTH, MODEL)),
            whole((BOTH, MODEL)),
            whole((BOTH, MODEL)),
            whole((8, MODEL)),
            pl.BlockSpec((1, MODEL), lambda j: (0, j)),
            pl.BlockSpec((WIDE, 32, MODEL), lambda j: (0, 2 + j, 0)),
            pl.BlockSpec((16, 64, MODEL), lambda j: (j, 0, 0)),
        ],
        out_specs=[
            whole((BOTH, MODEL)),
            whole((BOTH, MODEL)),
            pl.BlockSpec((BOTH, MODEL), lambda j: (0, j)),
            pl.BlockSpec((BOTH, MODEL), lambda j: (0, j)),
            whole((BOTH, MODEL)),
        ],
        out_shape=[
            jax.ShapeDtypeStruct((BOTH, MODEL), F32),
            jax.ShapeDtypeStruct((BOTH, MODEL), BF),
            jax.ShapeDtypeStruct((BOTH, HIDDEN), F32),
            jax.ShapeDtypeStruct((BOTH, HIDDEN), BF),
            jax.ShapeDtypeStruct((BOTH, MODEL), BF),
        ],
        scratch_shapes=[pltpu.VMEM((BOTH, MODEL), F32)],
        compiler_params=params(),
        cost_estimate=cost(7),
    )(rows, part_own, part_recv, vec, bias, weights, weights)


def mlp_back_steps(
    grad, vec_ref, mlp_own_ref, mlp_recv_ref, pre_ref, one_ref, two_ref,
    grad_ref, low_ref, grad_pre_ref, out_ref, sums_ref, acc_ref,
):
    at = pl.program_id(0)

    @pl.when(at == 0)
    def _():
        rows = grad()
        grad_ref[...] = rows
        rows = rows.astype(F32)
        scaled = rows * row_of(vec_ref, SCALE_M)
        low_ref[...] = scaled.astype(BF)
        branch = joined(mlp_own_ref, mlp_recv_ref) + row_of(vec_ref, SHIFT_M)
        sums_ref[...] = jnp.zeros((8, MODEL), F32)
        sums_ref[0:1, :] = column_sum(scaled)
        sums_ref[1:2, :] = column_sum(rows * branch)

    pre = pre_ref[...]
    slope = 0.5 * (1.0 + lax.erf(pre * ROOT_HALF)) + pre * jnp.exp(-0.5 * pre * pre) * INV_ROOT_TAU
    grad_pre = (nt(low_ref[...], two_ref[...].reshape(MODEL, MODEL)) * slope).astype(BF)
    grad_pre_ref[...] = grad_pre
    part = nt(grad_pre, one_ref[...].reshape(MODEL, MODEL))
    bias_sum = jnp.sum(grad_pre.astype(F32), axis=0, keepdims=True)

    @pl.when(at == 0)
    def _():
        acc_ref[...] = part
        sums_ref[2:3, :] = bias_sum

    @pl.when(at == 1)
    def _():
        out_ref[...] = (acc_ref[...] + part).astype(BF)
        sums_ref[3:4, :] = bias_sum


def mlp_back_first_kernel(own_ref, other_ref, *refs):
    mlp_back_steps(lambda: jnp.concatenate([own_ref[...], other_ref[...]], axis=0), *refs)


def mlp_back_next_kernel(middle_grad_ref, part_own_ref, part_recv_ref, rows_ref, after_ref, *refs):
    *refs, input_grad_ref, acc_ref = refs

    def grad():
        hat, rstd = norm_parts(rows_ref[...].astype(F32))
        grad_norm = joined(part_own_ref, part_recv_ref)
        total = middle_grad_ref[...] + norm_back(grad_norm, hat, rstd, row_of(after_ref, GAIN_A))
        input_grad_ref[...] = total[:ROWS]
        return total.astype(BF)

    mlp_back_steps(grad, *refs, acc_ref)


def mlp_back_call(inputs, small, mlp_own, mlp_recv, pre, weights):
    first = len(inputs) == 2
    extra = [] if first else [(ROWS, MODEL)]
    return pl.pallas_call(
        mlp_back_first_kernel if first else mlp_back_next_kernel,
        grid=(2,),
        in_specs=[whole(part.shape) for part in inputs]
        + [
            whole((8, MODEL)),
            whole((BOTH, MODEL)),
            whole((BOTH, MODEL)),
            pl.BlockSpec((BOTH, MODEL), lambda j: (0, j)),
            pl.BlockSpec((WIDE, 32, MODEL), lambda j: (0, 2 + j, 0)),
            pl.BlockSpec((16, 64, MODEL), lambda j: (j, 0, 0)),
        ],
        out_specs=[
            whole((BOTH, MODEL)),
            whole((BOTH, MODEL)),
            pl.BlockSpec((BOTH, MODEL), lambda j: (0, j)),
            whole((BOTH, MODEL)),
            whole((8, MODEL)),
        ]
        + [whole(shape) for shape in extra],
        out_shape=[
            jax.ShapeDtypeStruct((BOTH, MODEL), BF),
            jax.ShapeDtypeStruct((BOTH, MODEL), BF),
            jax.ShapeDtypeStruct((BOTH, HIDDEN), BF),
            jax.ShapeDtypeStruct((BOTH, MODEL), BF),
            jax.ShapeDtypeStruct((8, MODEL), F32),
        ]
        + [jax.ShapeDtypeStruct(shape, F32) for shape in extra],
        scratch_shapes=[pltpu.VMEM((BOTH, MODEL), F32)],
        compiler_params=params(),
        cost_estimate=cost(8),
    )(*inputs, small[0], mlp_own, mlp_recv, pre, weights, weights)


PACK_ROWS = 240


def buffer_args(buffer, count_inputs):
    if buffer is None:
        return [], [], {}
    return [buffer], [pl.BlockSpec(memory_space=pl.ANY)], {count_inputs: 0}


def mlp_weight_kernel(low_ref, normed_ref, act_ref, grad_pre_ref, after_ref, *refs):
    grad_ref = refs[-1]
    at = pl.program_id(0)
    grad_two = tn(act_ref[...], low_ref[...]).astype(BF).reshape(16, 64, MODEL)
    grad_one = tn(normed_ref[...], grad_pre_ref[...]).astype(BF).reshape(WIDE, 32, MODEL)

    @pl.when(at == 0)
    def _():
        grad_ref[0:16, 0:64, :] = grad_two
        grad_ref[:, 64:96, :] = grad_one

    @pl.when(at == 1)
    def _():
        grad_ref[16:32, 0:64, :] = grad_two
        grad_ref[:, 96:128, :] = grad_one


def mlp_weight_call(low, normed, act, grad_pre, after, buffer):
    more, more_specs, aliases = buffer_args(buffer, 5)
    rows = 128 if buffer is None else PACK_ROWS
    return pl.pallas_call(
        mlp_weight_kernel,
        grid=(2,),
        in_specs=[
            whole((BOTH, MODEL)),
            whole((BOTH, MODEL)),
            pl.BlockSpec((BOTH, MODEL), lambda j: (0, j)),
            pl.BlockSpec((BOTH, MODEL), lambda j: (0, j)),
            pl.BlockSpec(memory_space=pl.ANY),
        ]
        + more_specs,
        out_specs=whole((WIDE, 128, MODEL)),
        out_shape=jax.ShapeDtypeStruct((WIDE, rows, MODEL), BF),
        input_output_aliases=aliases,
        compiler_params=params(),
        cost_estimate=cost(8),
    )(low, normed, act, grad_pre, after, *more)


def out_back_kernel(
    grad_ref, part_own_ref, part_recv_ref, middle_ref, proj_own_ref, proj_recv_ref, vec_ref,
    weight_ref, middle_grad_ref, send_ref, low_ref, sums_ref,
):
    hat, rstd = norm_parts(middle_ref[...])
    grad_norm = joined(part_own_ref, part_recv_ref)
    total = grad_ref[...].astype(F32) + norm_back(grad_norm, hat, rstd, row_of(vec_ref, GAIN_C))
    middle_grad_ref[...] = total
    scaled = total * row_of(vec_ref, SCALE_A)
    rows = scaled.astype(BF)
    low_ref[...] = rows
    grad_mix = nt(rows, weight_ref[...].reshape(HALF_W, MODEL))
    for pair in range(HEADS_DEV // 2):
        pack_heads(grad_mix[:, pair * 128 : pair * 128 + 128], send_ref, pair, 0)
    branch = joined(proj_own_ref, proj_recv_ref) + row_of(vec_ref, SHIFT_O)
    sums_ref[...] = jnp.zeros((8, MODEL), F32)
    sums_ref[0:1, :] = column_sum(grad_norm * hat)
    sums_ref[1:2, :] = column_sum(grad_norm)
    sums_ref[2:3, :] = column_sum(scaled)
    sums_ref[3:4, :] = column_sum(total * branch)


def out_back_call(grad, part_own, part_recv, middle, proj_own, proj_recv, small, weights):
    return pl.pallas_call(
        out_back_kernel,
        grid=(1,),
        in_specs=[whole((BOTH, MODEL))] * 6
        + [whole((8, MODEL)), pl.BlockSpec((WIDE, 16, MODEL), lambda i: (0, 8, 0))],
        out_specs=[
            whole((BOTH, MODEL)), whole((WIDE, 16, 128)), whole((BOTH, MODEL)), whole((8, MODEL))
        ],
        out_shape=[
            jax.ShapeDtypeStruct((BOTH, MODEL), F32),
            jax.ShapeDtypeStruct((WIDE, 16, 128), BF),
            jax.ShapeDtypeStruct((BOTH, MODEL), BF),
            jax.ShapeDtypeStruct((8, MODEL), F32),
        ],
        compiler_params=params(),
        cost_estimate=cost(4),
    )(grad, part_own, part_recv, middle, proj_own, proj_recv, small[0], weights)


def out_weight_kernel(mixture_ref, low_ref, grad_ref):
    grad_ref[...] = tn(mixture_ref[...], low_ref[...]).astype(BF).reshape(WIDE, 16, MODEL)


def out_weight_last_kernel(mixture_ref, low_ref, *refs):
    *sums_refs, before_ref, buffer_ref, grad_ref = refs
    grad_ref[:, 0:16, :] = tn(mixture_ref[...], low_ref[...]).astype(BF).reshape(WIDE, 16, MODEL)
    parts = [ref[0:4, :] for ref in sums_refs] + [before_ref[0:12, :].astype(F32)]
    rows = jnp.concatenate(parts, axis=0).astype(BF)
    grad_ref[:, 16:48, :] = jnp.broadcast_to(rows[None], (WIDE, 32, MODEL))


def out_weight_call(mixture, low):
    return pl.pallas_call(
        out_weight_kernel,
        grid=(1,),
        in_specs=[whole((BOTH, HALF_W)), whole((BOTH, MODEL))],
        out_specs=pl.BlockSpec((WIDE, 16, MODEL), lambda i: (0, 8, 0)),
        out_shape=jax.ShapeDtypeStruct((WIDE, PACK_ROWS, MODEL), BF),
        compiler_params=params(),
        cost_estimate=cost(2),
    )(mixture, low)


def out_weight_last_call(mixture, low, sums, before, buffer):
    count = 3 + len(sums)
    return pl.pallas_call(
        out_weight_last_kernel,
        grid=(1,),
        in_specs=[whole((BOTH, HALF_W)), whole((BOTH, MODEL))]
        + [whole((8, MODEL)) for _ in sums]
        + [whole((16, MODEL)), pl.BlockSpec(memory_space=pl.ANY)],
        out_specs=pl.BlockSpec((WIDE, 48, MODEL), lambda i: (0, 4, 0)),
        out_shape=jax.ShapeDtypeStruct((WIDE, PACK_ROWS, MODEL), BF),
        input_output_aliases={count: 0},
        compiler_params=params(),
        cost_estimate=cost(3),
    )(mixture, low, *sums, before, buffer)


def qkv_back_kernel(recv_ref, rows_ref, vec_ref, weight_ref, part_ref, grads_ref, sums_ref):
    grad_q = unpack_heads(recv_ref, BOTH).astype(BF)
    mask = low_lanes((BOTH, 128))
    key_columns, value_columns = [], []
    for pair in range(HEADS_DEV // 2):
        sums = []
        for head in (2 * pair, 2 * pair + 1):
            total = recv_ref[head * QUARTERS, 0:BOTH, :].astype(F32)
            for quarter in range(1, QUARTERS):
                total = total + recv_ref[head * QUARTERS + quarter, 0:BOTH, :].astype(F32)
            sums.append(total)
        key_columns.append(jnp.where(mask, sums[0], turn(sums[1])))
        value_columns.append(jnp.where(mask, turn(sums[0]), sums[1]))
    grad_k = jnp.concatenate(key_columns, axis=1).astype(BF)
    grad_v = jnp.concatenate(value_columns, axis=1).astype(BF)
    grads_ref[:, 0:HALF_W] = grad_q
    grads_ref[:, HALF_W:MODEL] = grad_k
    grads_ref[:, MODEL : MODEL + HALF_W] = grad_v
    result = (
        nt(grad_q, qkv_weight(weight_ref, 0))
        + nt(grad_k, qkv_weight(weight_ref, 1))
        + nt(grad_v, qkv_weight(weight_ref, 2))
    )
    part_ref[...] = result.astype(BF)
    hat, _ = norm_parts(rows_ref[...].astype(F32))
    sums_ref[...] = jnp.zeros((8, MODEL), F32)
    sums_ref[0:1, :] = column_sum(result * hat)
    sums_ref[1:2, :] = column_sum(result)
    sums_ref[2:3, 0:HALF_W] = column_sum(grad_q.astype(F32))
    sums_ref[2:3, HALF_W:MODEL] = column_sum(grad_v.astype(F32))


def qkv_back_call(recv, rows, small, weight, block_at):
    return pl.pallas_call(
        qkv_back_kernel,
        grid=(1,),
        in_specs=[
            whole((WIDE, SEND_ROWS, 128)),
            whole((BOTH, MODEL)),
            whole((8, MODEL)),
            qkv_block(block_at),
        ],
        out_specs=[whole((BOTH, MODEL)), whole((BOTH, 3 * HALF_W)), whole((8, MODEL))],
        out_shape=[
            jax.ShapeDtypeStruct((BOTH, MODEL), BF),
            jax.ShapeDtypeStruct((BOTH, 3 * HALF_W), BF),
            jax.ShapeDtypeStruct((8, MODEL), F32),
        ],
        compiler_params=params(),
        cost_estimate=cost(5),
    )(recv, rows, small[0], weight)


def store_qkv_grads(normed_ref, grads_ref, grad_ref):
    rows = normed_ref[...]

    def part(which):
        grads = grads_ref[:, which * HALF_W : which * HALF_W + HALF_W]
        return tn(rows, grads).astype(BF).reshape(WIDE, 32, HALF_W)

    grad_ref[:, 0:32, 0:HALF_W] = part(0)
    grad_ref[:, 0:32, HALF_W:MODEL] = part(1)
    values = part(2)
    grad_ref[:, 32:48, 0:HALF_W] = values[:, 0:16]
    grad_ref[:, 32:48, HALF_W:MODEL] = values[:, 16:32]


def qkv_weight_kernel(normed_ref, grads_ref, buffer_ref, grad_ref):
    store_qkv_grads(normed_ref, grads_ref, grad_ref)


def qkv_weight_last_kernel(normed_ref, grads_ref, sums_ref, grad_ref):
    store_qkv_grads(normed_ref, grads_ref, grad_ref)
    grad_ref[:, 48:56, :] = jnp.broadcast_to(sums_ref[...].astype(BF)[None], (WIDE, 8, MODEL))


def qkv_weight_call(normed, grads, buffer):
    return pl.pallas_call(
        qkv_weight_kernel,
        grid=(1,),
        in_specs=[whole((BOTH, MODEL)), whole((BOTH, 3 * HALF_W)), pl.BlockSpec(memory_space=pl.ANY)],
        out_specs=qkv_block(3),
        out_shape=jax.ShapeDtypeStruct((WIDE, PACK_ROWS, MODEL), BF),
        input_output_aliases={2: 0},
        compiler_params=params(),
        cost_estimate=cost(4),
    )(normed, grads, buffer)


def qkv_weight_last_call(normed, grads, sums):
    return pl.pallas_call(
        qkv_weight_last_kernel,
        grid=(1,),
        in_specs=[whole((BOTH, MODEL)), whole((BOTH, 3 * HALF_W)), whole((8, MODEL))],
        out_specs=whole((WIDE, 56, MODEL)),
        out_shape=jax.ShapeDtypeStruct((WIDE, 56, MODEL), BF),
        compiler_params=params(),
        cost_estimate=cost(4),
    )(normed, grads, sums)


def all_to_all(block):
    return lax.all_to_all(block, "wide", 0, 0, tiled=True)


def layer_forward(inputs, ids, qkv, rest, small):
    flags, key_ids, query_ids = ids
    sent, rows, normed_a = qkv_call(inputs, small, *qkv)
    recv = all_to_all(sent)
    mix_sent, mix_keep, lse = attend_call(flags, recv, key_ids, query_ids)
    mixture, proj = out_call(all_to_all(mix_sent), rest)
    proj_recv = swap(proj, "tensor")
    middle, normed_c, pre, act, mlp = mlp_call(rows, proj, proj_recv, small, rest)
    mlp_recv = swap(mlp, "tensor")
    return dict(
        rows=rows, normed_a=normed_a, recv=recv, keep=mix_keep, lse=lse, mixture=mixture,
        proj=proj, proj_recv=proj_recv, middle=middle, normed_c=normed_c, pre=pre, act=act,
        mlp=mlp, mlp_recv=mlp_recv,
    )


def layer_backward(inputs, kept, ids, qkv, rest, small):
    flags, key_ids, query_ids = ids
    grad, low_m, grad_pre, part, mlp_sums, *input_grad = mlp_back_call(
        inputs, small, kept["mlp"], kept["mlp_recv"], kept["pre"], rest
    )
    middle_grad, mix_grad, low_a, out_sums = out_back_call(
        grad, part, swap(part, "tensor"), kept["middle"], kept["proj"], kept["proj_recv"], small, rest
    )
    back = attend_back_call(
        flags, kept["recv"], all_to_all(mix_grad), kept["keep"], kept["lse"], key_ids, query_ids
    )
    qkv_part, qkv_grads, qkv_sums = qkv_back_call(all_to_all(back), kept["rows"], small, *qkv)
    carried = (middle_grad, qkv_part, swap(qkv_part, "tensor"), kept["rows"])
    for_weights = dict(
        low_m=low_m, grad_pre=grad_pre, low_a=low_a, qkv_grads=qkv_grads,
        mlp_sums=mlp_sums, out_sums=out_sums, qkv_sums=qkv_sums,
    )
    return carried, for_weights, input_grad


def body(
    x_in, out_cot, image_ids, w_qkv, w_out, w_fc1, w_fc2, gains, shifts, layer_scales, qv_bias, fc1_bias
):
    section = lax.axis_index("section")
    tensor = lax.axis_index("tensor")
    wide = lax.axis_index("wide")
    is_first = section == 0

    def one(array):
        return lax.dynamic_index_in_dim(array, section, 0, keepdims=False)

    qkv = w_qkv[0]
    small_row = jnp.concatenate(
        [
            gains.reshape(-1),
            shifts.reshape(-1),
            layer_scales.reshape(-1),
            qv_bias.reshape(-1),
            fc1_bias.reshape(-1),
            jnp.zeros((672,), BF),
        ]
    ).reshape(1, MODEL)
    pack_a = jnp.concatenate(
        [
            jnp.concatenate([qkv[:, 0], qkv[:, 1]], axis=1),
            jnp.concatenate([qkv[0:16, 2], qkv[16:32, 2]], axis=1),
            small_row,
            jnp.zeros((15, MODEL), BF),
        ],
        axis=0,
    )
    pack_b = jnp.concatenate([w_fc2[0], w_fc1[0][:, :MODEL], w_fc1[0][:, MODEL:], w_out[0]], axis=0)
    own_rows, own_cot = one(x_in), one(out_cot)
    other_both = swap(jnp.concatenate([own_rows, own_cot], axis=0), "tensor")
    other_rows, other_cot = other_both[:ROWS], other_both[ROWS:]
    other_a = swap(pack_a, "section")
    pack_b = jnp.concatenate([pack_b, other_rows[:16]], axis=0)
    other_b = swap(pack_b, "section")

    def gather(block):
        return lax.all_gather(block, "wide", axis=0, tiled=False)

    def behind(block, rows):
        return jnp.concatenate([block[:144], rows], axis=0)

    attn_both = gather(
        jnp.where(
            is_first,
            jnp.concatenate([pack_a, pack_a[48:64], pack_a[48:64], other_a], axis=0),
            jnp.concatenate([other_a, other_a[48:64], other_a[48:64], pack_a], axis=0),
        )
    )
    rest_first = gather(behind(jnp.where(is_first, pack_b, other_b), attn_both[0, 48:64]))

    def rest_second(rows):
        return gather(behind(jnp.where(is_first, other_b, pack_b), rows))

    def small_rows(at):
        block = attn_both[:, at, :].astype(F32)
        vec = jnp.transpose(block[:, :256].reshape(WIDE, 8, 32), (1, 0, 2)).reshape(8, MODEL)
        bias = jnp.transpose(block[:, 256:288].reshape(WIDE, 2, 16), (1, 0, 2)).reshape(2, HALF_W)
        return vec, bias, block[:, 288:352].reshape(1, HIDDEN)

    small = (small_rows(48), small_rows(96 + 48))

    id_grid = one(image_ids).reshape(2, WIDE, ROWS)
    sorted_ids = jnp.where(tensor == 0, id_grid, id_grid[::-1])
    key_ids = sorted_ids.reshape(CHUNKS, 1, 512)
    quarter = lax.rem(wide, QUARTERS)
    half_ids = lax.dynamic_index_in_dim(sorted_ids, quarter // 2, 0, keepdims=False)
    quarter_ids = lax.dynamic_slice_in_dim(half_ids, lax.rem(quarter, 2) * 32, 32, 1)
    query_ids = jnp.transpose(quarter_ids.reshape(BLOCKS_Q, 8, 2, 16), (0, 2, 1, 3)).reshape(
        BLOCKS_Q, 256, 1
    )
    key_low, key_high = jnp.min(key_ids[:, 0], axis=1), jnp.max(key_ids[:, 0], axis=1)
    query_low, query_high = jnp.min(query_ids[..., 0], axis=1), jnp.max(query_ids[..., 0], axis=1)
    flags = (
        (query_low[:, None] <= key_high[None]) & (query_high[:, None] >= key_low[None])
    ).astype(jnp.int32)
    ids = (flags, key_ids, query_ids)

    qkv_parts = ((attn_both, 0), (attn_both, 2))
    kept0 = layer_forward((own_rows, other_rows), ids, qkv_parts[0], rest_first, small[0])
    rest = (rest_first, rest_second(kept0["proj"][:16]))
    kept1 = layer_forward(
        (kept0["middle"], kept0["mlp"], kept0["mlp_recv"], small[0][0]),
        ids, qkv_parts[1], rest[1], small[1],
    )
    branch1 = kept1["mlp"][:ROWS].astype(F32) + kept1["mlp_recv"][ROWS:].astype(F32)
    out1 = (
        kept1["middle"][:ROWS]
        + small[1][0][SCALE_M] * (branch1 + small[1][0][SHIFT_M])
    ).astype(BF)
    out0 = kept1["rows"][:ROWS]

    def rs(pack):
        return lax.psum_scatter(
            pack.reshape(WIDE * pack.shape[1], MODEL), "wide", scatter_dimension=0, tiled=True
        )

    carried1, back1, _ = layer_backward(
        (own_cot, other_cot), kept1, ids, qkv_parts[1], rest[1], small[1]
    )
    sum_mlp1 = rs(
        mlp_weight_call(
            back1["low_m"], kept1["normed_c"], kept1["act"], back1["grad_pre"], back1["out_sums"], None
        )
    )
    pack = out_weight_call(kept1["mixture"], back1["low_a"])
    pack = qkv_weight_call(kept1["normed_a"], back1["qkv_grads"], pack)

    carried0, back0, (grad_x1,) = layer_backward(
        carried1 + (small[1][0],), kept0, ids, qkv_parts[0], rest[0], small[0]
    )
    pack = mlp_weight_call(
        back0["low_m"], kept0["normed_c"], kept0["act"], back0["grad_pre"], back0["low_m"], pack
    )
    pack = out_weight_last_call(
        kept0["mixture"],
        back0["low_a"],
        (back1["mlp_sums"], back1["out_sums"], back1["qkv_sums"], back0["mlp_sums"], back0["out_sums"]),
        sum_mlp1,
        pack,
    )
    sum_mid = rs(pack)
    last_pack = qkv_weight_last_call(kept0["normed_a"], back0["qkv_grads"], back0["qkv_sums"])
    sum_last = jnp.sum(all_to_all(last_pack).astype(F32), axis=0)

    middle_grad0, part0, part_recv0, _ = carried0
    hat0, rstd0 = norm_parts(own_rows.astype(F32))
    grad_norm0 = part0[:ROWS].astype(F32) + part_recv0[ROWS:].astype(F32)
    grad_x0 = middle_grad0[:ROWS] + norm_back(grad_norm0, hat0, rstd0, small[0][0][GAIN_A])

    def lanes(rows, width):
        return lax.dynamic_slice_in_dim(rows, wide * width, width, rows.ndim - 1)

    def own_sums(mlp, outs, qkv_rows):
        norms = jnp.concatenate([mlp[0:2], outs, qkv_rows[0:2]], axis=0)
        pair = qkv_rows[2].reshape(2, HALF_W)
        return jnp.concatenate(
            [lanes(norms, 32).reshape(-1), lanes(pair, 16).reshape(-1), lanes(mlp[2:4].reshape(-1), 64)]
        )

    sums = sum_mid[208:228]
    mlp1, outs1, qkv1, mlp0, outs0 = (sums[at : at + 4] for at in range(0, 20, 4))
    mid0 = jnp.concatenate([sum_mid[0:128], sum_mid[192:208]], axis=0)
    mid1 = jnp.concatenate([sum_mlp1, sum_mid[128:144]], axis=0)
    mid_total = jnp.where(is_first, mid0, mid1).astype(F32) + swap(
        jnp.where(is_first, mid1, mid0), "section"
    ).astype(F32)

    def with_sums(rows, vector):
        return jnp.concatenate([rows, jnp.pad(vector, (0, 672)).reshape(1, MODEL)], axis=0)

    late0 = with_sums(sum_last[0:48].astype(BF), own_sums(mlp0, outs0, sum_last[48:52].astype(BF)))
    late1 = with_sums(sum_mid[144:192], own_sums(mlp1, outs1, qkv1))
    late_own = jnp.where(is_first, late0, late1)
    late_away = jnp.where(is_first, late1, late0)
    late_total = late_own.astype(F32) + swap(late_away, "section").astype(F32)
    own_part, away_part = late_own[48, 192:256], late_away[48, 192:256]
    across = lax.ppermute(away_part, ("section", "tensor"), [(0, 3), (3, 0), (1, 2), (2, 1)])
    heads_total = late_total[48, 192:256] + (
        swap(own_part, "tensor").astype(F32) + across.astype(F32)
    )
    mlp_total, out_total = mid_total[0:128], mid_total[128:144]
    qkv_total, tiny = late_total[0:48], late_total[48]
    norms = jnp.concatenate([tiny[0:192], heads_total]).reshape(8, 32)
    g_gains = jnp.stack([norms[6], norms[2]])
    g_shifts = jnp.stack([norms[7], norms[4], norms[3], norms[0]])
    g_scales = jnp.stack([norms[5], norms[1]])
    g_qv = tiny[256:288].reshape(2, 16)
    g_fc1_bias = tiny[288:352]
    g_fc2 = mlp_total[0:64]
    g_fc1 = jnp.concatenate([mlp_total[64:96], mlp_total[96:128]], axis=1)
    pairs = qkv_total[0:32]
    value_grad = jnp.concatenate([qkv_total[32:48, :HALF_W], qkv_total[32:48, HALF_W:]], axis=0)
    g_qkv = jnp.stack([pairs[:, :HALF_W], pairs[:, HALF_W:], value_grad], axis=1)

    def by_micro(first, second):
        own = jnp.where(is_first, first, second)
        came = swap(jnp.where(is_first, second, first), "section")
        return jnp.stack([jnp.where(is_first, own, came), jnp.where(is_first, came, own)])

    return (
        by_micro(out0, out1)[None],
        by_micro(grad_x0, grad_x1)[None],
        g_qkv[None],
        out_total[None],
        g_fc1[None],
        g_fc2[None],
        g_gains[None],
        g_shifts[None],
        g_scales[None],
        g_qv[None],
        g_fc1_bias[None],
    )


def solution(mesh):
    in_specs = (
        P(None, ("tensor", "wide"), None),
        P(None, ("tensor", "wide"), None),
        P(),
        P("section", "wide", None, "tensor"),
        P("section", ("tensor", "wide"), None),
        P("section", "wide", "tensor"),
        P("section", ("tensor", "wide"), None),
        P("section", None, "wide"),
        P("section", None, "wide"),
        P("section", None, "wide"),
        P("section", None, ("tensor", "wide")),
        P("section", ("tensor", "wide")),
    )
    out_specs = (
        P("section", None, ("tensor", "wide"), None),
        P("section", None, ("tensor", "wide"), None),
        P("section", "wide", None, "tensor"),
        P("section", ("tensor", "wide"), None),
        P("section", "wide", "tensor"),
        P("section", ("tensor", "wide"), None),
        P("section", None, "wide"),
        P("section", None, "wide"),
        P("section", None, "wide"),
        P("section", None, ("tensor", "wide")),
        P("section", ("tensor", "wide")),
    )
    return jax.shard_map(body, mesh=mesh, in_specs=in_specs, out_specs=out_specs, check_vma=False)
```

```python
import jax
import jax.numpy as jnp
from jax import lax
from jax.experimental import pallas as pl
from jax.experimental.pallas import tpu as pltpu
from jax.sharding import PartitionSpec as P

HEAD = 64
EPS = 1e-06
NEG_FILL = -1e30
ROOT_HALF = 0.7071067811865476
INV_ROOT_TAU = 0.3989422804014327
SCALE = HEAD ** (-0.5)
BF = jnp.bfloat16
F32 = jnp.float32
MIB = 1024 * 1024

ROWS = 64
BOTH = 128
WIDE = 32
HEADS_DEV = 8
QUARTERS = 4
HALF_W = 512
MODEL = 1024
HIDDEN = 2048
SEND_ROWS = 144
BLOCKS_Q = 4
CHUNKS = 8


def params(limit=56):
    return pltpu.CompilerParams(vmem_limit_bytes=limit * MIB)


def cost(micros):
    return pl.CostEstimate(flops=int(micros * 1e9), bytes_accessed=100000, transcendentals=0)


def whole(shape):
    count = len(shape)
    return pl.BlockSpec(shape, lambda *g: (0,) * count)


def swap(block, axis):
    return lax.ppermute(block, axis, [(0, 1), (1, 0)])


def nt(left, right):
    return lax.dot_general(left, right, (((1,), (1,)), ((), ())), preferred_element_type=F32)


def tn(left, right):
    return lax.dot_general(left, right, (((0,), (0,)), ((), ())), preferred_element_type=F32)


def nn(left, right):
    return jnp.dot(left, right, preferred_element_type=F32)


def low_lanes(shape):
    return lax.broadcasted_iota(jnp.int32, shape, len(shape) - 1) < HEAD


def turn(tile):
    return pltpu.roll(tile, HEAD, 1)


def pack_heads(tile, out_ref, pair, row0):
    rolled = turn(tile)
    for quarter in range(QUARTERS):
        first = slice(quarter * 32, quarter * 32 + 16)
        second = slice(quarter * 32 + 16, quarter * 32 + 32)
        mask = low_lanes((16, 128))
        even = jnp.where(mask, tile[first], rolled[second])
        odd = jnp.where(mask, rolled[first], tile[second])
        out_ref[(2 * pair) * QUARTERS + quarter, row0 : row0 + 16, :] = even.astype(BF)
        out_ref[(2 * pair + 1) * QUARTERS + quarter, row0 : row0 + 16, :] = odd.astype(BF)


def unpack_heads(in_ref, row0, base=0):
    mask = low_lanes((16, 128))
    columns = []
    for pair in range(HEADS_DEV // 2):
        pieces = []
        for quarter in range(QUARTERS):
            even = in_ref[base + (2 * pair) * QUARTERS + quarter, row0 : row0 + 16, :].astype(F32)
            odd = in_ref[base + (2 * pair + 1) * QUARTERS + quarter, row0 : row0 + 16, :].astype(F32)
            pieces.append(jnp.where(mask, even, turn(odd)))
            pieces.append(jnp.where(mask, turn(even), odd))
        columns.append(jnp.concatenate(pieces, axis=0))
    return jnp.concatenate(columns, axis=1)


def norm_parts(rows_in):
    centre = jnp.mean(rows_in, axis=-1, keepdims=True)
    centred = rows_in - centre
    spread = jnp.mean(centred * centred, axis=-1, keepdims=True)
    rstd_rows = lax.rsqrt(spread + EPS)
    return centred * rstd_rows, rstd_rows


def norm_back(grad_rows, normal_rows, rstd_rows, gain_row):
    scaled = grad_rows * gain_row
    first_mean = jnp.mean(scaled, axis=-1, keepdims=True)
    second_mean = jnp.mean(scaled * normal_rows, axis=-1, keepdims=True)
    return rstd_rows * (scaled - first_mean - normal_rows * second_mean)


def joined(own_ref, recv_ref):
    recv = jnp.concatenate([recv_ref[ROWS:], recv_ref[:ROWS]], axis=0)
    return own_ref[...].astype(F32) + recv.astype(F32)


def column_sum(rows):
    return jnp.sum(rows[:ROWS], axis=0, keepdims=True) + jnp.sum(rows[ROWS:], axis=0, keepdims=True)


GAIN_A, GAIN_C, SHIFT_A, SHIFT_O, SHIFT_C, SHIFT_M, SCALE_A, SCALE_M = range(8)


def row_of(ref, at):
    return ref[at : at + 1, :]


def qkv_weight(ref, which):
    if which < 2:
        return ref[:, 0:32, which * HALF_W : which * HALF_W + HALF_W].reshape(MODEL, HALF_W)
    parts = [ref[:, 32:48, 0:HALF_W], ref[:, 32:48, HALF_W:MODEL]]
    return jnp.concatenate(parts, axis=1).reshape(MODEL, HALF_W)


def project_and_pack(rows, vec_ref, bias_ref, weight_ref, out_ref, rows_ref, normed_ref):
    rows_ref[...] = rows
    hat, _ = norm_parts(rows.astype(F32))
    normed = (hat * row_of(vec_ref, GAIN_A) + row_of(vec_ref, SHIFT_A)).astype(BF)
    normed_ref[...] = normed
    queries = nn(normed, qkv_weight(weight_ref, 0)) + bias_ref[0:1, :]
    keys = nn(normed, qkv_weight(weight_ref, 1))
    values = nn(normed, qkv_weight(weight_ref, 2)) + bias_ref[1:2, :]
    mask = low_lanes((BOTH, 128))
    for pair in range(HEADS_DEV // 2):
        columns = slice(pair * 128, pair * 128 + 128)
        key_tile, value_tile, query_tile = keys[:, columns], values[:, columns], queries[:, columns]
        even = jnp.where(mask, key_tile, turn(value_tile)).astype(BF)
        odd = jnp.where(mask, turn(key_tile), value_tile).astype(BF)
        for quarter in range(QUARTERS):
            out_ref[(2 * pair) * QUARTERS + quarter, 0:BOTH, :] = even
            out_ref[(2 * pair + 1) * QUARTERS + quarter, 0:BOTH, :] = odd
        pack_heads(query_tile, out_ref, pair, BOTH)


def qkv_first_kernel(own_ref, other_ref, vec_ref, bias_ref, weight_ref, out_ref, rows_ref, normed_ref):
    rows = jnp.concatenate([own_ref[...], other_ref[...]], axis=0)
    project_and_pack(rows, vec_ref, bias_ref, weight_ref, out_ref, rows_ref, normed_ref)


def qkv_next_kernel(
    middle_ref, mlp_own_ref, mlp_recv_ref, before_ref, vec_ref, bias_ref, weight_ref,
    out_ref, rows_ref, normed_ref,
):
    branch = joined(mlp_own_ref, mlp_recv_ref) + row_of(before_ref, SHIFT_M)
    rows = (middle_ref[...] + row_of(before_ref, SCALE_M) * branch).astype(BF)
    project_and_pack(rows, vec_ref, bias_ref, weight_ref, out_ref, rows_ref, normed_ref)


def qkv_block(index):
    return pl.BlockSpec((WIDE, 48, MODEL), lambda i: (0, index, 0))


def qkv_call(inputs, small, weight, block_at):
    vec, bias, _ = small
    first = len(inputs) == 2
    return pl.pallas_call(
        qkv_first_kernel if first else qkv_next_kernel,
        grid=(1,),
        in_specs=[whole(part.shape) for part in inputs]
        + [whole((8, MODEL)), whole((2, HALF_W)), qkv_block(block_at)],
        out_specs=[whole((WIDE, SEND_ROWS, 128)), whole((BOTH, MODEL)), whole((BOTH, MODEL))],
        out_shape=[
            jax.ShapeDtypeStruct((WIDE, SEND_ROWS, 128), BF),
            jax.ShapeDtypeStruct((BOTH, MODEL), BF),
            jax.ShapeDtypeStruct((BOTH, MODEL), BF),
        ],
        compiler_params=params(),
        cost_estimate=cost(5),
    )(*inputs, vec, bias, weight)


def query_tiles(packed):
    mask = low_lanes((128, 128))
    return jnp.concatenate(
        [jnp.where(mask, packed, 0.0), jnp.where(mask, turn(packed), 0.0)], axis=0
    )


def key_chunk(recv_ref, chunk):
    half, group = chunk // 4, chunk % 4
    block = recv_ref[group * 8 : group * 8 + 8, half * ROWS : half * ROWS + ROWS, :]
    return block.reshape(512, 128)


def lane_tiles(fn, block):
    return fn(fn(block[:, 0:128], block[:, 128:256]), fn(block[:, 256:384], block[:, 384:512]))


def attend_kernel(
    flag_ref, recv_ref, key_id_ref, query_id_ref, out_ref, keep_ref, lse_ref,
    score_ref, top_ref, total_ref, acc_ref,
):
    at = pl.program_id(0)
    packed = recv_ref[pl.ds(at * 8, 8), BOTH : BOTH + 16, :].astype(F32).reshape(128, 128)
    queries = (query_tiles(packed) * SCALE).astype(BF)
    query_ids = query_id_ref[0]
    top_ref[...] = jnp.full((256, 128), NEG_FILL, F32)
    total_ref[...] = jnp.zeros((256, 128), F32)
    acc_ref[...] = jnp.zeros((256, 128), F32)
    for chunk in range(CHUNKS):

        @pl.when(flag_ref[at, chunk] != 0)
        def _():
            scores = nt(queries, key_chunk(recv_ref, chunk))
            scores = jnp.where(query_ids == key_id_ref[chunk], scores, NEG_FILL)
            score_ref[chunk] = scores
            top_ref[...] = jnp.maximum(top_ref[...], lane_tiles(jnp.maximum, scores))

    top = jnp.max(top_ref[...], axis=1, keepdims=True)
    for chunk in range(CHUNKS):

        @pl.when(flag_ref[at, chunk] != 0)
        def _():
            expo = jnp.exp(score_ref[chunk] - top)
            total_ref[...] += lane_tiles(jnp.add, expo)
            acc_ref[...] += nn(expo.astype(BF), key_chunk(recv_ref, chunk))

    total = jnp.sum(total_ref[...], axis=1, keepdims=True)
    mixture = acc_ref[...] / total
    lse_ref[...] = top + jnp.log(total)
    mask = low_lanes((128, 128))
    joined = jnp.where(mask, turn(mixture[:128]), mixture[128:]).reshape(8, 16, 128)
    keep_ref[...] = joined
    out_ref[0] = joined.astype(BF)
    out_ref[1] = joined.astype(BF)


def attend_call(flags, recv, key_ids, query_ids):
    return pl.pallas_call(
        attend_kernel,
        grid_spec=pltpu.PrefetchScalarGridSpec(
            num_scalar_prefetch=1,
            grid=(BLOCKS_Q,),
            in_specs=[
                pl.BlockSpec((WIDE, SEND_ROWS, 128), lambda i, f: (0, 0, 0)),
                pl.BlockSpec((CHUNKS, 1, 512), lambda i, f: (0, 0, 0)),
                pl.BlockSpec((1, 256, 1), lambda i, f: (i, 0, 0)),
            ],
            out_specs=[
                pl.BlockSpec((2, 8, 16, 128), lambda i, f: (0, i, 0, 0)),
                pl.BlockSpec((8, 16, 128), lambda i, f: (i, 0, 0)),
                pl.BlockSpec((256, 1), lambda i, f: (i, 0)),
            ],
            scratch_shapes=[
                pltpu.VMEM((CHUNKS, 256, 512), F32),
                pltpu.VMEM((256, 128), F32),
                pltpu.VMEM((256, 128), F32),
                pltpu.VMEM((256, 128), F32),
            ],
        ),
        out_shape=[
            jax.ShapeDtypeStruct((2, WIDE, 16, 128), BF),
            jax.ShapeDtypeStruct((WIDE, 16, 128), F32),
            jax.ShapeDtypeStruct((1024, 1), F32),
        ],
        compiler_params=params(),
        cost_estimate=cost(12),
    )(flags, recv, key_ids, query_ids)


def attend_back_kernel(
    flag_ref, recv_ref, grad_ref, keep_ref, lse_ref, key_id_ref, query_id_ref, out_ref,
    key_grad_ref, query_grad_ref,
):
    at = pl.program_id(0)

    @pl.when(at == 0)
    def _():
        key_grad_ref[...] = jnp.zeros((WIDE, BOTH, 128), F32)

    mask = low_lanes((128, 128))
    packed = recv_ref[pl.ds(at * 8, 8), BOTH : BOTH + 16, :].astype(F32).reshape(128, 128)
    queries = (query_tiles(packed) * SCALE).astype(BF)
    grads = grad_ref[...].astype(F32).reshape(128, 128)
    grad_tile = jnp.concatenate(
        [jnp.where(mask, 0.0, turn(grads)), jnp.where(mask, 0.0, grads)], axis=0
    ).astype(BF)
    product = grads * keep_ref[...].reshape(128, 128)
    delta = jnp.concatenate(
        [
            jnp.sum(jnp.where(mask, product, 0.0), axis=1, keepdims=True),
            jnp.sum(jnp.where(mask, 0.0, product), axis=1, keepdims=True),
        ],
        axis=0,
    )
    lse = lse_ref[...]
    query_ids = query_id_ref[0]
    both = jnp.concatenate([queries, grad_tile], axis=0)
    query_grad_ref[...] = jnp.zeros((256, 128), F32)
    for chunk in range(CHUNKS):

        @pl.when(flag_ref[at, chunk] != 0)
        def _():
            half, group = chunk // 4, chunk % 4
            keys = key_chunk(recv_ref, chunk)
            scores = nt(queries, keys)
            scores = jnp.where(query_ids == key_id_ref[chunk], scores, NEG_FILL)
            chance = jnp.exp(scores - lse)
            grad_scores = (chance * (nt(grad_tile, keys) - delta)).astype(BF)
            query_grad_ref[...] += nn(grad_scores, keys)
            stacked = jnp.concatenate([grad_scores, chance.astype(BF)], axis=0)
            key_grad_ref[group * 8 : group * 8 + 8, half * ROWS : half * ROWS + ROWS, :] += tn(
                stacked, both
            ).reshape(8, ROWS, 128)

    query_grad = query_grad_ref[...] * SCALE
    joined = jnp.where(mask, query_grad[:128], turn(query_grad[128:]))
    out_ref[pl.ds(at * 8, 8), BOTH : BOTH + 16, :] = joined.astype(BF).reshape(8, 16, 128)

    @pl.when(at == BLOCKS_Q - 1)
    def _():
        out_ref[:, 0:BOTH, :] = key_grad_ref[...].astype(BF)


def attend_back_call(flags, recv, grads, keep, lse, key_ids, query_ids):
    return pl.pallas_call(
        attend_back_kernel,
        grid_spec=pltpu.PrefetchScalarGridSpec(
            num_scalar_prefetch=1,
            grid=(BLOCKS_Q,),
            in_specs=[
                pl.BlockSpec((WIDE, SEND_ROWS, 128), lambda i, f: (0, 0, 0)),
                pl.BlockSpec((8, 16, 128), lambda i, f: (i, 0, 0)),
                pl.BlockSpec((8, 16, 128), lambda i, f: (i, 0, 0)),
                pl.BlockSpec((256, 1), lambda i, f: (i, 0)),
                pl.BlockSpec((CHUNKS, 1, 512), lambda i, f: (0, 0, 0)),
                pl.BlockSpec((1, 256, 1), lambda i, f: (i, 0, 0)),
            ],
            out_specs=pl.BlockSpec((WIDE, SEND_ROWS, 128), lambda i, f: (0, 0, 0)),
            scratch_shapes=[
                pltpu.VMEM((WIDE, BOTH, 128), F32),
                pltpu.VMEM((256, 128), F32),
            ],
        ),
        out_shape=jax.ShapeDtypeStruct((WIDE, SEND_ROWS, 128), BF),
        compiler_params=params(),
        cost_estimate=cost(16),
    )(flags, recv, grads, keep, lse, key_ids, query_ids)


def mlp_kernel(
    place_ref, rows_ref, recv_ref, vec_ref, bias_ref, out_weight_ref, one_ref, two_ref,
    mixture_ref, branch_ref, middle_ref, normed_ref, pre_ref, act_ref, out_ref, acc_ref,
):
    at = pl.program_id(0)

    @pl.when(at == 0)
    def _():
        tensor = place_ref[0]
        own = unpack_heads(recv_ref, 0, tensor * WIDE).astype(BF)
        partner = unpack_heads(recv_ref, 0, (1 - tensor) * WIDE).astype(BF)
        partner = jnp.concatenate([partner[ROWS:], partner[:ROWS]], axis=0)
        mixture_ref[...] = own
        proj = nn(own, out_weight_ref[:, 0:16, :].reshape(HALF_W, MODEL)) + nn(
            partner, out_weight_ref[:, 16:32, :].reshape(HALF_W, MODEL)
        )
        branch = proj + row_of(vec_ref, SHIFT_O)
        branch_ref[...] = branch
        middle = rows_ref[...].astype(F32) + row_of(vec_ref, SCALE_A) * branch
        middle_ref[...] = middle
        hat, _ = norm_parts(middle)
        normed_ref[...] = (hat * row_of(vec_ref, GAIN_C) + row_of(vec_ref, SHIFT_C)).astype(BF)

    pre = nn(normed_ref[...], one_ref[...].reshape(MODEL, MODEL)) + bias_ref[...]
    act = (0.5 * pre * (1.0 + lax.erf(pre * ROOT_HALF))).astype(BF)
    pre_ref[...] = pre
    act_ref[...] = act
    part = nn(act, two_ref[...].reshape(MODEL, MODEL))

    @pl.when(at == 0)
    def _():
        acc_ref[...] = part

    @pl.when(at == 1)
    def _():
        out_ref[...] = (acc_ref[...] + part).astype(BF)


def mlp_call(place, rows, recv, small, weights):
    vec, _, bias = small
    return pl.pallas_call(
        mlp_kernel,
        grid=(2,),
        in_specs=[
            pl.BlockSpec(memory_space=pltpu.SMEM),
            whole((BOTH, MODEL)),
            whole((2 * WIDE, 16, 128)),
            whole((8, MODEL)),
            pl.BlockSpec((1, MODEL), lambda j: (0, j)),
            pl.BlockSpec((WIDE, 32, MODEL), lambda j: (0, 4, 0)),
            pl.BlockSpec((WIDE, 32, MODEL), lambda j: (0, 2 + j, 0)),
            pl.BlockSpec((16, 64, MODEL), lambda j: (j, 0, 0)),
        ],
        out_specs=[
            whole((BOTH, HALF_W)),
            whole((BOTH, MODEL)),
            whole((BOTH, MODEL)),
            whole((BOTH, MODEL)),
            pl.BlockSpec((BOTH, MODEL), lambda j: (0, j)),
            pl.BlockSpec((BOTH, MODEL), lambda j: (0, j)),
            whole((BOTH, MODEL)),
        ],
        out_shape=[
            jax.ShapeDtypeStruct((BOTH, HALF_W), BF),
            jax.ShapeDtypeStruct((BOTH, MODEL), F32),
            jax.ShapeDtypeStruct((BOTH, MODEL), F32),
            jax.ShapeDtypeStruct((BOTH, MODEL), BF),
            jax.ShapeDtypeStruct((BOTH, HIDDEN), F32),
            jax.ShapeDtypeStruct((BOTH, HIDDEN), BF),
            jax.ShapeDtypeStruct((BOTH, MODEL), BF),
        ],
        scratch_shapes=[pltpu.VMEM((BOTH, MODEL), F32)],
        compiler_params=params(),
        cost_estimate=cost(8),
    )(place, rows, recv, vec, bias, weights, weights, weights)


def mlp_back_steps(
    grad, vec_ref, mlp_own_ref, mlp_recv_ref, pre_ref, one_ref, two_ref,
    grad_ref, low_ref, grad_pre_ref, out_ref, sums_ref, acc_ref,
):
    at = pl.program_id(0)

    @pl.when(at == 0)
    def _():
        rows = grad()
        grad_ref[...] = rows
        rows = rows.astype(F32)
        scaled = rows * row_of(vec_ref, SCALE_M)
        low_ref[...] = scaled.astype(BF)
        branch = joined(mlp_own_ref, mlp_recv_ref) + row_of(vec_ref, SHIFT_M)
        sums_ref[...] = jnp.zeros((8, MODEL), F32)
        sums_ref[0:1, :] = column_sum(scaled)
        sums_ref[1:2, :] = column_sum(rows * branch)

    pre = pre_ref[...]
    slope = 0.5 * (1.0 + lax.erf(pre * ROOT_HALF)) + pre * jnp.exp(-0.5 * pre * pre) * INV_ROOT_TAU
    grad_pre = (nt(low_ref[...], two_ref[...].reshape(MODEL, MODEL)) * slope).astype(BF)
    grad_pre_ref[...] = grad_pre
    part = nt(grad_pre, one_ref[...].reshape(MODEL, MODEL))
    bias_sum = jnp.sum(grad_pre.astype(F32), axis=0, keepdims=True)

    @pl.when(at == 0)
    def _():
        acc_ref[...] = part
        sums_ref[2:3, :] = bias_sum

    @pl.when(at == 1)
    def _():
        out_ref[...] = (acc_ref[...] + part).astype(BF)
        sums_ref[3:4, :] = bias_sum


def mlp_back_first_kernel(own_ref, other_ref, *refs):
    mlp_back_steps(lambda: jnp.concatenate([own_ref[...], other_ref[...]], axis=0), *refs)


def mlp_back_next_kernel(middle_grad_ref, part_own_ref, part_recv_ref, rows_ref, after_ref, *refs):
    *refs, input_grad_ref, acc_ref = refs

    def grad():
        hat, rstd = norm_parts(rows_ref[...].astype(F32))
        grad_norm = joined(part_own_ref, part_recv_ref)
        total = middle_grad_ref[...] + norm_back(grad_norm, hat, rstd, row_of(after_ref, GAIN_A))
        input_grad_ref[...] = total[:ROWS]
        return total.astype(BF)

    mlp_back_steps(grad, *refs, acc_ref)


def mlp_back_call(inputs, small, mlp_own, mlp_recv, pre, weights):
    first = len(inputs) == 2
    extra = [] if first else [(ROWS, MODEL)]
    return pl.pallas_call(
        mlp_back_first_kernel if first else mlp_back_next_kernel,
        grid=(2,),
        in_specs=[whole(part.shape) for part in inputs]
        + [
            whole((8, MODEL)),
            whole((BOTH, MODEL)),
            whole((BOTH, MODEL)),
            pl.BlockSpec((BOTH, MODEL), lambda j: (0, j)),
            pl.BlockSpec((WIDE, 32, MODEL), lambda j: (0, 2 + j, 0)),
            pl.BlockSpec((16, 64, MODEL), lambda j: (j, 0, 0)),
        ],
        out_specs=[
            whole((BOTH, MODEL)),
            whole((BOTH, MODEL)),
            pl.BlockSpec((BOTH, MODEL), lambda j: (0, j)),
            whole((BOTH, MODEL)),
            whole((8, MODEL)),
        ]
        + [whole(shape) for shape in extra],
        out_shape=[
            jax.ShapeDtypeStruct((BOTH, MODEL), BF),
            jax.ShapeDtypeStruct((BOTH, MODEL), BF),
            jax.ShapeDtypeStruct((BOTH, HIDDEN), BF),
            jax.ShapeDtypeStruct((BOTH, MODEL), BF),
            jax.ShapeDtypeStruct((8, MODEL), F32),
        ]
        + [jax.ShapeDtypeStruct(shape, F32) for shape in extra],
        scratch_shapes=[pltpu.VMEM((BOTH, MODEL), F32)],
        compiler_params=params(),
        cost_estimate=cost(8),
    )(*inputs, small[0], mlp_own, mlp_recv, pre, weights, weights)


PACK_ROWS = 240
CHIPS = WIDE // 2


def store_split(place_ref, value, mine_ref, away_ref, pairs, rows, columns):
    value = value.reshape(value.shape[0] // 2, 2, *value.shape[1:])
    for core in range(2):

        @pl.when(place_ref[1] == core)
        def _():
            mine_ref[pairs, rows, columns] = value[:, core]
            away_ref[pairs, rows, columns] = value[:, 1 - core]


EVERY = slice(None)


def split_spec(rows, index):
    return [pl.BlockSpec((CHIPS, rows, MODEL), lambda *g: (0, index, 0))] * 2


def split_shape(rows):
    return [jax.ShapeDtypeStruct((CHIPS, rows, MODEL), BF)] * 2


ANYWHERE = pl.BlockSpec(memory_space=pl.ANY)
SCALARS = pl.BlockSpec(memory_space=pltpu.SMEM)


def mlp_weight_grads(low_ref, normed_ref, act_ref, grad_pre_ref):
    grad_two = tn(act_ref[...], low_ref[...]).astype(BF).reshape(16, 64, MODEL)
    grad_one = tn(normed_ref[...], grad_pre_ref[...]).astype(BF).reshape(WIDE, 32, MODEL)
    return grad_two, grad_one


MLP_WEIGHT_SPECS = [
    whole((BOTH, MODEL)),
    whole((BOTH, MODEL)),
    pl.BlockSpec((BOTH, MODEL), lambda j: (0, j)),
    pl.BlockSpec((BOTH, MODEL), lambda j: (0, j)),
]


def mlp_weight_kernel(low_ref, normed_ref, act_ref, grad_pre_ref, after_ref, grad_ref):
    grad_two, grad_one = mlp_weight_grads(low_ref, normed_ref, act_ref, grad_pre_ref)
    for at in range(2):

        @pl.when(pl.program_id(0) == at)
        def _():
            grad_ref[16 * at : 16 * at + 16, 0:64, :] = grad_two
            grad_ref[:, 64 + 32 * at : 96 + 32 * at, :] = grad_one


def mlp_weight_call(low, normed, act, grad_pre, after):
    return pl.pallas_call(
        mlp_weight_kernel,
        grid=(2,),
        in_specs=MLP_WEIGHT_SPECS + [ANYWHERE],
        out_specs=whole((WIDE, 128, MODEL)),
        out_shape=jax.ShapeDtypeStruct((WIDE, 128, MODEL), BF),
        compiler_params=params(),
        cost_estimate=cost(8),
    )(low, normed, act, grad_pre, after)


def mlp_weight_split_kernel(
    place_ref, low_ref, normed_ref, act_ref, grad_pre_ref, mine_in, away_in, mine_ref, away_ref
):
    grad_two, grad_one = mlp_weight_grads(low_ref, normed_ref, act_ref, grad_pre_ref)
    for at in range(2):

        @pl.when(pl.program_id(0) == at)
        def _():
            half = slice(8 * at, 8 * at + 8)
            store_split(place_ref, grad_two, mine_ref, away_ref, half, slice(0, 64), EVERY)
            rows = slice(64 + 32 * at, 96 + 32 * at)
            store_split(place_ref, grad_one, mine_ref, away_ref, EVERY, rows, EVERY)


def mlp_weight_split_call(place, low, normed, act, grad_pre, pack):
    return pl.pallas_call(
        mlp_weight_split_kernel,
        grid=(2,),
        in_specs=[SCALARS] + MLP_WEIGHT_SPECS + [ANYWHERE] * 2,
        out_specs=split_spec(128, 0),
        out_shape=split_shape(PACK_ROWS),
        input_output_aliases={5: 0, 6: 1},
        compiler_params=params(),
        cost_estimate=cost(8),
    )(place, low, normed, act, grad_pre, *pack)


def out_back_kernel(
    grad_ref, part_own_ref, part_recv_ref, middle_ref, branch_ref, vec_ref,
    weight_ref, middle_grad_ref, send_ref, low_ref, sums_ref,
):
    hat, rstd = norm_parts(middle_ref[...])
    grad_norm = joined(part_own_ref, part_recv_ref)
    total = grad_ref[...].astype(F32) + norm_back(grad_norm, hat, rstd, row_of(vec_ref, GAIN_C))
    middle_grad_ref[...] = total
    scaled = total * row_of(vec_ref, SCALE_A)
    rows = scaled.astype(BF)
    low_ref[...] = rows
    grad_mix = nt(rows, weight_ref[...].reshape(HALF_W, MODEL))
    for pair in range(HEADS_DEV // 2):
        pack_heads(grad_mix[:, pair * 128 : pair * 128 + 128], send_ref, pair, 0)
    sums_ref[...] = jnp.zeros((8, MODEL), F32)
    sums_ref[0:1, :] = column_sum(grad_norm * hat)
    sums_ref[1:2, :] = column_sum(grad_norm)
    sums_ref[2:3, :] = column_sum(scaled)
    sums_ref[3:4, :] = column_sum(total * branch_ref[...])


def out_back_call(grad, part_own, part_recv, middle, branch, small, weights):
    return pl.pallas_call(
        out_back_kernel,
        grid=(1,),
        in_specs=[whole((BOTH, MODEL))] * 5
        + [whole((8, MODEL)), pl.BlockSpec((WIDE, 16, MODEL), lambda i: (0, 8, 0))],
        out_specs=[
            whole((BOTH, MODEL)), whole((WIDE, 16, 128)), whole((BOTH, MODEL)), whole((8, MODEL))
        ],
        out_shape=[
            jax.ShapeDtypeStruct((BOTH, MODEL), F32),
            jax.ShapeDtypeStruct((WIDE, 16, 128), BF),
            jax.ShapeDtypeStruct((BOTH, MODEL), BF),
            jax.ShapeDtypeStruct((8, MODEL), F32),
        ],
        compiler_params=params(),
        cost_estimate=cost(4),
    )(grad, part_own, part_recv, middle, branch, small[0], weights)


def out_weight_kernel(place_ref, mixture_ref, low_ref, mine_ref, away_ref):
    grad = tn(mixture_ref[...], low_ref[...]).astype(BF).reshape(WIDE, 16, MODEL)
    store_split(place_ref, grad, mine_ref, away_ref, EVERY, EVERY, EVERY)


def out_weight_last_kernel(place_ref, mixture_ref, low_ref, *refs):
    *sums_refs, before_ref, mine_in, away_in, mine_ref, away_ref = refs
    grad = tn(mixture_ref[...], low_ref[...]).astype(BF).reshape(WIDE, 16, MODEL)
    store_split(place_ref, grad, mine_ref, away_ref, EVERY, slice(0, 16), EVERY)
    parts = [ref[0:4, :] for ref in sums_refs] + [before_ref[0:12, :].astype(F32)]
    rows = jnp.concatenate(parts, axis=0).astype(BF)
    rows = jnp.broadcast_to(rows[None], (CHIPS, 32, MODEL))
    mine_ref[:, 16:48, :] = rows
    away_ref[:, 16:48, :] = rows


def out_weight_call(place, mixture, low):
    return pl.pallas_call(
        out_weight_kernel,
        grid=(1,),
        in_specs=[SCALARS, whole((BOTH, HALF_W)), whole((BOTH, MODEL))],
        out_specs=split_spec(16, 8),
        out_shape=split_shape(PACK_ROWS),
        compiler_params=params(),
        cost_estimate=cost(2),
    )(place, mixture, low)


def out_weight_last_call(place, mixture, low, sums, before, pack):
    count = 4 + len(sums)
    return pl.pallas_call(
        out_weight_last_kernel,
        grid=(1,),
        in_specs=[SCALARS, whole((BOTH, HALF_W)), whole((BOTH, MODEL))]
        + [whole((8, MODEL)) for _ in sums]
        + [whole((16, MODEL)), ANYWHERE, ANYWHERE],
        out_specs=split_spec(48, 4),
        out_shape=split_shape(PACK_ROWS),
        input_output_aliases={count: 0, count + 1: 1},
        compiler_params=params(),
        cost_estimate=cost(3),
    )(place, mixture, low, *sums, before, *pack)


def qkv_back_kernel(recv_ref, rows_ref, vec_ref, weight_ref, part_ref, grads_ref, sums_ref):
    grad_q = unpack_heads(recv_ref, BOTH).astype(BF)
    mask = low_lanes((BOTH, 128))
    key_columns, value_columns = [], []
    for pair in range(HEADS_DEV // 2):
        sums = []
        for head in (2 * pair, 2 * pair + 1):
            total = recv_ref[head * QUARTERS, 0:BOTH, :].astype(F32)
            for quarter in range(1, QUARTERS):
                total = total + recv_ref[head * QUARTERS + quarter, 0:BOTH, :].astype(F32)
            sums.append(total)
        key_columns.append(jnp.where(mask, sums[0], turn(sums[1])))
        value_columns.append(jnp.where(mask, turn(sums[0]), sums[1]))
    grad_k = jnp.concatenate(key_columns, axis=1).astype(BF)
    grad_v = jnp.concatenate(value_columns, axis=1).astype(BF)
    grads_ref[:, 0:HALF_W] = grad_q
    grads_ref[:, HALF_W:MODEL] = grad_k
    grads_ref[:, MODEL : MODEL + HALF_W] = grad_v
    result = (
        nt(grad_q, qkv_weight(weight_ref, 0))
        + nt(grad_k, qkv_weight(weight_ref, 1))
        + nt(grad_v, qkv_weight(weight_ref, 2))
    )
    part_ref[...] = result.astype(BF)
    hat, _ = norm_parts(rows_ref[...].astype(F32))
    sums_ref[...] = jnp.zeros((8, MODEL), F32)
    sums_ref[0:1, :] = column_sum(result * hat)
    sums_ref[1:2, :] = column_sum(result)
    sums_ref[2:3, 0:HALF_W] = column_sum(grad_q.astype(F32))
    sums_ref[2:3, HALF_W:MODEL] = column_sum(grad_v.astype(F32))


def qkv_back_call(recv, rows, small, weight, block_at):
    return pl.pallas_call(
        qkv_back_kernel,
        grid=(1,),
        in_specs=[
            whole((WIDE, SEND_ROWS, 128)),
            whole((BOTH, MODEL)),
            whole((8, MODEL)),
            qkv_block(block_at),
        ],
        out_specs=[whole((BOTH, MODEL)), whole((BOTH, 3 * HALF_W)), whole((8, MODEL))],
        out_shape=[
            jax.ShapeDtypeStruct((BOTH, MODEL), BF),
            jax.ShapeDtypeStruct((BOTH, 3 * HALF_W), BF),
            jax.ShapeDtypeStruct((8, MODEL), F32),
        ],
        compiler_params=params(),
        cost_estimate=cost(5),
    )(recv, rows, small[0], weight)


def store_qkv_grads(place_ref, normed_ref, grads_ref, mine_ref, away_ref):
    rows = normed_ref[...]

    def part(which):
        grads = grads_ref[:, which * HALF_W : which * HALF_W + HALF_W]
        return tn(rows, grads).astype(BF).reshape(WIDE, 32, HALF_W)

    low, high = slice(0, HALF_W), slice(HALF_W, MODEL)
    store_split(place_ref, part(0), mine_ref, away_ref, EVERY, slice(0, 32), low)
    store_split(place_ref, part(1), mine_ref, away_ref, EVERY, slice(0, 32), high)
    values = part(2)
    store_split(place_ref, values[:, 0:16], mine_ref, away_ref, EVERY, slice(32, 48), low)
    store_split(place_ref, values[:, 16:32], mine_ref, away_ref, EVERY, slice(32, 48), high)


def qkv_weight_kernel(place_ref, normed_ref, grads_ref, mine_in, away_in, mine_ref, away_ref):
    store_qkv_grads(place_ref, normed_ref, grads_ref, mine_ref, away_ref)


def qkv_weight_last_kernel(place_ref, normed_ref, grads_ref, sums_ref, mine_ref, away_ref):
    store_qkv_grads(place_ref, normed_ref, grads_ref, mine_ref, away_ref)
    rows = jnp.broadcast_to(sums_ref[...].astype(BF)[None], (CHIPS, 8, MODEL))
    mine_ref[:, 48:56, :] = rows
    away_ref[:, 48:56, :] = rows


def qkv_weight_call(place, normed, grads, pack):
    return pl.pallas_call(
        qkv_weight_kernel,
        grid=(1,),
        in_specs=[SCALARS, whole((BOTH, MODEL)), whole((BOTH, 3 * HALF_W)), ANYWHERE, ANYWHERE],
        out_specs=split_spec(48, 3),
        out_shape=split_shape(PACK_ROWS),
        input_output_aliases={3: 0, 4: 1},
        compiler_params=params(),
        cost_estimate=cost(4),
    )(place, normed, grads, *pack)


def qkv_weight_last_call(place, normed, grads, sums):
    return pl.pallas_call(
        qkv_weight_last_kernel,
        grid=(1,),
        in_specs=[SCALARS, whole((BOTH, MODEL)), whole((BOTH, 3 * HALF_W)), whole((8, MODEL))],
        out_specs=split_spec(56, 0),
        out_shape=split_shape(56),
        compiler_params=params(),
        cost_estimate=cost(4),
    )(place, normed, grads, sums)


def all_to_all(block):
    return lax.all_to_all(block, "wide", 0, 0, tiled=True)


def layer_forward(place, inputs, ids, qkv, rest, small):
    flags, key_ids, query_ids = ids
    sent, rows, normed_a = qkv_call(inputs, small, *qkv)
    recv = all_to_all(sent)
    mix_sent, mix_keep, lse = attend_call(flags, recv, key_ids, query_ids)
    mix_recv = lax.all_to_all(
        mix_sent.reshape(2 * WIDE, 16, 128), ("tensor", "wide"), 0, 0, tiled=True
    )
    mixture, branch, middle, normed_c, pre, act, mlp = mlp_call(place, rows, mix_recv, small, rest)
    mlp_recv = swap(mlp, "tensor")
    return dict(
        rows=rows, normed_a=normed_a, recv=recv, keep=mix_keep, lse=lse, mixture=mixture,
        branch=branch, middle=middle, normed_c=normed_c, pre=pre, act=act, mlp=mlp, mlp_recv=mlp_recv,
    )


def layer_backward(inputs, kept, ids, qkv, rest, small):
    flags, key_ids, query_ids = ids
    grad, low_m, grad_pre, part, mlp_sums, *input_grad = mlp_back_call(
        inputs, small, kept["mlp"], kept["mlp_recv"], kept["pre"], rest
    )
    middle_grad, mix_grad, low_a, out_sums = out_back_call(
        grad, part, swap(part, "tensor"), kept["middle"], kept["branch"], small, rest
    )
    back = attend_back_call(
        flags, kept["recv"], all_to_all(mix_grad), kept["keep"], kept["lse"], key_ids, query_ids
    )
    qkv_part, qkv_grads, qkv_sums = qkv_back_call(all_to_all(back), kept["rows"], small, *qkv)
    carried = (middle_grad, qkv_part, swap(qkv_part, "tensor"), kept["rows"])
    for_weights = dict(
        low_m=low_m, grad_pre=grad_pre, low_a=low_a, qkv_grads=qkv_grads,
        mlp_sums=mlp_sums, out_sums=out_sums, qkv_sums=qkv_sums,
    )
    return carried, for_weights, input_grad


def body(
    x_in, out_cot, image_ids, w_qkv, w_out, w_fc1, w_fc2, gains, shifts, layer_scales, qv_bias, fc1_bias
):
    section = lax.axis_index("section")
    tensor = lax.axis_index("tensor")
    wide = lax.axis_index("wide")
    is_first = section == 0

    def one(array):
        return lax.dynamic_index_in_dim(array, section, 0, keepdims=False)

    place = jnp.stack([tensor, lax.rem(wide, 2)]).astype(jnp.int32)

    qkv = w_qkv[0]
    small_rows = jnp.concatenate(
        [
            jnp.pad(jnp.concatenate([gains[0], shifts[0], layer_scales[0]], axis=0), ((0, 0), (0, 32))),
            jnp.pad(qv_bias[0], ((0, 0), (0, 48))),
            fc1_bias,
        ],
        axis=0,
    )
    pack_a = jnp.concatenate(
        [
            jnp.concatenate([qkv[:, 0], qkv[:, 1]], axis=1),
            jnp.concatenate([qkv[0:16, 2], qkv[16:32, 2]], axis=1),
            jnp.pad(small_rows, ((0, 5), (0, MODEL - 64))),
        ],
        axis=0,
    )
    own_rows, own_cot = one(x_in), one(out_cot)
    partner = swap(jnp.concatenate([own_rows, own_cot, w_out[0]], axis=0), "tensor")
    other_rows, other_cot, other_out = partner[:ROWS], partner[ROWS:BOTH], partner[BOTH:]
    pack_b = jnp.concatenate(
        [w_fc2[0], w_fc1[0][:, :MODEL], w_fc1[0][:, MODEL:], w_out[0], other_out], axis=0
    )
    other_a = swap(pack_a, "section")
    other_b = swap(pack_b, "section")

    def gather(block):
        return lax.all_gather(block, "wide", axis=0, tiled=False)

    def joined_a(first, second):
        vectors = jnp.concatenate([first[48:64, :HALF_W], second[48:64, :HALF_W]], axis=1)
        return jnp.concatenate([first[:48], second[:48], vectors], axis=0)

    attn_both = gather(jnp.where(is_first, joined_a(pack_a, other_a), joined_a(other_a, pack_a)))

    rest_first = gather(
        jnp.concatenate([jnp.where(is_first, pack_b, other_b), attn_both[0, 96:112]], axis=0)
    )

    def rest_second(rows):
        return gather(jnp.concatenate([jnp.where(is_first, other_b, pack_b), rows], axis=0))

    def small_of(layer):
        block = attn_both[:, 96:107, layer * HALF_W : layer * HALF_W + 64].astype(F32)
        vec = jnp.transpose(block[:, 0:8, 0:32], (1, 0, 2)).reshape(8, MODEL)
        bias = jnp.transpose(block[:, 8:10, 0:16], (1, 0, 2)).reshape(2, HALF_W)
        return vec, bias, block[:, 10].reshape(1, HIDDEN)

    small = (small_of(0), small_of(1))

    id_grid = one(image_ids).reshape(2, WIDE, ROWS)
    sorted_ids = jnp.where(tensor == 0, id_grid, id_grid[::-1])
    key_ids = sorted_ids.reshape(CHUNKS, 1, 512)
    quarter = lax.rem(wide, QUARTERS)
    half_ids = lax.dynamic_index_in_dim(sorted_ids, quarter // 2, 0, keepdims=False)
    quarter_ids = lax.dynamic_slice_in_dim(half_ids, lax.rem(quarter, 2) * 32, 32, 1)
    query_ids = jnp.transpose(quarter_ids.reshape(BLOCKS_Q, 8, 2, 16), (0, 2, 1, 3)).reshape(
        BLOCKS_Q, 256, 1
    )
    key_low, key_high = jnp.min(key_ids[:, 0], axis=1), jnp.max(key_ids[:, 0], axis=1)
    query_low, query_high = jnp.min(query_ids[..., 0], axis=1), jnp.max(query_ids[..., 0], axis=1)
    flags = (
        (query_low[:, None] <= key_high[None]) & (query_high[:, None] >= key_low[None])
    ).astype(jnp.int32)
    ids = (flags, key_ids, query_ids)

    qkv_parts = ((attn_both, 0), (attn_both, 1))
    kept0 = layer_forward(place, (own_rows, other_rows), ids, qkv_parts[0], rest_first, small[0])
    rest = (rest_first, rest_second(kept0["mlp"][:16]))
    kept1 = layer_forward(
        place,
        (kept0["middle"], kept0["mlp"], kept0["mlp_recv"], small[0][0]),
        ids, qkv_parts[1], rest[1], small[1],
    )
    branch1 = kept1["mlp"][:ROWS].astype(F32) + kept1["mlp_recv"][ROWS:].astype(F32)
    out1 = (
        kept1["middle"][:ROWS]
        + small[1][0][SCALE_M] * (branch1 + small[1][0][SHIFT_M])
    ).astype(BF)
    out0 = kept1["rows"][:ROWS]

    def rs(pack):
        return lax.psum_scatter(
            pack.reshape(WIDE * pack.shape[1], MODEL), "wide", scatter_dimension=0, tiled=True
        )

    carried1, back1, _ = layer_backward(
        (own_cot, other_cot), kept1, ids, qkv_parts[1], rest[1], small[1]
    )
    sum_mlp1 = rs(
        mlp_weight_call(
            back1["low_m"], kept1["normed_c"], kept1["act"], back1["grad_pre"], back1["out_sums"]
        )
    )
    pack = out_weight_call(place, kept1["mixture"], back1["low_a"])
    pack = qkv_weight_call(place, kept1["normed_a"], back1["qkv_grads"], pack)

    carried0, back0, (grad_x1,) = layer_backward(
        carried1 + (small[1][0],), kept0, ids, qkv_parts[0], rest[0], small[0]
    )
    pack = mlp_weight_split_call(
        place, back0["low_m"], kept0["normed_c"], kept0["act"], back0["grad_pre"], pack
    )
    pack = out_weight_last_call(
        place,
        kept0["mixture"],
        back0["low_a"],
        (back1["mlp_sums"], back1["out_sums"], back1["qkv_sums"], back0["mlp_sums"], back0["out_sums"]),
        sum_mlp1,
        pack,
    )

    same_core = [list(range(core, WIDE, 2)) for core in range(2)]

    def over_chip(mine, away):
        came = lax.ppermute(away, "wide", [(i, i ^ 1) for i in range(WIDE)])
        return (mine.astype(F32) + came.astype(F32)).astype(BF)

    sum_mid = lax.psum_scatter(
        over_chip(*pack).reshape(CHIPS * PACK_ROWS, MODEL),
        "wide", scatter_dimension=0, axis_index_groups=same_core, tiled=True,
    )
    last_pack = qkv_weight_last_call(place, kept0["normed_a"], back0["qkv_grads"], back0["qkv_sums"])
    last_recv = lax.all_to_all(
        over_chip(*last_pack), "wide", 0, 0, axis_index_groups=same_core, tiled=True
    )
    sum_last = jnp.sum(last_recv.astype(F32), axis=0)

    middle_grad0, part0, part_recv0, _ = carried0
    hat0, rstd0 = norm_parts(own_rows.astype(F32))
    grad_norm0 = part0[:ROWS].astype(F32) + part_recv0[ROWS:].astype(F32)
    grad_x0 = middle_grad0[:ROWS] + norm_back(grad_norm0, hat0, rstd0, small[0][0][GAIN_A])

    def lanes(rows, width):
        return lax.dynamic_slice_in_dim(rows, wide * width, width, rows.ndim - 1)

    def own_sums(mlp, outs, qkv_rows):
        norms = jnp.concatenate([mlp[0:2], outs, qkv_rows[0:2]], axis=0)
        pair = qkv_rows[2].reshape(2, HALF_W)
        return jnp.concatenate(
            [lanes(norms, 32).reshape(-1), lanes(pair, 16).reshape(-1), lanes(mlp[2:4].reshape(-1), 64)]
        )

    sums = sum_mid[208:228]
    mlp1, outs1, qkv1, mlp0, outs0 = (sums[at : at + 4] for at in range(0, 20, 4))
    mid0 = jnp.concatenate([sum_mid[0:128], sum_mid[192:208]], axis=0)
    mid1 = jnp.concatenate([sum_mlp1, sum_mid[128:144]], axis=0)
    mid_total = jnp.where(is_first, mid0, mid1).astype(F32) + swap(
        jnp.where(is_first, mid1, mid0), "section"
    ).astype(F32)

    def with_sums(rows, vector):
        return jnp.concatenate([rows, jnp.pad(vector, (0, 672)).reshape(1, MODEL)], axis=0)

    late0 = with_sums(sum_last[0:48].astype(BF), own_sums(mlp0, outs0, sum_last[48:52].astype(BF)))
    late1 = with_sums(sum_mid[144:192], own_sums(mlp1, outs1, qkv1))
    late_own = jnp.where(is_first, late0, late1)
    late_away = jnp.where(is_first, late1, late0)
    late_total = late_own.astype(F32) + swap(late_away, "section").astype(F32)
    own_part, away_part = late_own[48, 192:256], late_away[48, 192:256]
    across = lax.ppermute(away_part, ("section", "tensor"), [(0, 3), (3, 0), (1, 2), (2, 1)])
    heads_total = late_total[48, 192:256] + (
        swap(own_part, "tensor").astype(F32) + across.astype(F32)
    )
    mlp_total, out_total = mid_total[0:128], mid_total[128:144]
    qkv_total, tiny = late_total[0:48], late_total[48]
    norms = jnp.concatenate([tiny[0:192], heads_total]).reshape(8, 32)
    g_gains = jnp.stack([norms[6], norms[2]])
    g_shifts = jnp.stack([norms[7], norms[4], norms[3], norms[0]])
    g_scales = jnp.stack([norms[5], norms[1]])
    g_qv = tiny[256:288].reshape(2, 16)
    g_fc1_bias = tiny[288:352]
    g_fc2 = mlp_total[0:64]
    g_fc1 = jnp.concatenate([mlp_total[64:96], mlp_total[96:128]], axis=1)
    pairs = qkv_total[0:32]
    value_grad = jnp.concatenate([qkv_total[32:48, :HALF_W], qkv_total[32:48, HALF_W:]], axis=0)
    g_qkv = jnp.stack([pairs[:, :HALF_W], pairs[:, HALF_W:], value_grad], axis=1)

    def by_micro(first, second):
        own = jnp.where(is_first, first, second)
        came = swap(jnp.where(is_first, second, first), "section")
        return jnp.stack([jnp.where(is_first, own, came), jnp.where(is_first, came, own)])

    return (
        by_micro(out0, out1)[None],
        by_micro(grad_x0, grad_x1)[None],
        g_qkv[None],
        out_total[None],
        g_fc1[None],
        g_fc2[None],
        g_gains[None],
        g_shifts[None],
        g_scales[None],
        g_qv[None],
        g_fc1_bias[None],
    )


def solution(mesh):
    in_specs = (
        P(None, ("tensor", "wide"), None),
        P(None, ("tensor", "wide"), None),
        P(),
        P("section", "wide", None, "tensor"),
        P("section", ("tensor", "wide"), None),
        P("section", "wide", "tensor"),
        P("section", ("tensor", "wide"), None),
        P("section", None, "wide"),
        P("section", None, "wide"),
        P("section", None, "wide"),
        P("section", None, ("tensor", "wide")),
        P("section", ("tensor", "wide")),
    )
    out_specs = (
        P("section", None, ("tensor", "wide"), None),
        P("section", None, ("tensor", "wide"), None),
        P("section", "wide", None, "tensor"),
        P("section", ("tensor", "wide"), None),
        P("section", "wide", "tensor"),
        P("section", ("tensor", "wide"), None),
        P("section", None, "wide"),
        P("section", None, "wide"),
        P("section", None, "wide"),
        P("section", None, ("tensor", "wide")),
        P("section", ("tensor", "wide")),
    )
    return jax.shard_map(body, mesh=mesh, in_specs=in_specs, out_specs=out_specs, check_vma=False)
```

```python
import jax
import jax.numpy as jnp
from jax import lax
from jax.experimental import pallas as pl
from jax.experimental.pallas import tpu as pltpu
from jax.sharding import PartitionSpec as P

HEAD = 64
EPS = 1e-06
NEG_FILL = -1e30
ROOT_HALF = 0.7071067811865476
INV_ROOT_TAU = 0.3989422804014327
SCALE = HEAD ** (-0.5)
BF = jnp.bfloat16
F32 = jnp.float32
MIB = 1024 * 1024

ROWS = 64
BOTH = 128
WIDE = 32
HEADS_DEV = 8
QUARTERS = 4
HALF_W = 512
MODEL = 1024
HIDDEN = 2048
SEND_ROWS = 144
BLOCKS_Q = 4
CHUNKS = 8


def params(limit=56):
    return pltpu.CompilerParams(vmem_limit_bytes=limit * MIB)


def cost(micros):
    return pl.CostEstimate(flops=int(micros * 1e9), bytes_accessed=100000, transcendentals=0)


def whole(shape):
    count = len(shape)
    return pl.BlockSpec(shape, lambda *g: (0,) * count)


def swap(block, axis):
    return lax.ppermute(block, axis, [(0, 1), (1, 0)])


def nt(left, right):
    return lax.dot_general(left, right, (((1,), (1,)), ((), ())), preferred_element_type=F32)


def tn(left, right):
    return lax.dot_general(left, right, (((0,), (0,)), ((), ())), preferred_element_type=F32)


def nn(left, right):
    return jnp.dot(left, right, preferred_element_type=F32)


def low_lanes(shape):
    return lax.broadcasted_iota(jnp.int32, shape, len(shape) - 1) < HEAD


def turn(tile):
    return pltpu.roll(tile, HEAD, 1)


def pack_heads(tile, out_ref, pair, row0):
    rolled = turn(tile)
    for quarter in range(QUARTERS):
        first = slice(quarter * 32, quarter * 32 + 16)
        second = slice(quarter * 32 + 16, quarter * 32 + 32)
        mask = low_lanes((16, 128))
        even = jnp.where(mask, tile[first], rolled[second])
        odd = jnp.where(mask, rolled[first], tile[second])
        out_ref[(2 * pair) * QUARTERS + quarter, row0 : row0 + 16, :] = even.astype(BF)
        out_ref[(2 * pair + 1) * QUARTERS + quarter, row0 : row0 + 16, :] = odd.astype(BF)


def unpack_heads(in_ref, row0, base=0):
    mask = low_lanes((16, 128))
    columns = []
    for pair in range(HEADS_DEV // 2):
        pieces = []
        for quarter in range(QUARTERS):
            even = in_ref[base + (2 * pair) * QUARTERS + quarter, row0 : row0 + 16, :].astype(F32)
            odd = in_ref[base + (2 * pair + 1) * QUARTERS + quarter, row0 : row0 + 16, :].astype(F32)
            pieces.append(jnp.where(mask, even, turn(odd)))
            pieces.append(jnp.where(mask, turn(even), odd))
        columns.append(jnp.concatenate(pieces, axis=0))
    return jnp.concatenate(columns, axis=1)


def norm_parts(rows_in):
    centre = jnp.mean(rows_in, axis=-1, keepdims=True)
    centred = rows_in - centre
    spread = jnp.mean(centred * centred, axis=-1, keepdims=True)
    rstd_rows = lax.rsqrt(spread + EPS)
    return centred * rstd_rows, rstd_rows


def norm_back(grad_rows, normal_rows, rstd_rows, gain_row):
    scaled = grad_rows * gain_row
    first_mean = jnp.mean(scaled, axis=-1, keepdims=True)
    second_mean = jnp.mean(scaled * normal_rows, axis=-1, keepdims=True)
    return rstd_rows * (scaled - first_mean - normal_rows * second_mean)


def joined(own_ref, recv_ref):
    recv = jnp.concatenate([recv_ref[ROWS:], recv_ref[:ROWS]], axis=0)
    return own_ref[...].astype(F32) + recv.astype(F32)


def column_sum(rows):
    return jnp.sum(rows[:ROWS], axis=0, keepdims=True) + jnp.sum(rows[ROWS:], axis=0, keepdims=True)


GAIN_A, GAIN_C, SHIFT_A, SHIFT_O, SHIFT_C, SHIFT_M, SCALE_A, SCALE_M = range(8)


def row_of(ref, at):
    return ref[at : at + 1, :]


def qkv_weight(ref, which):
    if which < 2:
        return ref[:, 0:32, which * HALF_W : which * HALF_W + HALF_W].reshape(MODEL, HALF_W)
    parts = [ref[:, 32:48, 0:HALF_W], ref[:, 32:48, HALF_W:MODEL]]
    return jnp.concatenate(parts, axis=1).reshape(MODEL, HALF_W)


def project_and_pack(rows, vec_ref, bias_ref, weight_ref, out_ref, rows_ref, normed_ref):
    rows_ref[...] = rows
    hat, _ = norm_parts(rows.astype(F32))
    normed = (hat * row_of(vec_ref, GAIN_A) + row_of(vec_ref, SHIFT_A)).astype(BF)
    normed_ref[...] = normed
    queries = nn(normed, qkv_weight(weight_ref, 0)) + bias_ref[0:1, :]
    keys = nn(normed, qkv_weight(weight_ref, 1))
    values = nn(normed, qkv_weight(weight_ref, 2)) + bias_ref[1:2, :]
    mask = low_lanes((BOTH, 128))
    for pair in range(HEADS_DEV // 2):
        columns = slice(pair * 128, pair * 128 + 128)
        key_tile, value_tile, query_tile = keys[:, columns], values[:, columns], queries[:, columns]
        even = jnp.where(mask, key_tile, turn(value_tile)).astype(BF)
        odd = jnp.where(mask, turn(key_tile), value_tile).astype(BF)
        for quarter in range(QUARTERS):
            out_ref[(2 * pair) * QUARTERS + quarter, 0:BOTH, :] = even
            out_ref[(2 * pair + 1) * QUARTERS + quarter, 0:BOTH, :] = odd
        pack_heads(query_tile, out_ref, pair, BOTH)


def qkv_first_kernel(own_ref, other_ref, vec_ref, bias_ref, weight_ref, out_ref, rows_ref, normed_ref):
    rows = jnp.concatenate([own_ref[...], other_ref[...]], axis=0)
    project_and_pack(rows, vec_ref, bias_ref, weight_ref, out_ref, rows_ref, normed_ref)


def qkv_next_kernel(
    middle_ref, mlp_own_ref, mlp_recv_ref, before_ref, vec_ref, bias_ref, weight_ref,
    out_ref, rows_ref, normed_ref,
):
    branch = joined(mlp_own_ref, mlp_recv_ref) + row_of(before_ref, SHIFT_M)
    rows = (middle_ref[...] + row_of(before_ref, SCALE_M) * branch).astype(BF)
    project_and_pack(rows, vec_ref, bias_ref, weight_ref, out_ref, rows_ref, normed_ref)


def qkv_block(index):
    return pl.BlockSpec((WIDE, 48, MODEL), lambda i: (0, index, 0))


def qkv_call(inputs, small, weight, block_at):
    vec, bias, _ = small
    first = len(inputs) == 2
    return pl.pallas_call(
        qkv_first_kernel if first else qkv_next_kernel,
        grid=(1,),
        in_specs=[whole(part.shape) for part in inputs]
        + [whole((8, MODEL)), whole((2, HALF_W)), qkv_block(block_at)],
        out_specs=[whole((WIDE, SEND_ROWS, 128)), whole((BOTH, MODEL)), whole((BOTH, MODEL))],
        out_shape=[
            jax.ShapeDtypeStruct((WIDE, SEND_ROWS, 128), BF),
            jax.ShapeDtypeStruct((BOTH, MODEL), BF),
            jax.ShapeDtypeStruct((BOTH, MODEL), BF),
        ],
        compiler_params=params(),
        cost_estimate=cost(5),
    )(*inputs, vec, bias, weight)


def query_tiles(packed):
    mask = low_lanes((128, 128))
    return jnp.concatenate(
        [jnp.where(mask, packed, 0.0), jnp.where(mask, turn(packed), 0.0)], axis=0
    )


def key_chunk(recv_ref, chunk):
    half, group = chunk // 4, chunk % 4
    block = recv_ref[group * 8 : group * 8 + 8, half * ROWS : half * ROWS + ROWS, :]
    return block.reshape(512, 128)


def lane_tiles(fn, block):
    return fn(fn(block[:, 0:128], block[:, 128:256]), fn(block[:, 256:384], block[:, 384:512]))


def attend_kernel(
    flag_ref, recv_ref, key_id_ref, query_id_ref, out_ref, keep_ref, lse_ref,
    score_ref, top_ref, total_ref, acc_ref,
):
    at = pl.program_id(0)
    packed = recv_ref[pl.ds(at * 8, 8), BOTH : BOTH + 16, :].astype(F32).reshape(128, 128)
    queries = (query_tiles(packed) * SCALE).astype(BF)
    query_ids = query_id_ref[0]
    top_ref[...] = jnp.full((256, 128), NEG_FILL, F32)
    total_ref[...] = jnp.zeros((256, 128), F32)
    acc_ref[...] = jnp.zeros((256, 128), F32)
    for chunk in range(CHUNKS):

        @pl.when(flag_ref[at, chunk] != 0)
        def _():
            scores = nt(queries, key_chunk(recv_ref, chunk))
            scores = jnp.where(query_ids == key_id_ref[chunk], scores, NEG_FILL)
            score_ref[chunk] = scores
            top_ref[...] = jnp.maximum(top_ref[...], lane_tiles(jnp.maximum, scores))

    top = jnp.max(top_ref[...], axis=1, keepdims=True)
    for chunk in range(CHUNKS):

        @pl.when(flag_ref[at, chunk] != 0)
        def _():
            expo = jnp.exp(score_ref[chunk] - top)
            total_ref[...] += lane_tiles(jnp.add, expo)
            acc_ref[...] += nn(expo.astype(BF), key_chunk(recv_ref, chunk))

    total = jnp.sum(total_ref[...], axis=1, keepdims=True)
    mixture = acc_ref[...] / total
    lse_ref[...] = top + jnp.log(total)
    mask = low_lanes((128, 128))
    joined = jnp.where(mask, turn(mixture[:128]), mixture[128:]).reshape(8, 16, 128)
    keep_ref[...] = joined
    out_ref[0] = joined.astype(BF)
    out_ref[1] = joined.astype(BF)


def attend_call(flags, recv, key_ids, query_ids):
    return pl.pallas_call(
        attend_kernel,
        grid_spec=pltpu.PrefetchScalarGridSpec(
            num_scalar_prefetch=1,
            grid=(BLOCKS_Q,),
            in_specs=[
                pl.BlockSpec((WIDE, SEND_ROWS, 128), lambda i, f: (0, 0, 0)),
                pl.BlockSpec((CHUNKS, 1, 512), lambda i, f: (0, 0, 0)),
                pl.BlockSpec((1, 256, 1), lambda i, f: (i, 0, 0)),
            ],
            out_specs=[
                pl.BlockSpec((2, 8, 16, 128), lambda i, f: (0, i, 0, 0)),
                pl.BlockSpec((8, 16, 128), lambda i, f: (i, 0, 0)),
                pl.BlockSpec((256, 1), lambda i, f: (i, 0)),
            ],
            scratch_shapes=[
                pltpu.VMEM((CHUNKS, 256, 512), F32),
                pltpu.VMEM((256, 128), F32),
                pltpu.VMEM((256, 128), F32),
                pltpu.VMEM((256, 128), F32),
            ],
        ),
        out_shape=[
            jax.ShapeDtypeStruct((2, WIDE, 16, 128), BF),
            jax.ShapeDtypeStruct((WIDE, 16, 128), F32),
            jax.ShapeDtypeStruct((1024, 1), F32),
        ],
        compiler_params=params(),
        cost_estimate=cost(12),
    )(flags, recv, key_ids, query_ids)


def attend_back_kernel(
    flag_ref, recv_ref, grad_ref, keep_ref, lse_ref, key_id_ref, query_id_ref, out_ref,
    key_grad_ref, query_grad_ref,
):
    at = pl.program_id(0)

    @pl.when(at == 0)
    def _():
        key_grad_ref[...] = jnp.zeros((WIDE, BOTH, 128), F32)

    mask = low_lanes((128, 128))
    packed = recv_ref[pl.ds(at * 8, 8), BOTH : BOTH + 16, :].astype(F32).reshape(128, 128)
    queries = (query_tiles(packed) * SCALE).astype(BF)
    grads = grad_ref[...].astype(F32).reshape(128, 128)
    grad_tile = jnp.concatenate(
        [jnp.where(mask, 0.0, turn(grads)), jnp.where(mask, 0.0, grads)], axis=0
    ).astype(BF)
    product = grads * keep_ref[...].reshape(128, 128)
    delta = jnp.concatenate(
        [
            jnp.sum(jnp.where(mask, product, 0.0), axis=1, keepdims=True),
            jnp.sum(jnp.where(mask, 0.0, product), axis=1, keepdims=True),
        ],
        axis=0,
    )
    lse = lse_ref[...]
    query_ids = query_id_ref[0]
    both = jnp.concatenate([queries, grad_tile], axis=0)
    query_grad_ref[...] = jnp.zeros((256, 128), F32)
    for chunk in range(CHUNKS):

        @pl.when(flag_ref[at, chunk] != 0)
        def _():
            half, group = chunk // 4, chunk % 4
            keys = key_chunk(recv_ref, chunk)
            scores = nt(queries, keys)
            scores = jnp.where(query_ids == key_id_ref[chunk], scores, NEG_FILL)
            chance = jnp.exp(scores - lse)
            grad_scores = (chance * (nt(grad_tile, keys) - delta)).astype(BF)
            query_grad_ref[...] += nn(grad_scores, keys)
            stacked = jnp.concatenate([grad_scores, chance.astype(BF)], axis=0)
            key_grad_ref[group * 8 : group * 8 + 8, half * ROWS : half * ROWS + ROWS, :] += tn(
                stacked, both
            ).reshape(8, ROWS, 128)

    query_grad = query_grad_ref[...] * SCALE
    joined = jnp.where(mask, query_grad[:128], turn(query_grad[128:]))
    out_ref[pl.ds(at * 8, 8), BOTH : BOTH + 16, :] = joined.astype(BF).reshape(8, 16, 128)

    @pl.when(at == BLOCKS_Q - 1)
    def _():
        out_ref[:, 0:BOTH, :] = key_grad_ref[...].astype(BF)


def attend_back_call(flags, recv, grads, keep, lse, key_ids, query_ids):
    return pl.pallas_call(
        attend_back_kernel,
        grid_spec=pltpu.PrefetchScalarGridSpec(
            num_scalar_prefetch=1,
            grid=(BLOCKS_Q,),
            in_specs=[
                pl.BlockSpec((WIDE, SEND_ROWS, 128), lambda i, f: (0, 0, 0)),
                pl.BlockSpec((8, 16, 128), lambda i, f: (i, 0, 0)),
                pl.BlockSpec((8, 16, 128), lambda i, f: (i, 0, 0)),
                pl.BlockSpec((256, 1), lambda i, f: (i, 0)),
                pl.BlockSpec((CHUNKS, 1, 512), lambda i, f: (0, 0, 0)),
                pl.BlockSpec((1, 256, 1), lambda i, f: (i, 0, 0)),
            ],
            out_specs=pl.BlockSpec((WIDE, SEND_ROWS, 128), lambda i, f: (0, 0, 0)),
            scratch_shapes=[
                pltpu.VMEM((WIDE, BOTH, 128), F32),
                pltpu.VMEM((256, 128), F32),
            ],
        ),
        out_shape=jax.ShapeDtypeStruct((WIDE, SEND_ROWS, 128), BF),
        compiler_params=params(),
        cost_estimate=cost(16),
    )(flags, recv, grads, keep, lse, key_ids, query_ids)


KEPT_C, KEPT_A, KEPT_MIX = slice(2048, 3072), slice(3072, 4096), slice(4096, 4608)
KEPT_WIDTH = 4608
TALL = BOTH + 16


def mlp_kernel(
    place_ref, rows_ref, normed_ref, recv_ref, vec_ref, bias_ref, out_weight_ref, one_ref, two_ref,
    branch_ref, middle_ref, pre_ref, kept_ref, out_ref, acc_ref,
):
    at = pl.program_id(0)

    @pl.when(at == 0)
    def _():
        tensor = place_ref[0]
        own = unpack_heads(recv_ref, 0, tensor * WIDE).astype(BF)
        partner = unpack_heads(recv_ref, 0, (1 - tensor) * WIDE).astype(BF)
        partner = jnp.concatenate([partner[ROWS:], partner[:ROWS]], axis=0)
        kept_ref[:, KEPT_A] = normed_ref[...]
        kept_ref[:, KEPT_MIX] = own
        proj = nn(own, out_weight_ref[:, 0:16, :].reshape(HALF_W, MODEL)) + nn(
            partner, out_weight_ref[:, 16:32, :].reshape(HALF_W, MODEL)
        )
        branch = proj + row_of(vec_ref, SHIFT_O)
        branch_ref[...] = branch
        middle = rows_ref[...].astype(F32) + row_of(vec_ref, SCALE_A) * branch
        middle_ref[...] = middle
        hat, _ = norm_parts(middle)
        kept_ref[:, KEPT_C] = (hat * row_of(vec_ref, GAIN_C) + row_of(vec_ref, SHIFT_C)).astype(BF)

    pre = nn(kept_ref[:, KEPT_C], one_ref[...].reshape(MODEL, MODEL)) + bias_ref[...]
    act = (0.5 * pre * (1.0 + lax.erf(pre * ROOT_HALF))).astype(BF)
    pre_ref[...] = pre
    part = nn(act, two_ref[...].reshape(MODEL, MODEL))

    @pl.when(at == 0)
    def _():
        kept_ref[:, 0:MODEL] = act
        acc_ref[...] = part

    @pl.when(at == 1)
    def _():
        kept_ref[:, MODEL:HIDDEN] = act
        out_ref[...] = (acc_ref[...] + part).astype(BF)


def mlp_call(place, rows, normed, recv, small, weights):
    vec, _, bias = small
    return pl.pallas_call(
        mlp_kernel,
        grid=(2,),
        in_specs=[
            pl.BlockSpec(memory_space=pltpu.SMEM),
            whole((BOTH, MODEL)),
            whole((BOTH, MODEL)),
            whole((2 * WIDE, 16, 128)),
            whole((8, MODEL)),
            pl.BlockSpec((1, MODEL), lambda j: (0, j)),
            pl.BlockSpec((WIDE, 32, MODEL), lambda j: (0, 4, 0)),
            pl.BlockSpec((WIDE, 32, MODEL), lambda j: (0, 2 + j, 0)),
            pl.BlockSpec((16, 64, MODEL), lambda j: (j, 0, 0)),
        ],
        out_specs=[
            whole((BOTH, MODEL)),
            whole((BOTH, MODEL)),
            pl.BlockSpec((BOTH, MODEL), lambda j: (0, j)),
            whole((BOTH, KEPT_WIDTH)),
            whole((BOTH, MODEL)),
        ],
        out_shape=[
            jax.ShapeDtypeStruct((BOTH, MODEL), F32),
            jax.ShapeDtypeStruct((BOTH, MODEL), F32),
            jax.ShapeDtypeStruct((BOTH, HIDDEN), F32),
            jax.ShapeDtypeStruct((BOTH, KEPT_WIDTH), BF),
            jax.ShapeDtypeStruct((BOTH, MODEL), BF),
        ],
        scratch_shapes=[pltpu.VMEM((BOTH, MODEL), F32)],
        compiler_params=params(),
        cost_estimate=cost(8),
    )(place, rows, normed, recv, vec, bias, weights, weights, weights)


def mlp_back_steps(
    grad, vec_ref, mlp_own_ref, mlp_recv_ref, pre_ref, one_ref, two_ref,
    grad_ref, back_ref, out_ref, acc_ref, sums_ref,
):
    at = pl.program_id(0)

    @pl.when(at == 0)
    def _():
        rows = grad()
        grad_ref[...] = rows
        rows = rows.astype(F32)
        scaled = rows * row_of(vec_ref, SCALE_M)
        back_ref[0:BOTH, 2048:3072] = scaled.astype(BF)
        branch = joined(mlp_own_ref, mlp_recv_ref) + row_of(vec_ref, SHIFT_M)
        sums_ref[...] = jnp.zeros((16, MODEL), F32)
        sums_ref[0:1, :] = column_sum(scaled)
        sums_ref[1:2, :] = column_sum(rows * branch)

    pre = pre_ref[...]
    slope = 0.5 * (1.0 + lax.erf(pre * ROOT_HALF)) + pre * jnp.exp(-0.5 * pre * pre) * INV_ROOT_TAU
    grad_pre = (nt(back_ref[0:BOTH, 2048:3072], two_ref[...].reshape(MODEL, MODEL)) * slope).astype(BF)
    part = nt(grad_pre, one_ref[...].reshape(MODEL, MODEL))
    bias_sum = jnp.sum(grad_pre.astype(F32), axis=0, keepdims=True)

    @pl.when(at == 0)
    def _():
        back_ref[0:BOTH, 0:MODEL] = grad_pre
        acc_ref[...] = part
        sums_ref[2:3, :] = bias_sum

    @pl.when(at == 1)
    def _():
        back_ref[0:BOTH, MODEL:HIDDEN] = grad_pre
        out_ref[...] = (acc_ref[...] + part).astype(BF)
        sums_ref[3:4, :] = bias_sum
        back_ref[BOTH:TALL, 0:MODEL] = sums_ref[...].astype(BF)
        back_ref[BOTH:TALL, MODEL:3072] = jnp.zeros((16, 2048), BF)


def mlp_back_first_kernel(own_ref, other_ref, *refs):
    mlp_back_steps(lambda: jnp.concatenate([own_ref[...], other_ref[...]], axis=0), *refs)


def mlp_back_next_kernel(middle_grad_ref, part_own_ref, part_recv_ref, rows_ref, after_ref, *refs):
    *refs, input_grad_ref, acc_ref, sums_ref = refs

    def grad():
        hat, rstd = norm_parts(rows_ref[...].astype(F32))
        grad_norm = joined(part_own_ref, part_recv_ref)
        total = middle_grad_ref[...] + norm_back(grad_norm, hat, rstd, row_of(after_ref, GAIN_A))
        input_grad_ref[...] = total[:ROWS]
        return total.astype(BF)

    mlp_back_steps(grad, *refs, acc_ref, sums_ref)


def mlp_back_call(inputs, small, mlp_own, mlp_recv, pre, weights):
    first = len(inputs) == 2
    extra = [] if first else [(ROWS, MODEL)]
    return pl.pallas_call(
        mlp_back_first_kernel if first else mlp_back_next_kernel,
        grid=(2,),
        in_specs=[whole(part.shape) for part in inputs]
        + [
            whole((8, MODEL)),
            whole((BOTH, MODEL)),
            whole((BOTH, MODEL)),
            pl.BlockSpec((BOTH, MODEL), lambda j: (0, j)),
            pl.BlockSpec((WIDE, 32, MODEL), lambda j: (0, 2 + j, 0)),
            pl.BlockSpec((16, 64, MODEL), lambda j: (j, 0, 0)),
        ],
        out_specs=[whole((BOTH, MODEL)), whole((TALL, 3072)), whole((BOTH, MODEL))]
        + [whole(shape) for shape in extra],
        out_shape=[
            jax.ShapeDtypeStruct((BOTH, MODEL), BF),
            jax.ShapeDtypeStruct((TALL, 3072), BF),
            jax.ShapeDtypeStruct((BOTH, MODEL), BF),
        ]
        + [jax.ShapeDtypeStruct(shape, F32) for shape in extra],
        scratch_shapes=[pltpu.VMEM((BOTH, MODEL), F32), pltpu.VMEM((16, MODEL), F32)],
        compiler_params=params(),
        cost_estimate=cost(8),
    )(*inputs, small[0], mlp_own, mlp_recv, pre, weights, weights)


PACK_ROWS = 240
CHIPS = WIDE // 2


ANYWHERE = pl.BlockSpec(memory_space=pl.ANY)
SCALARS = pl.BlockSpec(memory_space=pltpu.SMEM)
EVERY = slice(None)


def store_mine(place_ref, value, grad_ref, pairs, rows, columns):
    value = value.reshape(value.shape[0] // 2, 2, *value.shape[1:])
    for core in range(2):

        @pl.when(place_ref[1] == core)
        def _():
            grad_ref[pairs, rows, columns] = value[:, core].astype(BF)


def both_cores(own_ref, other_ref):
    return jnp.concatenate([own_ref[0:BOTH], other_ref[0:BOTH]], axis=0)


def twice(spec):
    return [spec, spec]


def mlp_weight_kernel(place_ref, *refs):
    act, normed, low, grad_pre = (both_cores(*refs[at : at + 2]) for at in range(0, 8, 2))
    grad_ref = refs[-1]
    grad_two = tn(act, low).reshape(16, 64, MODEL)
    grad_one = tn(normed, grad_pre).reshape(WIDE, 32, MODEL)
    for at in range(2):

        @pl.when(pl.program_id(0) == at)
        def _():
            store_mine(
                place_ref, grad_two, grad_ref, slice(8 * at, 8 * at + 8), slice(0, 64), EVERY
            )
            rows = slice(64 + 32 * at, 96 + 32 * at)
            store_mine(place_ref, grad_one, grad_ref, EVERY, rows, EVERY)


def mlp_weight_call(place, kept, back, more, pack=None):
    rows, extra, aliases = 128, [more], {}
    if pack is not None:
        rows, extra, aliases = PACK_ROWS, [pack], {9: 0}
    return pl.pallas_call(
        mlp_weight_kernel,
        grid=(2,),
        in_specs=[SCALARS]
        + twice(pl.BlockSpec((BOTH, MODEL), lambda j: (0, j)))
        + twice(pl.BlockSpec((BOTH, MODEL), lambda j: (0, 2)))
        + twice(pl.BlockSpec((BOTH, MODEL), lambda j: (0, 2)))
        + twice(pl.BlockSpec((BOTH, MODEL), lambda j: (0, j)))
        + [ANYWHERE],
        out_specs=pl.BlockSpec((CHIPS, 128, MODEL), lambda j: (0, 0, 0)),
        out_shape=jax.ShapeDtypeStruct((CHIPS, rows, MODEL), BF),
        input_output_aliases=aliases,
        compiler_params=params(),
        cost_estimate=cost(7),
    )(place, *kept, *kept, *back, *back, *extra)


def out_back_kernel(
    grad_ref, part_own_ref, part_recv_ref, middle_ref, branch_ref, vec_ref,
    weight_ref, middle_grad_ref, send_ref, low_ref, sums_ref,
):
    hat, rstd = norm_parts(middle_ref[...])
    grad_norm = joined(part_own_ref, part_recv_ref)
    total = grad_ref[...].astype(F32) + norm_back(grad_norm, hat, rstd, row_of(vec_ref, GAIN_C))
    middle_grad_ref[...] = total
    scaled = total * row_of(vec_ref, SCALE_A)
    rows = scaled.astype(BF)
    low_ref[0:BOTH, :] = rows
    grad_mix = nt(rows, weight_ref[...].reshape(HALF_W, MODEL))
    for pair in range(HEADS_DEV // 2):
        pack_heads(grad_mix[:, pair * 128 : pair * 128 + 128], send_ref, pair, 0)
    sums_ref[...] = jnp.zeros((16, MODEL), F32)
    sums_ref[0:1, :] = column_sum(grad_norm * hat)
    sums_ref[1:2, :] = column_sum(grad_norm)
    sums_ref[2:3, :] = column_sum(scaled)
    sums_ref[3:4, :] = column_sum(total * branch_ref[...])
    low_ref[BOTH:TALL, :] = sums_ref[...].astype(BF)


def out_back_call(grad, part_own, part_recv, middle, branch, small, weights):
    return pl.pallas_call(
        out_back_kernel,
        grid=(1,),
        in_specs=[whole((BOTH, MODEL))] * 5
        + [whole((8, MODEL)), pl.BlockSpec((WIDE, 16, MODEL), lambda i: (0, 8, 0))],
        out_specs=[whole((BOTH, MODEL)), whole((WIDE, 16, 128)), whole((TALL, MODEL))],
        out_shape=[
            jax.ShapeDtypeStruct((BOTH, MODEL), F32),
            jax.ShapeDtypeStruct((WIDE, 16, 128), BF),
            jax.ShapeDtypeStruct((TALL, MODEL), BF),
        ],
        scratch_shapes=[pltpu.VMEM((16, MODEL), F32)],
        compiler_params=params(),
        cost_estimate=cost(4),
    )(grad, part_own, part_recv, middle, branch, small[0], weights)


def store_out_grads(place_ref, refs, grad_ref, rows):
    grad = tn(both_cores(*refs[0:2]), both_cores(*refs[2:4])).reshape(WIDE, 16, MODEL)
    store_mine(place_ref, grad, grad_ref, EVERY, rows, EVERY)


def out_weight_kernel(place_ref, *refs):
    store_out_grads(place_ref, refs, refs[-1], EVERY)


def out_weight_last_kernel(place_ref, *refs):
    *sums_refs, before_ref, _, grad_ref = refs[4:]
    store_out_grads(place_ref, refs, grad_ref, slice(0, 16))
    parts = [
        own[0:4, :].astype(F32) + other[0:4, :].astype(F32)
        for own, other in zip(sums_refs[0::2], sums_refs[1::2])
    ]
    rows = jnp.concatenate(parts + [before_ref[0:12, :].astype(F32)], axis=0).astype(BF)
    grad_ref[:, 16:48, :] = jnp.broadcast_to(rows[None], (CHIPS, 32, MODEL))


OUT_WEIGHT_SPECS = (
    [SCALARS]
    + twice(pl.BlockSpec((BOTH, HALF_W), lambda i: (0, 8)))
    + twice(pl.BlockSpec((BOTH, MODEL), lambda i: (0, 0)))
)
SUMS_SPEC = pl.BlockSpec((16, MODEL), lambda i: (8, 0))


def out_weight_call(place, kept, low):
    return pl.pallas_call(
        out_weight_kernel,
        grid=(1,),
        in_specs=OUT_WEIGHT_SPECS,
        out_specs=pl.BlockSpec((CHIPS, 16, MODEL), lambda i: (0, 8, 0)),
        out_shape=jax.ShapeDtypeStruct((CHIPS, PACK_ROWS, MODEL), BF),
        compiler_params=params(),
        cost_estimate=cost(2),
    )(place, *kept, *low)


def out_weight_last_call(place, kept, low, sums, before, pack):
    flat = [array for pair in sums for array in pair]
    return pl.pallas_call(
        out_weight_last_kernel,
        grid=(1,),
        in_specs=OUT_WEIGHT_SPECS + [SUMS_SPEC] * len(flat) + [whole((16, MODEL)), ANYWHERE],
        out_specs=pl.BlockSpec((CHIPS, 48, MODEL), lambda i: (0, 4, 0)),
        out_shape=jax.ShapeDtypeStruct((CHIPS, PACK_ROWS, MODEL), BF),
        input_output_aliases={6 + len(flat): 0},
        compiler_params=params(),
        cost_estimate=cost(3),
    )(place, *kept, *low, *flat, before, pack)


def qkv_back_kernel(recv_ref, rows_ref, vec_ref, weight_ref, part_ref, grads_ref, sums_ref):
    grad_q = unpack_heads(recv_ref, BOTH).astype(BF)
    mask = low_lanes((BOTH, 128))
    key_columns, value_columns = [], []
    for pair in range(HEADS_DEV // 2):
        sums = []
        for head in (2 * pair, 2 * pair + 1):
            total = recv_ref[head * QUARTERS, 0:BOTH, :].astype(F32)
            for quarter in range(1, QUARTERS):
                total = total + recv_ref[head * QUARTERS + quarter, 0:BOTH, :].astype(F32)
            sums.append(total)
        key_columns.append(jnp.where(mask, sums[0], turn(sums[1])))
        value_columns.append(jnp.where(mask, turn(sums[0]), sums[1]))
    grad_k = jnp.concatenate(key_columns, axis=1).astype(BF)
    grad_v = jnp.concatenate(value_columns, axis=1).astype(BF)
    grads_ref[0:BOTH, 0:HALF_W] = grad_q
    grads_ref[0:BOTH, HALF_W:MODEL] = grad_k
    grads_ref[0:BOTH, MODEL : MODEL + HALF_W] = grad_v
    result = (
        nt(grad_q, qkv_weight(weight_ref, 0))
        + nt(grad_k, qkv_weight(weight_ref, 1))
        + nt(grad_v, qkv_weight(weight_ref, 2))
    )
    part_ref[...] = result.astype(BF)
    hat, _ = norm_parts(rows_ref[...].astype(F32))
    sums_ref[...] = jnp.zeros((16, MODEL), F32)
    sums_ref[0:1, :] = column_sum(result * hat)
    sums_ref[1:2, :] = column_sum(result)
    sums_ref[2:3, 0:HALF_W] = column_sum(grad_q.astype(F32))
    sums_ref[2:3, HALF_W:MODEL] = column_sum(grad_v.astype(F32))
    grads_ref[BOTH:TALL, 0:MODEL] = sums_ref[...].astype(BF)
    grads_ref[BOTH:TALL, MODEL : MODEL + HALF_W] = jnp.zeros((16, HALF_W), BF)


def qkv_back_call(recv, rows, small, weight, block_at):
    return pl.pallas_call(
        qkv_back_kernel,
        grid=(1,),
        in_specs=[
            whole((WIDE, SEND_ROWS, 128)),
            whole((BOTH, MODEL)),
            whole((8, MODEL)),
            qkv_block(block_at),
        ],
        out_specs=[whole((BOTH, MODEL)), whole((TALL, 3 * HALF_W))],
        out_shape=[
            jax.ShapeDtypeStruct((BOTH, MODEL), BF),
            jax.ShapeDtypeStruct((TALL, 3 * HALF_W), BF),
        ],
        scratch_shapes=[pltpu.VMEM((16, MODEL), F32)],
        compiler_params=params(),
        cost_estimate=cost(5),
    )(recv, rows, small[0], weight)


def store_qkv_grads(place_ref, refs, grad_ref):
    rows = both_cores(*refs[0:2])

    def part(which):
        columns = slice(which * HALF_W, which * HALF_W + HALF_W)
        grads = jnp.concatenate([ref[0:BOTH, columns] for ref in refs[2:4]], axis=0)
        return tn(rows, grads).reshape(WIDE, 32, HALF_W)

    low, high = slice(0, HALF_W), slice(HALF_W, MODEL)
    store_mine(place_ref, part(0), grad_ref, EVERY, slice(0, 32), low)
    store_mine(place_ref, part(1), grad_ref, EVERY, slice(0, 32), high)
    values = part(2)
    store_mine(place_ref, values[:, 0:16], grad_ref, EVERY, slice(32, 48), low)
    store_mine(place_ref, values[:, 16:32], grad_ref, EVERY, slice(32, 48), high)


def qkv_weight_kernel(place_ref, *refs):
    store_qkv_grads(place_ref, refs, refs[-1])


def qkv_weight_last_kernel(place_ref, *refs):
    grad_ref = refs[-1]
    store_qkv_grads(place_ref, refs, grad_ref)
    rows = sum(ref[BOTH : BOTH + 8, 0:MODEL].astype(F32) for ref in refs[2:4]).astype(BF)
    grad_ref[:, 48:56, :] = jnp.broadcast_to(rows[None], (CHIPS, 8, MODEL))


QKV_WEIGHT_SPECS = (
    [SCALARS]
    + twice(pl.BlockSpec((BOTH, MODEL), lambda i: (0, 3)))
    + twice(whole((TALL, 3 * HALF_W)))
)


def qkv_weight_call(place, kept, grads, pack):
    return pl.pallas_call(
        qkv_weight_kernel,
        grid=(1,),
        in_specs=QKV_WEIGHT_SPECS + [ANYWHERE],
        out_specs=qkv_chips(3),
        out_shape=jax.ShapeDtypeStruct((CHIPS, PACK_ROWS, MODEL), BF),
        input_output_aliases={5: 0},
        compiler_params=params(),
        cost_estimate=cost(4),
    )(place, *kept, *grads, pack)


def qkv_chips(index):
    return pl.BlockSpec((CHIPS, 48, MODEL), lambda i: (0, index, 0))


def qkv_weight_last_call(place, kept, grads):
    return pl.pallas_call(
        qkv_weight_last_kernel,
        grid=(1,),
        in_specs=QKV_WEIGHT_SPECS,
        out_specs=whole((CHIPS, 56, MODEL)),
        out_shape=jax.ShapeDtypeStruct((CHIPS, 56, MODEL), BF),
        compiler_params=params(),
        cost_estimate=cost(4),
    )(place, *kept, *grads)


def with_core(block):
    return block, lax.ppermute(block, "wide", [(i, i ^ 1) for i in range(WIDE)])


def all_to_all(block):
    return lax.all_to_all(block, "wide", 0, 0, tiled=True)


def layer_forward(place, inputs, ids, qkv, rest, small):
    flags, key_ids, query_ids = ids
    sent, rows, normed_a = qkv_call(inputs, small, *qkv)
    recv = all_to_all(sent)
    mix_sent, mix_keep, lse = attend_call(flags, recv, key_ids, query_ids)
    mix_recv = lax.all_to_all(
        mix_sent.reshape(2 * WIDE, 16, 128), ("tensor", "wide"), 0, 0, tiled=True
    )
    branch, middle, pre, wide_kept, mlp = mlp_call(place, rows, normed_a, mix_recv, small, rest)
    mlp_recv = swap(mlp, "tensor")
    return dict(
        rows=rows, recv=recv, keep=mix_keep, lse=lse, branch=branch, middle=middle, pre=pre,
        mlp=mlp, mlp_recv=mlp_recv, for_weights=with_core(wide_kept),
    )


def layer_backward(inputs, kept, ids, qkv, rest, small):
    flags, key_ids, query_ids = ids
    grad, mlp_back, part, *input_grad = mlp_back_call(
        inputs, small, kept["mlp"], kept["mlp_recv"], kept["pre"], rest
    )
    middle_grad, mix_grad, low_a = out_back_call(
        grad, part, swap(part, "tensor"), kept["middle"], kept["branch"], small, rest
    )
    back = attend_back_call(
        flags, kept["recv"], all_to_all(mix_grad), kept["keep"], kept["lse"], key_ids, query_ids
    )
    qkv_part, qkv_grads = qkv_back_call(all_to_all(back), kept["rows"], small, *qkv)
    carried = (middle_grad, qkv_part, swap(qkv_part, "tensor"), kept["rows"])
    for_weights = with_core(mlp_back), with_core(low_a), with_core(qkv_grads)
    return carried, for_weights, input_grad


def body(
    x_in, out_cot, image_ids, w_qkv, w_out, w_fc1, w_fc2, gains, shifts, layer_scales, qv_bias, fc1_bias
):
    section = lax.axis_index("section")
    tensor = lax.axis_index("tensor")
    wide = lax.axis_index("wide")
    is_first = section == 0

    def one(array):
        return lax.dynamic_index_in_dim(array, section, 0, keepdims=False)

    place = jnp.stack([tensor, lax.rem(wide, 2)]).astype(jnp.int32)

    qkv = w_qkv[0]
    small_rows = jnp.concatenate(
        [
            jnp.pad(jnp.concatenate([gains[0], shifts[0], layer_scales[0]], axis=0), ((0, 0), (0, 32))),
            jnp.pad(qv_bias[0], ((0, 0), (0, 48))),
            fc1_bias,
        ],
        axis=0,
    )
    pack_a = jnp.concatenate(
        [
            jnp.concatenate([qkv[:, 0], qkv[:, 1]], axis=1),
            jnp.concatenate([qkv[0:16, 2], qkv[16:32, 2]], axis=1),
            jnp.pad(small_rows, ((0, 5), (0, MODEL - 64))),
        ],
        axis=0,
    )
    own_rows, own_cot = one(x_in), one(out_cot)
    partner = swap(jnp.concatenate([own_rows, own_cot, w_out[0]], axis=0), "tensor")
    other_rows, other_cot, other_out = partner[:ROWS], partner[ROWS:BOTH], partner[BOTH:]
    pack_b = jnp.concatenate(
        [w_fc2[0], w_fc1[0][:, :MODEL], w_fc1[0][:, MODEL:], w_out[0], other_out], axis=0
    )
    other_a = swap(pack_a, "section")
    other_b = swap(pack_b, "section")

    def gather(block):
        return lax.all_gather(block, "wide", axis=0, tiled=False)

    def joined_a(first, second):
        vectors = jnp.concatenate([first[48:64, :HALF_W], second[48:64, :HALF_W]], axis=1)
        return jnp.concatenate([first[:48], second[:48], vectors], axis=0)

    attn_both = gather(jnp.where(is_first, joined_a(pack_a, other_a), joined_a(other_a, pack_a)))

    rest_first = gather(
        jnp.concatenate([jnp.where(is_first, pack_b, other_b), attn_both[0, 96:112]], axis=0)
    )

    def rest_second(rows):
        return gather(jnp.concatenate([jnp.where(is_first, other_b, pack_b), rows], axis=0))

    def small_of(layer):
        block = attn_both[:, 96:107, layer * HALF_W : layer * HALF_W + 64].astype(F32)
        vec = jnp.transpose(block[:, 0:8, 0:32], (1, 0, 2)).reshape(8, MODEL)
        bias = jnp.transpose(block[:, 8:10, 0:16], (1, 0, 2)).reshape(2, HALF_W)
        return vec, bias, block[:, 10].reshape(1, HIDDEN)

    small = (small_of(0), small_of(1))

    id_grid = one(image_ids).reshape(2, WIDE, ROWS)
    sorted_ids = jnp.where(tensor == 0, id_grid, id_grid[::-1])
    key_ids = sorted_ids.reshape(CHUNKS, 1, 512)
    quarter = lax.rem(wide, QUARTERS)
    half_ids = lax.dynamic_index_in_dim(sorted_ids, quarter // 2, 0, keepdims=False)
    quarter_ids = lax.dynamic_slice_in_dim(half_ids, lax.rem(quarter, 2) * 32, 32, 1)
    query_ids = jnp.transpose(quarter_ids.reshape(BLOCKS_Q, 8, 2, 16), (0, 2, 1, 3)).reshape(
        BLOCKS_Q, 256, 1
    )
    key_low, key_high = jnp.min(key_ids[:, 0], axis=1), jnp.max(key_ids[:, 0], axis=1)
    query_low, query_high = jnp.min(query_ids[..., 0], axis=1), jnp.max(query_ids[..., 0], axis=1)
    flags = (
        (query_low[:, None] <= key_high[None]) & (query_high[:, None] >= key_low[None])
    ).astype(jnp.int32)
    ids = (flags, key_ids, query_ids)

    qkv_parts = ((attn_both, 0), (attn_both, 1))
    kept0 = layer_forward(place, (own_rows, other_rows), ids, qkv_parts[0], rest_first, small[0])
    rest = (rest_first, rest_second(kept0["mlp"][:16]))
    kept1 = layer_forward(
        place,
        (kept0["middle"], kept0["mlp"], kept0["mlp_recv"], small[0][0]),
        ids, qkv_parts[1], rest[1], small[1],
    )
    branch1 = kept1["mlp"][:ROWS].astype(F32) + kept1["mlp_recv"][ROWS:].astype(F32)
    out1 = (
        kept1["middle"][:ROWS]
        + small[1][0][SCALE_M] * (branch1 + small[1][0][SHIFT_M])
    ).astype(BF)
    out0 = kept1["rows"][:ROWS]

    same_core = [list(range(core, WIDE, 2)) for core in range(2)]

    def over_chips(pack):
        return lax.psum_scatter(
            pack.reshape(CHIPS * pack.shape[1], MODEL),
            "wide", scatter_dimension=0, axis_index_groups=same_core, tiled=True,
        )

    carried1, back1, _ = layer_backward(
        (own_cot, other_cot), kept1, ids, qkv_parts[1], rest[1], small[1]
    )
    kept_pair0, kept_pair1 = kept0["for_weights"], kept1["for_weights"]
    mlp_back1, low1, grads1 = back1
    sum_mlp1 = over_chips(mlp_weight_call(place, kept_pair1, mlp_back1, low1[0]))
    pack = out_weight_call(place, kept_pair1, low1)
    pack = qkv_weight_call(place, kept_pair1, grads1, pack)

    carried0, back0, (grad_x1,) = layer_backward(
        carried1 + (small[1][0],), kept0, ids, qkv_parts[0], rest[0], small[0]
    )
    mlp_back0, low0, grads0 = back0
    pack = mlp_weight_call(place, kept_pair0, mlp_back0, None, pack)
    pack = out_weight_last_call(
        place, kept_pair0, low0, (mlp_back1, low1, grads1, mlp_back0, low0), sum_mlp1, pack
    )
    sum_mid = over_chips(pack)
    last_recv = lax.all_to_all(
        qkv_weight_last_call(place, kept_pair0, grads0),
        "wide", 0, 0, axis_index_groups=same_core, tiled=True,
    )
    sum_last = jnp.sum(last_recv.astype(F32), axis=0)

    middle_grad0, part0, part_recv0, _ = carried0
    hat0, rstd0 = norm_parts(own_rows.astype(F32))
    grad_norm0 = part0[:ROWS].astype(F32) + part_recv0[ROWS:].astype(F32)
    grad_x0 = middle_grad0[:ROWS] + norm_back(grad_norm0, hat0, rstd0, small[0][0][GAIN_A])

    def lanes(rows, width):
        return lax.dynamic_slice_in_dim(rows, wide * width, width, rows.ndim - 1)

    def own_sums(mlp, outs, qkv_rows):
        norms = jnp.concatenate([mlp[0:2], outs, qkv_rows[0:2]], axis=0)
        pair = qkv_rows[2].reshape(2, HALF_W)
        return jnp.concatenate(
            [lanes(norms, 32).reshape(-1), lanes(pair, 16).reshape(-1), lanes(mlp[2:4].reshape(-1), 64)]
        )

    sums = sum_mid[208:228]
    mlp1, outs1, qkv1, mlp0, outs0 = (sums[at : at + 4] for at in range(0, 20, 4))
    mid0 = jnp.concatenate([sum_mid[0:128], sum_mid[192:208]], axis=0)
    mid1 = jnp.concatenate([sum_mlp1, sum_mid[128:144]], axis=0)
    mid_total = jnp.where(is_first, mid0, mid1).astype(F32) + swap(
        jnp.where(is_first, mid1, mid0), "section"
    ).astype(F32)

    def with_sums(rows, vector):
        return jnp.concatenate([rows, jnp.pad(vector, (0, 672)).reshape(1, MODEL)], axis=0)

    late0 = with_sums(sum_last[0:48].astype(BF), own_sums(mlp0, outs0, sum_last[48:52].astype(BF)))
    late1 = with_sums(sum_mid[144:192], own_sums(mlp1, outs1, qkv1))
    late_own = jnp.where(is_first, late0, late1)
    late_away = jnp.where(is_first, late1, late0)
    late_total = late_own.astype(F32) + swap(late_away, "section").astype(F32)
    own_part, away_part = late_own[48, 192:256], late_away[48, 192:256]
    across = lax.ppermute(away_part, ("section", "tensor"), [(0, 3), (3, 0), (1, 2), (2, 1)])
    heads_total = late_total[48, 192:256] + (
        swap(own_part, "tensor").astype(F32) + across.astype(F32)
    )
    mlp_total, out_total = mid_total[0:128], mid_total[128:144]
    qkv_total, tiny = late_total[0:48], late_total[48]
    norms = jnp.concatenate([tiny[0:192], heads_total]).reshape(8, 32)
    g_gains = jnp.stack([norms[6], norms[2]])
    g_shifts = jnp.stack([norms[7], norms[4], norms[3], norms[0]])
    g_scales = jnp.stack([norms[5], norms[1]])
    g_qv = tiny[256:288].reshape(2, 16)
    g_fc1_bias = tiny[288:352]
    g_fc2 = mlp_total[0:64]
    g_fc1 = jnp.concatenate([mlp_total[64:96], mlp_total[96:128]], axis=1)
    pairs = qkv_total[0:32]
    value_grad = jnp.concatenate([qkv_total[32:48, :HALF_W], qkv_total[32:48, HALF_W:]], axis=0)
    g_qkv = jnp.stack([pairs[:, :HALF_W], pairs[:, HALF_W:], value_grad], axis=1)

    def by_micro(first, second):
        own = jnp.where(is_first, first, second)
        came = swap(jnp.where(is_first, second, first), "section")
        return jnp.stack([jnp.where(is_first, own, came), jnp.where(is_first, came, own)])

    return (
        by_micro(out0, out1)[None],
        by_micro(grad_x0, grad_x1)[None],
        g_qkv[None],
        out_total[None],
        g_fc1[None],
        g_fc2[None],
        g_gains[None],
        g_shifts[None],
        g_scales[None],
        g_qv[None],
        g_fc1_bias[None],
    )


def solution(mesh):
    in_specs = (
        P(None, ("tensor", "wide"), None),
        P(None, ("tensor", "wide"), None),
        P(),
        P("section", "wide", None, "tensor"),
        P("section", ("tensor", "wide"), None),
        P("section", "wide", "tensor"),
        P("section", ("tensor", "wide"), None),
        P("section", None, "wide"),
        P("section", None, "wide"),
        P("section", None, "wide"),
        P("section", None, ("tensor", "wide")),
        P("section", ("tensor", "wide")),
    )
    out_specs = (
        P("section", None, ("tensor", "wide"), None),
        P("section", None, ("tensor", "wide"), None),
        P("section", "wide", None, "tensor"),
        P("section", ("tensor", "wide"), None),
        P("section", "wide", "tensor"),
        P("section", ("tensor", "wide"), None),
        P("section", None, "wide"),
        P("section", None, "wide"),
        P("section", None, "wide"),
        P("section", None, ("tensor", "wide")),
        P("section", ("tensor", "wide")),
    )
    return jax.shard_map(body, mesh=mesh, in_specs=in_specs, out_specs=out_specs, check_vma=False)
```

```python
import jax
import jax.numpy as jnp
from jax import lax
from jax.experimental import pallas as pl
from jax.experimental.pallas import tpu as pltpu
from jax.sharding import PartitionSpec as P

HEAD = 64
EPS = 1e-06
NEG_FILL = -1e30
ROOT_HALF = 0.7071067811865476
INV_ROOT_TAU = 0.3989422804014327
SCALE = HEAD ** (-0.5)
BF = jnp.bfloat16
F32 = jnp.float32
MIB = 1024 * 1024

ROWS = 64
BOTH = 128
WIDE = 32
HEADS_DEV = 8
QUARTERS = 4
HALF_W = 512
MODEL = 1024
HIDDEN = 2048
SEND_ROWS = 144
BLOCKS_Q = 4
CHUNKS = 8


def params(limit=56):
    return pltpu.CompilerParams(vmem_limit_bytes=limit * MIB)


def cost(micros):
    return pl.CostEstimate(flops=int(micros * 1e9), bytes_accessed=100000, transcendentals=0)


def whole(shape):
    count = len(shape)
    return pl.BlockSpec(shape, lambda *g: (0,) * count)


ANYWHERE = pl.BlockSpec(memory_space=pl.ANY)
SCALARS = pl.BlockSpec(memory_space=pltpu.SMEM)
EVERY = slice(None)


def swap(block, axis):
    return lax.ppermute(block, axis, [(0, 1), (1, 0)])


def nt(left, right):
    return lax.dot_general(left, right, (((1,), (1,)), ((), ())), preferred_element_type=F32)


def tn(left, right):
    return lax.dot_general(left, right, (((0,), (0,)), ((), ())), preferred_element_type=F32)


def nn(left, right):
    return jnp.dot(left, right, preferred_element_type=F32)


def low_lanes(shape):
    return lax.broadcasted_iota(jnp.int32, shape, len(shape) - 1) < HEAD


def turn(tile):
    return pltpu.roll(tile, HEAD, 1)


def pack_heads(tile, out_ref, pair, row0):
    rolled = turn(tile)
    for quarter in range(QUARTERS):
        first = slice(quarter * 32, quarter * 32 + 16)
        second = slice(quarter * 32 + 16, quarter * 32 + 32)
        mask = low_lanes((16, 128))
        even = jnp.where(mask, tile[first], rolled[second])
        odd = jnp.where(mask, rolled[first], tile[second])
        out_ref[(2 * pair) * QUARTERS + quarter, row0 : row0 + 16, :] = even.astype(BF)
        out_ref[(2 * pair + 1) * QUARTERS + quarter, row0 : row0 + 16, :] = odd.astype(BF)


def unpack_heads(in_ref, row0, base=0):
    mask = low_lanes((16, 128))
    columns = []
    for pair in range(HEADS_DEV // 2):
        pieces = []
        for quarter in range(QUARTERS):
            even = in_ref[base + (2 * pair) * QUARTERS + quarter, row0 : row0 + 16, :].astype(F32)
            odd = in_ref[base + (2 * pair + 1) * QUARTERS + quarter, row0 : row0 + 16, :].astype(F32)
            pieces.append(jnp.where(mask, even, turn(odd)))
            pieces.append(jnp.where(mask, turn(even), odd))
        columns.append(jnp.concatenate(pieces, axis=0))
    return jnp.concatenate(columns, axis=1)


def norm_parts(rows_in):
    centre = jnp.mean(rows_in, axis=-1, keepdims=True)
    centred = rows_in - centre
    spread = jnp.mean(centred * centred, axis=-1, keepdims=True)
    rstd_rows = lax.rsqrt(spread + EPS)
    return centred * rstd_rows, rstd_rows


def norm_back(grad_rows, normal_rows, rstd_rows, gain_row):
    scaled = grad_rows * gain_row
    first_mean = jnp.mean(scaled, axis=-1, keepdims=True)
    second_mean = jnp.mean(scaled * normal_rows, axis=-1, keepdims=True)
    return rstd_rows * (scaled - first_mean - normal_rows * second_mean)


def joined(own_ref, recv_ref):
    recv = jnp.concatenate([recv_ref[ROWS:], recv_ref[:ROWS]], axis=0)
    return own_ref[...].astype(F32) + recv.astype(F32)


def column_sum(rows):
    return jnp.sum(rows[:ROWS], axis=0, keepdims=True) + jnp.sum(rows[ROWS:], axis=0, keepdims=True)


GAIN_A, GAIN_C, SHIFT_A, SHIFT_O, SHIFT_C, SHIFT_M, SCALE_A, SCALE_M = range(8)


def row_of(ref, at):
    return ref[at : at + 1, :]


def qkv_weight(ref, which):
    if which < 2:
        return ref[:, 0:32, which * HALF_W : which * HALF_W + HALF_W].reshape(MODEL, HALF_W)
    parts = [ref[:, 32:48, 0:HALF_W], ref[:, 32:48, HALF_W:MODEL]]
    return jnp.concatenate(parts, axis=1).reshape(MODEL, HALF_W)


def project_and_pack(rows, vec_ref, bias_ref, weight_ref, out_ref, rows_ref, normed_ref):
    rows_ref[...] = rows
    hat, _ = norm_parts(rows.astype(F32))
    normed = (hat * row_of(vec_ref, GAIN_A) + row_of(vec_ref, SHIFT_A)).astype(BF)
    normed_ref[...] = normed
    queries = nn(normed, qkv_weight(weight_ref, 0)) + bias_ref[0:1, :]
    keys = nn(normed, qkv_weight(weight_ref, 1))
    values = nn(normed, qkv_weight(weight_ref, 2)) + bias_ref[1:2, :]
    mask = low_lanes((BOTH, 128))
    for pair in range(HEADS_DEV // 2):
        columns = slice(pair * 128, pair * 128 + 128)
        key_tile, value_tile, query_tile = keys[:, columns], values[:, columns], queries[:, columns]
        even = jnp.where(mask, key_tile, turn(value_tile)).astype(BF)
        odd = jnp.where(mask, turn(key_tile), value_tile).astype(BF)
        for quarter in range(QUARTERS):
            out_ref[(2 * pair) * QUARTERS + quarter, 0:BOTH, :] = even
            out_ref[(2 * pair + 1) * QUARTERS + quarter, 0:BOTH, :] = odd
        pack_heads(query_tile, out_ref, pair, BOTH)


def qkv_first_kernel(own_ref, other_ref, vec_ref, bias_ref, weight_ref, out_ref, rows_ref, normed_ref):
    rows = jnp.concatenate([own_ref[...], other_ref[...]], axis=0)
    project_and_pack(rows, vec_ref, bias_ref, weight_ref, out_ref, rows_ref, normed_ref)


def qkv_next_kernel(
    middle_ref, mlp_own_ref, mlp_recv_ref, before_ref, vec_ref, bias_ref, weight_ref,
    out_ref, rows_ref, normed_ref,
):
    branch = joined(mlp_own_ref, mlp_recv_ref) + row_of(before_ref, SHIFT_M)
    rows = (middle_ref[...] + row_of(before_ref, SCALE_M) * branch).astype(BF)
    project_and_pack(rows, vec_ref, bias_ref, weight_ref, out_ref, rows_ref, normed_ref)


def qkv_block(index):
    return pl.BlockSpec((WIDE, 48, MODEL), lambda i: (0, index, 0))


def qkv_call(inputs, small, weight, block_at):
    vec, bias, _ = small
    first = len(inputs) == 2
    return pl.pallas_call(
        qkv_first_kernel if first else qkv_next_kernel,
        grid=(1,),
        in_specs=[whole(part.shape) for part in inputs]
        + [whole((8, MODEL)), whole((2, HALF_W)), qkv_block(block_at)],
        out_specs=[whole((WIDE, SEND_ROWS, 128)), whole((BOTH, MODEL)), whole((BOTH, MODEL))],
        out_shape=[
            jax.ShapeDtypeStruct((WIDE, SEND_ROWS, 128), BF),
            jax.ShapeDtypeStruct((BOTH, MODEL), BF),
            jax.ShapeDtypeStruct((BOTH, MODEL), BF),
        ],
        compiler_params=params(),
        cost_estimate=cost(5),
    )(*inputs, vec, bias, weight)


def query_tiles(packed):
    mask = low_lanes((128, 128))
    return jnp.concatenate(
        [jnp.where(mask, packed, 0.0), jnp.where(mask, turn(packed), 0.0)], axis=0
    )


def key_chunk(recv_ref, chunk):
    half, group = chunk // 4, chunk % 4
    block = recv_ref[group * 8 : group * 8 + 8, half * ROWS : half * ROWS + ROWS, :]
    return block.reshape(512, 128)


def lane_tiles(fn, block):
    return fn(fn(block[:, 0:128], block[:, 128:256]), fn(block[:, 256:384], block[:, 384:512]))


def attend_kernel(
    flag_ref, recv_ref, key_id_ref, query_id_ref, out_ref, keep_ref, lse_ref,
    score_ref, top_ref, total_ref, acc_ref,
):
    at = pl.program_id(0)
    packed = recv_ref[pl.ds(at * 8, 8), BOTH : BOTH + 16, :].astype(F32).reshape(128, 128)
    queries = (query_tiles(packed) * SCALE).astype(BF)
    query_ids = query_id_ref[0]
    top_ref[...] = jnp.full((256, 128), NEG_FILL, F32)
    total_ref[...] = jnp.zeros((256, 128), F32)
    acc_ref[...] = jnp.zeros((256, 128), F32)
    for chunk in range(CHUNKS):

        @pl.when(flag_ref[at, chunk] != 0)
        def _():
            scores = nt(queries, key_chunk(recv_ref, chunk))
            scores = jnp.where(query_ids == key_id_ref[chunk], scores, NEG_FILL)
            score_ref[chunk] = scores
            top_ref[...] = jnp.maximum(top_ref[...], lane_tiles(jnp.maximum, scores))

    top = jnp.max(top_ref[...], axis=1, keepdims=True)
    for chunk in range(CHUNKS):

        @pl.when(flag_ref[at, chunk] != 0)
        def _():
            expo = jnp.exp(score_ref[chunk] - top)
            total_ref[...] += lane_tiles(jnp.add, expo)
            acc_ref[...] += nn(expo.astype(BF), key_chunk(recv_ref, chunk))

    total = jnp.sum(total_ref[...], axis=1, keepdims=True)
    mixture = acc_ref[...] / total
    lse_ref[...] = top + jnp.log(total)
    mask = low_lanes((128, 128))
    joined = jnp.where(mask, turn(mixture[:128]), mixture[128:]).reshape(8, 16, 128)
    keep_ref[...] = joined
    out_ref[0] = joined.astype(BF)
    out_ref[1] = joined.astype(BF)


def attend_call(flags, recv, key_ids, query_ids):
    return pl.pallas_call(
        attend_kernel,
        grid_spec=pltpu.PrefetchScalarGridSpec(
            num_scalar_prefetch=1,
            grid=(BLOCKS_Q,),
            in_specs=[
                pl.BlockSpec((WIDE, SEND_ROWS, 128), lambda i, f: (0, 0, 0)),
                pl.BlockSpec((CHUNKS, 1, 512), lambda i, f: (0, 0, 0)),
                pl.BlockSpec((1, 256, 1), lambda i, f: (i, 0, 0)),
            ],
            out_specs=[
                pl.BlockSpec((2, 8, 16, 128), lambda i, f: (0, i, 0, 0)),
                pl.BlockSpec((8, 16, 128), lambda i, f: (i, 0, 0)),
                pl.BlockSpec((256, 1), lambda i, f: (i, 0)),
            ],
            scratch_shapes=[
                pltpu.VMEM((CHUNKS, 256, 512), F32),
                pltpu.VMEM((256, 128), F32),
                pltpu.VMEM((256, 128), F32),
                pltpu.VMEM((256, 128), F32),
            ],
        ),
        out_shape=[
            jax.ShapeDtypeStruct((2, WIDE, 16, 128), BF),
            jax.ShapeDtypeStruct((WIDE, 16, 128), F32),
            jax.ShapeDtypeStruct((1024, 1), F32),
        ],
        compiler_params=params(),
        cost_estimate=cost(12),
    )(flags, recv, key_ids, query_ids)


def attend_back_kernel(
    flag_ref, recv_ref, grad_ref, keep_ref, lse_ref, key_id_ref, query_id_ref, out_ref,
    key_grad_ref, query_grad_ref,
):
    at = pl.program_id(0)

    @pl.when(at == 0)
    def _():
        key_grad_ref[...] = jnp.zeros((WIDE, BOTH, 128), F32)

    mask = low_lanes((128, 128))
    packed = recv_ref[pl.ds(at * 8, 8), BOTH : BOTH + 16, :].astype(F32).reshape(128, 128)
    queries = (query_tiles(packed) * SCALE).astype(BF)
    grads = grad_ref[...].astype(F32).reshape(128, 128)
    grad_tile = jnp.concatenate(
        [jnp.where(mask, 0.0, turn(grads)), jnp.where(mask, 0.0, grads)], axis=0
    ).astype(BF)
    product = grads * keep_ref[...].reshape(128, 128)
    delta = jnp.concatenate(
        [
            jnp.sum(jnp.where(mask, product, 0.0), axis=1, keepdims=True),
            jnp.sum(jnp.where(mask, 0.0, product), axis=1, keepdims=True),
        ],
        axis=0,
    )
    lse = lse_ref[...]
    query_ids = query_id_ref[0]
    both = jnp.concatenate([queries, grad_tile], axis=0)
    query_grad_ref[...] = jnp.zeros((256, 128), F32)
    for chunk in range(CHUNKS):

        @pl.when(flag_ref[at, chunk] != 0)
        def _():
            half, group = chunk // 4, chunk % 4
            keys = key_chunk(recv_ref, chunk)
            scores = nt(queries, keys)
            scores = jnp.where(query_ids == key_id_ref[chunk], scores, NEG_FILL)
            chance = jnp.exp(scores - lse)
            grad_scores = (chance * (nt(grad_tile, keys) - delta)).astype(BF)
            query_grad_ref[...] += nn(grad_scores, keys)
            stacked = jnp.concatenate([grad_scores, chance.astype(BF)], axis=0)
            key_grad_ref[group * 8 : group * 8 + 8, half * ROWS : half * ROWS + ROWS, :] += tn(
                stacked, both
            ).reshape(8, ROWS, 128)

    query_grad = query_grad_ref[...] * SCALE
    joined = jnp.where(mask, query_grad[:128], turn(query_grad[128:]))
    out_ref[pl.ds(at * 8, 8), BOTH : BOTH + 16, :] = joined.astype(BF).reshape(8, 16, 128)

    @pl.when(at == BLOCKS_Q - 1)
    def _():
        out_ref[:, 0:BOTH, :] = key_grad_ref[...].astype(BF)


def attend_back_call(flags, recv, grads, keep, lse, key_ids, query_ids):
    return pl.pallas_call(
        attend_back_kernel,
        grid_spec=pltpu.PrefetchScalarGridSpec(
            num_scalar_prefetch=1,
            grid=(BLOCKS_Q,),
            in_specs=[
                pl.BlockSpec((WIDE, SEND_ROWS, 128), lambda i, f: (0, 0, 0)),
                pl.BlockSpec((8, 16, 128), lambda i, f: (i, 0, 0)),
                pl.BlockSpec((8, 16, 128), lambda i, f: (i, 0, 0)),
                pl.BlockSpec((256, 1), lambda i, f: (i, 0)),
                pl.BlockSpec((CHUNKS, 1, 512), lambda i, f: (0, 0, 0)),
                pl.BlockSpec((1, 256, 1), lambda i, f: (i, 0, 0)),
            ],
            out_specs=pl.BlockSpec((WIDE, SEND_ROWS, 128), lambda i, f: (0, 0, 0)),
            scratch_shapes=[
                pltpu.VMEM((WIDE, BOTH, 128), F32),
                pltpu.VMEM((256, 128), F32),
            ],
        ),
        out_shape=jax.ShapeDtypeStruct((WIDE, SEND_ROWS, 128), BF),
        compiler_params=params(),
        cost_estimate=cost(16),
    )(flags, recv, grads, keep, lse, key_ids, query_ids)


KEPT_C, KEPT_A, KEPT_MIX = slice(2048, 3072), slice(3072, 4096), slice(4096, 4608)
KEPT_WIDTH = 4608
TALL = BOTH + 16


def mlp_kernel(
    place_ref, rows_ref, normed_ref, recv_ref, vec_ref, bias_ref, out_weight_ref, one_ref, two_ref,
    branch_ref, middle_ref, pre_ref, kept_ref, out_ref, acc_ref,
):
    at = pl.program_id(0)

    @pl.when(at == 0)
    def _():
        tensor = place_ref[0]
        own = unpack_heads(recv_ref, 0, tensor * WIDE).astype(BF)
        partner = unpack_heads(recv_ref, 0, (1 - tensor) * WIDE).astype(BF)
        partner = jnp.concatenate([partner[ROWS:], partner[:ROWS]], axis=0)
        kept_ref[:, KEPT_A] = normed_ref[...]
        kept_ref[:, KEPT_MIX] = own
        proj = nn(own, out_weight_ref[:, 0:16, :].reshape(HALF_W, MODEL)) + nn(
            partner, out_weight_ref[:, 16:32, :].reshape(HALF_W, MODEL)
        )
        branch = proj + row_of(vec_ref, SHIFT_O)
        branch_ref[...] = branch
        middle = rows_ref[...].astype(F32) + row_of(vec_ref, SCALE_A) * branch
        middle_ref[...] = middle
        hat, _ = norm_parts(middle)
        kept_ref[:, KEPT_C] = (hat * row_of(vec_ref, GAIN_C) + row_of(vec_ref, SHIFT_C)).astype(BF)

    pre = nn(kept_ref[:, KEPT_C], one_ref[...].reshape(MODEL, MODEL)) + bias_ref[...]
    act = (0.5 * pre * (1.0 + lax.erf(pre * ROOT_HALF))).astype(BF)
    pre_ref[...] = pre
    part = nn(act, two_ref[...].reshape(MODEL, MODEL))

    @pl.when(at == 0)
    def _():
        kept_ref[:, 0:MODEL] = act
        acc_ref[...] = part

    @pl.when(at == 1)
    def _():
        kept_ref[:, MODEL:HIDDEN] = act
        out_ref[...] = (acc_ref[...] + part).astype(BF)


def mlp_call(place, rows, normed, recv, small, weights):
    vec, _, bias = small
    return pl.pallas_call(
        mlp_kernel,
        grid=(2,),
        in_specs=[
            pl.BlockSpec(memory_space=pltpu.SMEM),
            whole((BOTH, MODEL)),
            whole((BOTH, MODEL)),
            whole((2 * WIDE, 16, 128)),
            whole((8, MODEL)),
            pl.BlockSpec((1, MODEL), lambda j: (0, j)),
            pl.BlockSpec((WIDE, 32, MODEL), lambda j: (0, 4, 0)),
            pl.BlockSpec((WIDE, 32, MODEL), lambda j: (0, 2 + j, 0)),
            pl.BlockSpec((16, 64, MODEL), lambda j: (j, 0, 0)),
        ],
        out_specs=[
            whole((BOTH, MODEL)),
            whole((BOTH, MODEL)),
            pl.BlockSpec((BOTH, MODEL), lambda j: (0, j)),
            whole((BOTH, KEPT_WIDTH)),
            whole((BOTH, MODEL)),
        ],
        out_shape=[
            jax.ShapeDtypeStruct((BOTH, MODEL), F32),
            jax.ShapeDtypeStruct((BOTH, MODEL), F32),
            jax.ShapeDtypeStruct((BOTH, HIDDEN), F32),
            jax.ShapeDtypeStruct((BOTH, KEPT_WIDTH), BF),
            jax.ShapeDtypeStruct((BOTH, MODEL), BF),
        ],
        scratch_shapes=[pltpu.VMEM((BOTH, MODEL), F32)],
        compiler_params=params(),
        cost_estimate=cost(8),
    )(place, rows, normed, recv, vec, bias, weights, weights, weights)


def mlp_back_steps(
    grad, vec_ref, pre_ref, one_ref, two_ref, grad_ref, back_ref, out_ref, acc_ref, sums_ref,
):
    at = pl.program_id(0)

    @pl.when(at == 0)
    def _():
        rows = grad()
        grad_ref[...] = rows
        rows = rows.astype(F32)
        scaled = rows * row_of(vec_ref, SCALE_M)
        back_ref[0:BOTH, 2048:3072] = scaled.astype(BF)
        sums_ref[...] = jnp.zeros((16, MODEL), F32)
        sums_ref[0:1, :] = column_sum(scaled)

    pre = pre_ref[...]
    slope = 0.5 * (1.0 + lax.erf(pre * ROOT_HALF)) + pre * jnp.exp(-0.5 * pre * pre) * INV_ROOT_TAU
    grad_pre = (nt(back_ref[0:BOTH, 2048:3072], two_ref[...].reshape(MODEL, MODEL)) * slope).astype(BF)
    part = nt(grad_pre, one_ref[...].reshape(MODEL, MODEL))
    bias_sum = jnp.sum(grad_pre.astype(F32), axis=0, keepdims=True)

    @pl.when(at == 0)
    def _():
        back_ref[0:BOTH, 0:MODEL] = grad_pre
        acc_ref[...] = part
        sums_ref[1:2, :] = bias_sum

    @pl.when(at == 1)
    def _():
        back_ref[0:BOTH, MODEL:HIDDEN] = grad_pre
        out_ref[...] = (acc_ref[...] + part).astype(BF)
        sums_ref[2:3, :] = bias_sum
        back_ref[BOTH:TALL, 0:MODEL] = sums_ref[...].astype(BF)
        back_ref[BOTH:TALL, MODEL:3072] = jnp.zeros((16, 2048), BF)


def mlp_back_first_kernel(own_ref, other_ref, *refs):
    mlp_back_steps(lambda: jnp.concatenate([own_ref[...], other_ref[...]], axis=0), *refs)


def mlp_back_next_kernel(
    middle_grad_ref, part_own_ref, part_recv_ref, rows_ref, after_ref, pack_ref, *refs
):
    *refs, input_grad_ref, acc_ref, sums_ref = refs

    def grad():
        hat, rstd = norm_parts(rows_ref[...].astype(F32))
        grad_norm = joined(part_own_ref, part_recv_ref)
        total = middle_grad_ref[...] + norm_back(grad_norm, hat, rstd, row_of(after_ref, GAIN_A))
        input_grad_ref[...] = total[:ROWS]
        return total.astype(BF)

    mlp_back_steps(grad, *refs, acc_ref, sums_ref)


def mlp_back_call(inputs, small, pre, weights):
    first = len(inputs) == 2
    extra = [] if first else [(ROWS, MODEL)]
    return pl.pallas_call(
        mlp_back_first_kernel if first else mlp_back_next_kernel,
        grid=(2,),
        in_specs=[ANYWHERE if part.ndim == 3 else whole(part.shape) for part in inputs]
        + [
            whole((8, MODEL)),
            pl.BlockSpec((BOTH, MODEL), lambda j: (0, j)),
            pl.BlockSpec((WIDE, 32, MODEL), lambda j: (0, 2 + j, 0)),
            pl.BlockSpec((16, 64, MODEL), lambda j: (j, 0, 0)),
        ],
        out_specs=[whole((BOTH, MODEL)), whole((TALL, 3072)), whole((BOTH, MODEL))]
        + [whole(shape) for shape in extra],
        out_shape=[
            jax.ShapeDtypeStruct((BOTH, MODEL), BF),
            jax.ShapeDtypeStruct((TALL, 3072), BF),
            jax.ShapeDtypeStruct((BOTH, MODEL), BF),
        ]
        + [jax.ShapeDtypeStruct(shape, F32) for shape in extra],
        scratch_shapes=[pltpu.VMEM((BOTH, MODEL), F32), pltpu.VMEM((16, MODEL), F32)],
        compiler_params=params(),
        cost_estimate=cost(8),
    )(*inputs, small[0], pre, weights, weights)


PACK_ROWS = 240
CHIPS = WIDE // 2


def store_mine(place_ref, value, grad_ref, pairs, rows, columns):
    value = value.reshape(value.shape[0] // 2, 2, *value.shape[1:])
    for core in range(2):

        @pl.when(place_ref[1] == core)
        def _():
            grad_ref[pairs, rows, columns] = value[:, core].astype(BF)


def both_cores(own_ref, other_ref):
    return jnp.concatenate([own_ref[0:BOTH], other_ref[0:BOTH]], axis=0)


def twice(spec):
    return [spec, spec]


def mlp_weight_kernel(place_ref, *refs):
    act, normed, low, grad_pre = (both_cores(*refs[at : at + 2]) for at in range(0, 8, 2))
    grad_ref = refs[-1]
    grad_two = tn(act, low).reshape(16, 64, MODEL)
    grad_one = tn(normed, grad_pre).reshape(WIDE, 32, MODEL)
    for at in range(2):

        @pl.when(pl.program_id(0) == at)
        def _():
            store_mine(
                place_ref, grad_two, grad_ref, slice(8 * at, 8 * at + 8), slice(0, 64), EVERY
            )
            rows = slice(64 + 32 * at, 96 + 32 * at)
            store_mine(place_ref, grad_one, grad_ref, EVERY, rows, EVERY)


def mlp_weight_call(place, kept, back, pack=None):
    rows, extra, aliases = 128, [], {}
    if pack is not None:
        rows, extra, aliases = PACK_ROWS, [pack], {9: 0}
    return pl.pallas_call(
        mlp_weight_kernel,
        grid=(2,),
        in_specs=[SCALARS]
        + twice(pl.BlockSpec((BOTH, MODEL), lambda j: (0, j)))
        + twice(pl.BlockSpec((BOTH, MODEL), lambda j: (0, 2)))
        + twice(pl.BlockSpec((BOTH, MODEL), lambda j: (0, 2)))
        + twice(pl.BlockSpec((BOTH, MODEL), lambda j: (0, j)))
        + [ANYWHERE] * len(extra),
        out_specs=pl.BlockSpec((CHIPS, 128, MODEL), lambda j: (0, 0, 0)),
        out_shape=jax.ShapeDtypeStruct((CHIPS, rows, MODEL), BF),
        input_output_aliases=aliases,
        compiler_params=params(),
        cost_estimate=cost(7),
    )(place, *kept, *kept, *back, *back, *extra)


def out_back_kernel(
    grad_ref, part_own_ref, part_recv_ref, middle_ref, branch_ref, mlp_own_ref, mlp_recv_ref, vec_ref,
    weight_ref, pack_ref, middle_grad_ref, send_ref, low_ref, sums_ref,
):
    hat, rstd = norm_parts(middle_ref[...])
    grad_norm = joined(part_own_ref, part_recv_ref)
    total = grad_ref[...].astype(F32) + norm_back(grad_norm, hat, rstd, row_of(vec_ref, GAIN_C))
    middle_grad_ref[...] = total
    scaled = total * row_of(vec_ref, SCALE_A)
    rows = scaled.astype(BF)
    low_ref[0:BOTH, :] = rows
    grad_mix = nt(rows, weight_ref[...].reshape(HALF_W, MODEL))
    for pair in range(HEADS_DEV // 2):
        pack_heads(grad_mix[:, pair * 128 : pair * 128 + 128], send_ref, pair, 0)
    sums_ref[...] = jnp.zeros((16, MODEL), F32)
    sums_ref[0:1, :] = column_sum(grad_norm * hat)
    sums_ref[1:2, :] = column_sum(grad_norm)
    sums_ref[2:3, :] = column_sum(scaled)
    sums_ref[3:4, :] = column_sum(total * branch_ref[...])
    branch = joined(mlp_own_ref, mlp_recv_ref) + row_of(vec_ref, SHIFT_M)
    sums_ref[4:5, :] = column_sum(grad_ref[...].astype(F32) * branch)
    low_ref[BOTH:TALL, :] = sums_ref[...].astype(BF)


def out_back_call(grad, part_own, part_recv, middle, branch, mlp, mlp_recv, small, weights, pack):
    return pl.pallas_call(
        out_back_kernel,
        grid=(1,),
        in_specs=[whole((BOTH, MODEL))] * 7
        + [whole((8, MODEL)), pl.BlockSpec((WIDE, 16, MODEL), lambda i: (0, 8, 0)), ANYWHERE],
        out_specs=[whole((BOTH, MODEL)), whole((WIDE, 16, 128)), whole((TALL, MODEL))],
        out_shape=[
            jax.ShapeDtypeStruct((BOTH, MODEL), F32),
            jax.ShapeDtypeStruct((WIDE, 16, 128), BF),
            jax.ShapeDtypeStruct((TALL, MODEL), BF),
        ],
        scratch_shapes=[pltpu.VMEM((16, MODEL), F32)],
        compiler_params=params(),
        cost_estimate=cost(4),
    )(grad, part_own, part_recv, middle, branch, mlp, mlp_recv, small[0], weights, pack)


def store_out_grads(place_ref, refs, grad_ref, rows):
    grad = tn(both_cores(*refs[0:2]), both_cores(*refs[2:4])).reshape(WIDE, 16, MODEL)
    store_mine(place_ref, grad, grad_ref, EVERY, rows, EVERY)


def out_weight_kernel(place_ref, *refs):
    store_out_grads(place_ref, refs, refs[-1], EVERY)


def out_weight_last_kernel(place_ref, *refs):
    *sums_refs, before_ref, _, grad_ref = refs[4:]
    store_out_grads(place_ref, refs, grad_ref, slice(0, 16))
    parts = [
        own[0:count, :].astype(F32) + other[0:count, :].astype(F32)
        for own, other, count in zip(sums_refs[0::2], sums_refs[1::2], (8, 8, 4, 4, 4))
    ]
    rows = jnp.concatenate(parts + [before_ref[0:4, :].astype(F32)], axis=0).astype(BF)
    grad_ref[:, 16:48, :] = jnp.broadcast_to(rows[None], (CHIPS, 32, MODEL))


OUT_WEIGHT_SPECS = (
    [SCALARS]
    + twice(pl.BlockSpec((BOTH, HALF_W), lambda i: (0, 8)))
    + twice(pl.BlockSpec((BOTH, MODEL), lambda i: (0, 0)))
)
SUMS_SPEC = pl.BlockSpec((16, MODEL), lambda i: (8, 0))


def out_weight_call(place, kept, low):
    return pl.pallas_call(
        out_weight_kernel,
        grid=(1,),
        in_specs=OUT_WEIGHT_SPECS,
        out_specs=pl.BlockSpec((CHIPS, 16, MODEL), lambda i: (0, 8, 0)),
        out_shape=jax.ShapeDtypeStruct((CHIPS, PACK_ROWS, MODEL), BF),
        compiler_params=params(),
        cost_estimate=cost(2),
    )(place, *kept, *low)


def out_weight_last_call(place, kept, low, sums, before, pack):
    flat = [array for pair in sums for array in pair]
    return pl.pallas_call(
        out_weight_last_kernel,
        grid=(1,),
        in_specs=OUT_WEIGHT_SPECS + [SUMS_SPEC] * len(flat) + [whole((16, MODEL)), ANYWHERE],
        out_specs=pl.BlockSpec((CHIPS, 48, MODEL), lambda i: (0, 4, 0)),
        out_shape=jax.ShapeDtypeStruct((CHIPS, PACK_ROWS, MODEL), BF),
        input_output_aliases={6 + len(flat): 0},
        compiler_params=params(),
        cost_estimate=cost(3),
    )(place, *kept, *low, *flat, before, pack)


def qkv_back_kernel(recv_ref, rows_ref, vec_ref, weight_ref, part_ref, grads_ref, sums_ref):
    grad_q = unpack_heads(recv_ref, BOTH).astype(BF)
    mask = low_lanes((BOTH, 128))
    key_columns, value_columns = [], []
    for pair in range(HEADS_DEV // 2):
        sums = []
        for head in (2 * pair, 2 * pair + 1):
            total = recv_ref[head * QUARTERS, 0:BOTH, :].astype(F32)
            for quarter in range(1, QUARTERS):
                total = total + recv_ref[head * QUARTERS + quarter, 0:BOTH, :].astype(F32)
            sums.append(total)
        key_columns.append(jnp.where(mask, sums[0], turn(sums[1])))
        value_columns.append(jnp.where(mask, turn(sums[0]), sums[1]))
    grad_k = jnp.concatenate(key_columns, axis=1).astype(BF)
    grad_v = jnp.concatenate(value_columns, axis=1).astype(BF)
    grads_ref[0:BOTH, 0:HALF_W] = grad_q
    grads_ref[0:BOTH, HALF_W:MODEL] = grad_k
    grads_ref[0:BOTH, MODEL : MODEL + HALF_W] = grad_v
    result = (
        nt(grad_q, qkv_weight(weight_ref, 0))
        + nt(grad_k, qkv_weight(weight_ref, 1))
        + nt(grad_v, qkv_weight(weight_ref, 2))
    )
    part_ref[...] = result.astype(BF)
    hat, _ = norm_parts(rows_ref[...].astype(F32))
    sums_ref[...] = jnp.zeros((16, MODEL), F32)
    sums_ref[0:1, :] = column_sum(result * hat)
    sums_ref[1:2, :] = column_sum(result)
    sums_ref[2:3, 0:HALF_W] = column_sum(grad_q.astype(F32))
    sums_ref[2:3, HALF_W:MODEL] = column_sum(grad_v.astype(F32))
    grads_ref[BOTH:TALL, 0:MODEL] = sums_ref[...].astype(BF)
    grads_ref[BOTH:TALL, MODEL : MODEL + HALF_W] = jnp.zeros((16, HALF_W), BF)


def qkv_back_call(recv, rows, small, weight, block_at):
    return pl.pallas_call(
        qkv_back_kernel,
        grid=(1,),
        in_specs=[
            whole((WIDE, SEND_ROWS, 128)),
            whole((BOTH, MODEL)),
            whole((8, MODEL)),
            qkv_block(block_at),
        ],
        out_specs=[whole((BOTH, MODEL)), whole((TALL, 3 * HALF_W))],
        out_shape=[
            jax.ShapeDtypeStruct((BOTH, MODEL), BF),
            jax.ShapeDtypeStruct((TALL, 3 * HALF_W), BF),
        ],
        scratch_shapes=[pltpu.VMEM((16, MODEL), F32)],
        compiler_params=params(),
        cost_estimate=cost(5),
    )(recv, rows, small[0], weight)


def store_qkv_grads(place_ref, refs, grad_ref):
    rows = both_cores(*refs[0:2])

    def part(which):
        columns = slice(which * HALF_W, which * HALF_W + HALF_W)
        grads = jnp.concatenate([ref[0:BOTH, columns] for ref in refs[2:4]], axis=0)
        return tn(rows, grads).reshape(WIDE, 32, HALF_W)

    low, high = slice(0, HALF_W), slice(HALF_W, MODEL)
    store_mine(place_ref, part(0), grad_ref, EVERY, slice(0, 32), low)
    store_mine(place_ref, part(1), grad_ref, EVERY, slice(0, 32), high)
    values = part(2)
    store_mine(place_ref, values[:, 0:16], grad_ref, EVERY, slice(32, 48), low)
    store_mine(place_ref, values[:, 16:32], grad_ref, EVERY, slice(32, 48), high)


def qkv_weight_kernel(place_ref, *refs):
    store_qkv_grads(place_ref, refs, refs[-1])


def qkv_weight_last_kernel(place_ref, *refs):
    grad_ref = refs[-1]
    store_qkv_grads(place_ref, refs, grad_ref)
    rows = sum(ref[BOTH : BOTH + 8, 0:MODEL].astype(F32) for ref in refs[2:4]).astype(BF)
    grad_ref[:, 48:56, :] = jnp.broadcast_to(rows[None], (CHIPS, 8, MODEL))


QKV_WEIGHT_SPECS = (
    [SCALARS]
    + twice(pl.BlockSpec((BOTH, MODEL), lambda i: (0, 3)))
    + twice(whole((TALL, 3 * HALF_W)))
)


def qkv_weight_call(place, kept, grads, pack):
    return pl.pallas_call(
        qkv_weight_kernel,
        grid=(1,),
        in_specs=QKV_WEIGHT_SPECS + [ANYWHERE],
        out_specs=qkv_chips(3),
        out_shape=jax.ShapeDtypeStruct((CHIPS, PACK_ROWS, MODEL), BF),
        input_output_aliases={5: 0},
        compiler_params=params(),
        cost_estimate=cost(4),
    )(place, *kept, *grads, pack)


def qkv_chips(index):
    return pl.BlockSpec((CHIPS, 48, MODEL), lambda i: (0, index, 0))


def qkv_weight_last_call(place, kept, grads):
    return pl.pallas_call(
        qkv_weight_last_kernel,
        grid=(1,),
        in_specs=QKV_WEIGHT_SPECS,
        out_specs=whole((CHIPS, 56, MODEL)),
        out_shape=jax.ShapeDtypeStruct((CHIPS, 56, MODEL), BF),
        compiler_params=params(),
        cost_estimate=cost(4),
    )(place, *kept, *grads)


def with_core(block):
    return block, lax.ppermute(block, "wide", [(i, i ^ 1) for i in range(WIDE)])


def all_to_all(block):
    return lax.all_to_all(block, "wide", 0, 0, tiled=True)


def layer_forward(place, inputs, ids, qkv, rest, small):
    flags, key_ids, query_ids = ids
    sent, rows, normed_a = qkv_call(inputs, small, *qkv)
    recv = all_to_all(sent)
    mix_sent, mix_keep, lse = attend_call(flags, recv, key_ids, query_ids)
    mix_recv = lax.all_to_all(
        mix_sent.reshape(2 * WIDE, 16, 128), ("tensor", "wide"), 0, 0, tiled=True
    )
    branch, middle, pre, wide_kept, mlp = mlp_call(place, rows, normed_a, mix_recv, small, rest)
    mlp_recv = swap(mlp, "tensor")
    return dict(
        rows=rows, recv=recv, keep=mix_keep, lse=lse, branch=branch, middle=middle, pre=pre,
        mlp=mlp, mlp_recv=mlp_recv, for_weights=with_core(wide_kept),
    )


def layer_backward(place, inputs, kept, ids, qkv, rest, small, pack=None):
    flags, key_ids, query_ids = ids
    grad, mlp_back, part, *input_grad = mlp_back_call(
        inputs, small, kept["pre"], rest
    )
    mlp_pair = with_core(mlp_back)
    pack = mlp_weight_call(place, kept["for_weights"], mlp_pair, pack)
    middle_grad, mix_grad, low_a = out_back_call(
        grad, part, swap(part, "tensor"), kept["middle"], kept["branch"], kept["mlp"],
        kept["mlp_recv"], small, rest, pack,
    )
    back = attend_back_call(
        flags, kept["recv"], all_to_all(mix_grad), kept["keep"], kept["lse"], key_ids, query_ids
    )
    qkv_part, qkv_grads = qkv_back_call(all_to_all(back), kept["rows"], small, *qkv)
    carried = (middle_grad, qkv_part, swap(qkv_part, "tensor"), kept["rows"])
    for_weights = mlp_pair, with_core(low_a), with_core(qkv_grads)
    return carried, pack, for_weights, input_grad


def body(
    x_in, out_cot, image_ids, w_qkv, w_out, w_fc1, w_fc2, gains, shifts, layer_scales, qv_bias, fc1_bias
):
    section = lax.axis_index("section")
    tensor = lax.axis_index("tensor")
    wide = lax.axis_index("wide")
    is_first = section == 0

    def one(array):
        return lax.dynamic_index_in_dim(array, section, 0, keepdims=False)

    place = jnp.stack([tensor, lax.rem(wide, 2)]).astype(jnp.int32)

    qkv = w_qkv[0]
    small_rows = jnp.concatenate(
        [
            jnp.pad(jnp.concatenate([gains[0], shifts[0], layer_scales[0]], axis=0), ((0, 0), (0, 32))),
            jnp.pad(qv_bias[0], ((0, 0), (0, 48))),
            fc1_bias,
        ],
        axis=0,
    )
    pack_a = jnp.concatenate(
        [
            jnp.concatenate([qkv[:, 0], qkv[:, 1]], axis=1),
            jnp.concatenate([qkv[0:16, 2], qkv[16:32, 2]], axis=1),
            jnp.pad(small_rows, ((0, 5), (0, MODEL - 64))),
        ],
        axis=0,
    )
    own_rows, own_cot = one(x_in), one(out_cot)
    partner = swap(jnp.concatenate([own_rows, own_cot, w_out[0]], axis=0), "tensor")
    other_rows, other_cot, other_out = partner[:ROWS], partner[ROWS:BOTH], partner[BOTH:]
    pack_b = jnp.concatenate(
        [w_fc2[0], w_fc1[0][:, :MODEL], w_fc1[0][:, MODEL:], w_out[0], other_out], axis=0
    )
    other_a = swap(pack_a, "section")
    other_b = swap(pack_b, "section")

    def gather(block):
        return lax.all_gather(block, "wide", axis=0, tiled=False)

    def joined_a(first, second):
        vectors = jnp.concatenate([first[48:64, :HALF_W], second[48:64, :HALF_W]], axis=1)
        return jnp.concatenate([first[:48], second[:48], vectors], axis=0)

    attn_both = gather(jnp.where(is_first, joined_a(pack_a, other_a), joined_a(other_a, pack_a)))

    rest_first = gather(
        jnp.concatenate([jnp.where(is_first, pack_b, other_b), attn_both[0, 96:112]], axis=0)
    )

    def rest_second(rows):
        return gather(jnp.concatenate([jnp.where(is_first, other_b, pack_b), rows], axis=0))

    def small_of(layer):
        block = attn_both[:, 96:107, layer * HALF_W : layer * HALF_W + 64].astype(F32)
        vec = jnp.transpose(block[:, 0:8, 0:32], (1, 0, 2)).reshape(8, MODEL)
        bias = jnp.transpose(block[:, 8:10, 0:16], (1, 0, 2)).reshape(2, HALF_W)
        return vec, bias, block[:, 10].reshape(1, HIDDEN)

    small = (small_of(0), small_of(1))

    id_grid = one(image_ids).reshape(2, WIDE, ROWS)
    sorted_ids = jnp.where(tensor == 0, id_grid, id_grid[::-1])
    key_ids = sorted_ids.reshape(CHUNKS, 1, 512)
    quarter = lax.rem(wide, QUARTERS)
    half_ids = lax.dynamic_index_in_dim(sorted_ids, quarter // 2, 0, keepdims=False)
    quarter_ids = lax.dynamic_slice_in_dim(half_ids, lax.rem(quarter, 2) * 32, 32, 1)
    query_ids = jnp.transpose(quarter_ids.reshape(BLOCKS_Q, 8, 2, 16), (0, 2, 1, 3)).reshape(
        BLOCKS_Q, 256, 1
    )
    key_low, key_high = jnp.min(key_ids[:, 0], axis=1), jnp.max(key_ids[:, 0], axis=1)
    query_low, query_high = jnp.min(query_ids[..., 0], axis=1), jnp.max(query_ids[..., 0], axis=1)
    flags = (
        (query_low[:, None] <= key_high[None]) & (query_high[:, None] >= key_low[None])
    ).astype(jnp.int32)
    ids = (flags, key_ids, query_ids)

    qkv_parts = ((attn_both, 0), (attn_both, 1))
    kept0 = layer_forward(place, (own_rows, other_rows), ids, qkv_parts[0], rest_first, small[0])
    rest = (rest_first, rest_second(kept0["mlp"][:16]))
    kept1 = layer_forward(
        place,
        (kept0["middle"], kept0["mlp"], kept0["mlp_recv"], small[0][0]),
        ids, qkv_parts[1], rest[1], small[1],
    )
    branch1 = kept1["mlp"][:ROWS].astype(F32) + kept1["mlp_recv"][ROWS:].astype(F32)
    out1 = (
        kept1["middle"][:ROWS]
        + small[1][0][SCALE_M] * (branch1 + small[1][0][SHIFT_M])
    ).astype(BF)
    out0 = kept1["rows"][:ROWS]

    same_core = [list(range(core, WIDE, 2)) for core in range(2)]

    def over_chips(pack):
        return lax.psum_scatter(
            pack.reshape(CHIPS * pack.shape[1], MODEL),
            "wide", scatter_dimension=0, axis_index_groups=same_core, tiled=True,
        )

    carried1, pack1, back1, _ = layer_backward(
        place, (own_cot, other_cot), kept1, ids, qkv_parts[1], rest[1], small[1]
    )
    kept_pair0, kept_pair1 = kept0["for_weights"], kept1["for_weights"]
    mlp_back1, low1, grads1 = back1
    sum_mlp1 = over_chips(pack1)
    pack = out_weight_call(place, kept_pair1, low1)
    pack = qkv_weight_call(place, kept_pair1, grads1, pack)

    carried0, pack, back0, (grad_x1,) = layer_backward(
        place, carried1 + (small[1][0], pack), kept0, ids, qkv_parts[0], rest[0], small[0], pack
    )
    mlp_back0, low0, grads0 = back0
    pack = out_weight_last_call(
        place, kept_pair0, low0, (low1, low0, grads1, mlp_back1, mlp_back0), sum_mlp1, pack
    )
    sum_mid = over_chips(pack)
    last_recv = lax.all_to_all(
        qkv_weight_last_call(place, kept_pair0, grads0),
        "wide", 0, 0, axis_index_groups=same_core, tiled=True,
    )
    sum_last = jnp.sum(last_recv.astype(F32), axis=0)

    middle_grad0, part0, part_recv0, _ = carried0
    hat0, rstd0 = norm_parts(own_rows.astype(F32))
    grad_norm0 = part0[:ROWS].astype(F32) + part_recv0[ROWS:].astype(F32)
    grad_x0 = middle_grad0[:ROWS] + norm_back(grad_norm0, hat0, rstd0, small[0][0][GAIN_A])

    def lanes(rows, width):
        return lax.dynamic_slice_in_dim(rows, wide * width, width, rows.ndim - 1)

    mid0 = jnp.concatenate([sum_mid[0:128], sum_mid[192:208]], axis=0)
    mid1 = jnp.concatenate([sum_mlp1, sum_mid[128:144]], axis=0)
    mid_total = jnp.where(is_first, mid0, mid1).astype(F32) + swap(
        jnp.where(is_first, mid1, mid0), "section"
    ).astype(F32)
    late0 = jnp.concatenate([sum_last[0:52].astype(BF), sum_mid[232:236], sum_mid[216:224]], axis=0)
    late1 = jnp.concatenate(
        [sum_mid[144:192], sum_mid[224:228], sum_mid[228:232], sum_mid[208:216]], axis=0
    )
    late_own = jnp.where(is_first, late0, late1)
    late_away = jnp.where(is_first, late1, late0)
    late_total = late_own.astype(F32) + swap(late_away, "section").astype(F32)
    across = lax.ppermute(late_away[48:50], ("section", "tensor"), [(0, 3), (3, 0), (1, 2), (2, 1)])
    heads_total = late_total[48:50] + (
        swap(late_own[48:50], "tensor").astype(F32) + across.astype(F32)
    )
    mlp_total, out_total, qkv_total = mid_total[0:128], mid_total[128:144], late_total[0:48]
    norms = lanes(jnp.concatenate([heads_total, late_total[52:53], late_total[56:61]], axis=0), 32)
    g_gains = jnp.stack([norms[0], norms[3]])
    g_shifts = jnp.stack([norms[1], norms[5], norms[4], norms[2]])
    g_scales = jnp.stack([norms[6], norms[7]])
    g_qv = lanes(late_total[50].reshape(2, HALF_W), 16)
    g_fc1_bias = lanes(late_total[53:55].reshape(HIDDEN), 64)
    g_fc2 = mlp_total[0:64]
    g_fc1 = jnp.concatenate([mlp_total[64:96], mlp_total[96:128]], axis=1)
    pairs = qkv_total[0:32]
    value_grad = jnp.concatenate([qkv_total[32:48, :HALF_W], qkv_total[32:48, HALF_W:]], axis=0)
    g_qkv = jnp.stack([pairs[:, :HALF_W], pairs[:, HALF_W:], value_grad], axis=1)

    def by_micro(first, second):
        own = jnp.where(is_first, first, second)
        came = swap(jnp.where(is_first, second, first), "section")
        return jnp.stack([jnp.where(is_first, own, came), jnp.where(is_first, came, own)])

    return (
        by_micro(out0, out1)[None],
        by_micro(grad_x0, grad_x1)[None],
        g_qkv[None],
        out_total[None],
        g_fc1[None],
        g_fc2[None],
        g_gains[None],
        g_shifts[None],
        g_scales[None],
        g_qv[None],
        g_fc1_bias[None],
    )


def solution(mesh):
    in_specs = (
        P(None, ("tensor", "wide"), None),
        P(None, ("tensor", "wide"), None),
        P(),
        P("section", "wide", None, "tensor"),
        P("section", ("tensor", "wide"), None),
        P("section", "wide", "tensor"),
        P("section", ("tensor", "wide"), None),
        P("section", None, "wide"),
        P("section", None, "wide"),
        P("section", None, "wide"),
        P("section", None, ("tensor", "wide")),
        P("section", ("tensor", "wide")),
    )
    out_specs = (
        P("section", None, ("tensor", "wide"), None),
        P("section", None, ("tensor", "wide"), None),
        P("section", "wide", None, "tensor"),
        P("section", ("tensor", "wide"), None),
        P("section", "wide", "tensor"),
        P("section", ("tensor", "wide"), None),
        P("section", None, "wide"),
        P("section", None, "wide"),
        P("section", None, "wide"),
        P("section", None, ("tensor", "wide")),
        P("section", ("tensor", "wide")),
    )
    return jax.shard_map(body, mesh=mesh, in_specs=in_specs, out_specs=out_specs, check_vma=False)
```

```python
import jax
import jax.numpy as jnp
from jax import lax
from jax.experimental import pallas as pl
from jax.experimental.pallas import tpu as pltpu
from jax.sharding import PartitionSpec as P

HEAD = 64
EPS = 1e-06
NEG_FILL = -1e30
ROOT_HALF = 0.7071067811865476
INV_ROOT_TAU = 0.3989422804014327
SCALE = HEAD ** (-0.5)
BF = jnp.bfloat16
F32 = jnp.float32
MIB = 1024 * 1024

ROWS = 64
BOTH = 128
WIDE = 32
HEADS_DEV = 8
QUARTERS = 4
HALF_W = 512
MODEL = 1024
HIDDEN = 2048
SEND_ROWS = 144
BLOCKS_Q = 4
CHUNKS = 8


def params(limit=56):
    return pltpu.CompilerParams(vmem_limit_bytes=limit * MIB)


def cost(micros):
    return pl.CostEstimate(flops=int(micros * 1e9), bytes_accessed=100000, transcendentals=0)


def whole(shape):
    count = len(shape)
    return pl.BlockSpec(shape, lambda *g: (0,) * count)


ANYWHERE = pl.BlockSpec(memory_space=pl.ANY)
SCALARS = pl.BlockSpec(memory_space=pltpu.SMEM)
EVERY = slice(None)


def swap(block, axis):
    return lax.ppermute(block, axis, [(0, 1), (1, 0)])


def nt(left, right):
    return lax.dot_general(left, right, (((1,), (1,)), ((), ())), preferred_element_type=F32)


def tn(left, right):
    return lax.dot_general(left, right, (((0,), (0,)), ((), ())), preferred_element_type=F32)


def nn(left, right):
    return jnp.dot(left, right, preferred_element_type=F32)


def low_lanes(shape):
    return lax.broadcasted_iota(jnp.int32, shape, len(shape) - 1) < HEAD


def turn(tile):
    return pltpu.roll(tile, HEAD, 1)


def pack_heads(tile, out_ref, pair, row0):
    rolled = turn(tile)
    for quarter in range(QUARTERS):
        first = slice(quarter * 32, quarter * 32 + 16)
        second = slice(quarter * 32 + 16, quarter * 32 + 32)
        mask = low_lanes((16, 128))
        even = jnp.where(mask, tile[first], rolled[second])
        odd = jnp.where(mask, rolled[first], tile[second])
        out_ref[(2 * pair) * QUARTERS + quarter, row0 : row0 + 16, :] = even.astype(BF)
        out_ref[(2 * pair + 1) * QUARTERS + quarter, row0 : row0 + 16, :] = odd.astype(BF)


def unpack_heads(in_ref, row0, base=0):
    mask = low_lanes((16, 128))
    columns = []
    for pair in range(HEADS_DEV // 2):
        pieces = []
        for quarter in range(QUARTERS):
            even = in_ref[base + (2 * pair) * QUARTERS + quarter, row0 : row0 + 16, :].astype(F32)
            odd = in_ref[base + (2 * pair + 1) * QUARTERS + quarter, row0 : row0 + 16, :].astype(F32)
            pieces.append(jnp.where(mask, even, turn(odd)))
            pieces.append(jnp.where(mask, turn(even), odd))
        columns.append(jnp.concatenate(pieces, axis=0))
    return jnp.concatenate(columns, axis=1)


def norm_parts(rows_in):
    centre = jnp.mean(rows_in, axis=-1, keepdims=True)
    centred = rows_in - centre
    spread = jnp.mean(centred * centred, axis=-1, keepdims=True)
    rstd_rows = lax.rsqrt(spread + EPS)
    return centred * rstd_rows, rstd_rows


def norm_back(grad_rows, normal_rows, rstd_rows, gain_row):
    scaled = grad_rows * gain_row
    first_mean = jnp.mean(scaled, axis=-1, keepdims=True)
    second_mean = jnp.mean(scaled * normal_rows, axis=-1, keepdims=True)
    return rstd_rows * (scaled - first_mean - normal_rows * second_mean)


def joined(own_ref, recv_ref):
    recv = jnp.concatenate([recv_ref[ROWS:], recv_ref[:ROWS]], axis=0)
    return own_ref[...].astype(F32) + recv.astype(F32)


def column_sum(rows):
    return jnp.sum(rows[:ROWS], axis=0, keepdims=True) + jnp.sum(rows[ROWS:], axis=0, keepdims=True)


GAIN_A, GAIN_C, SHIFT_A, SHIFT_O, SHIFT_C, SHIFT_M, SCALE_A, SCALE_M = range(8)


def row_of(ref, at):
    return ref[at : at + 1, :]


def qkv_weight(ref, which):
    if which < 2:
        return ref[:, 0:32, which * HALF_W : which * HALF_W + HALF_W].reshape(MODEL, HALF_W)
    parts = [ref[:, 32:48, 0:HALF_W], ref[:, 32:48, HALF_W:MODEL]]
    return jnp.concatenate(parts, axis=1).reshape(MODEL, HALF_W)


def project_and_pack(rows, vec_ref, bias_ref, weight_ref, out_ref, rows_ref, normed_ref):
    rows_ref[...] = rows
    hat, _ = norm_parts(rows.astype(F32))
    normed = (hat * row_of(vec_ref, GAIN_A) + row_of(vec_ref, SHIFT_A)).astype(BF)
    normed_ref[...] = normed
    queries = nn(normed, qkv_weight(weight_ref, 0)) + bias_ref[0:1, :]
    keys = nn(normed, qkv_weight(weight_ref, 1))
    values = nn(normed, qkv_weight(weight_ref, 2)) + bias_ref[1:2, :]
    mask = low_lanes((BOTH, 128))
    for pair in range(HEADS_DEV // 2):
        columns = slice(pair * 128, pair * 128 + 128)
        key_tile, value_tile, query_tile = keys[:, columns], values[:, columns], queries[:, columns]
        even = jnp.where(mask, key_tile, turn(value_tile)).astype(BF)
        odd = jnp.where(mask, turn(key_tile), value_tile).astype(BF)
        for quarter in range(QUARTERS):
            out_ref[(2 * pair) * QUARTERS + quarter, 0:BOTH, :] = even
            out_ref[(2 * pair + 1) * QUARTERS + quarter, 0:BOTH, :] = odd
        pack_heads(query_tile, out_ref, pair, BOTH)


def qkv_first_kernel(own_ref, other_ref, vec_ref, bias_ref, weight_ref, out_ref, rows_ref, normed_ref):
    rows = jnp.concatenate([own_ref[...], other_ref[...]], axis=0)
    project_and_pack(rows, vec_ref, bias_ref, weight_ref, out_ref, rows_ref, normed_ref)


def qkv_next_kernel(
    middle_ref, mlp_own_ref, mlp_recv_ref, before_ref, vec_ref, bias_ref, weight_ref,
    out_ref, rows_ref, normed_ref,
):
    branch = joined(mlp_own_ref, mlp_recv_ref) + row_of(before_ref, SHIFT_M)
    rows = (middle_ref[...] + row_of(before_ref, SCALE_M) * branch).astype(BF)
    project_and_pack(rows, vec_ref, bias_ref, weight_ref, out_ref, rows_ref, normed_ref)


def qkv_block(index):
    return pl.BlockSpec((WIDE, 48, MODEL), lambda i: (0, index, 0))


def qkv_call(inputs, small, weight, block_at):
    vec, bias, _ = small
    first = len(inputs) == 2
    return pl.pallas_call(
        qkv_first_kernel if first else qkv_next_kernel,
        grid=(1,),
        in_specs=[whole(part.shape) for part in inputs]
        + [whole((8, MODEL)), whole((2, HALF_W)), qkv_block(block_at)],
        out_specs=[whole((WIDE, SEND_ROWS, 128)), whole((BOTH, MODEL)), whole((BOTH, MODEL))],
        out_shape=[
            jax.ShapeDtypeStruct((WIDE, SEND_ROWS, 128), BF),
            jax.ShapeDtypeStruct((BOTH, MODEL), BF),
            jax.ShapeDtypeStruct((BOTH, MODEL), BF),
        ],
        compiler_params=params(),
        cost_estimate=cost(5),
    )(*inputs, vec, bias, weight)


def query_tiles(packed):
    mask = low_lanes((128, 128))
    return jnp.concatenate(
        [jnp.where(mask, packed, 0.0), jnp.where(mask, turn(packed), 0.0)], axis=0
    )


def key_chunk(recv_ref, chunk):
    half, group = chunk // 4, chunk % 4
    block = recv_ref[group * 8 : group * 8 + 8, half * ROWS : half * ROWS + ROWS, :]
    return block.reshape(512, 128)


def lane_tiles(fn, block):
    return fn(fn(block[:, 0:128], block[:, 128:256]), fn(block[:, 256:384], block[:, 384:512]))


def attend_kernel(
    flag_ref, recv_ref, key_id_ref, query_id_ref, out_ref, keep_ref, lse_ref,
    score_ref, top_ref, total_ref, acc_ref,
):
    at = pl.program_id(0)
    packed = recv_ref[pl.ds(at * 8, 8), BOTH : BOTH + 16, :].astype(F32).reshape(128, 128)
    queries = (query_tiles(packed) * SCALE).astype(BF)
    query_ids = query_id_ref[0]
    top_ref[...] = jnp.full((256, 128), NEG_FILL, F32)
    total_ref[...] = jnp.zeros((256, 128), F32)
    acc_ref[...] = jnp.zeros((256, 128), F32)
    for chunk in range(CHUNKS):

        @pl.when(flag_ref[at, chunk] != 0)
        def _():
            scores = nt(queries, key_chunk(recv_ref, chunk))
            scores = jnp.where(query_ids == key_id_ref[chunk], scores, NEG_FILL)
            score_ref[chunk] = scores
            top_ref[...] = jnp.maximum(top_ref[...], lane_tiles(jnp.maximum, scores))

    top = jnp.max(top_ref[...], axis=1, keepdims=True)
    for chunk in range(CHUNKS):

        @pl.when(flag_ref[at, chunk] != 0)
        def _():
            expo = jnp.exp(score_ref[chunk] - top)
            total_ref[...] += lane_tiles(jnp.add, expo)
            acc_ref[...] += nn(expo.astype(BF), key_chunk(recv_ref, chunk))

    total = jnp.sum(total_ref[...], axis=1, keepdims=True)
    mixture = acc_ref[...] / total
    lse_ref[...] = top + jnp.log(total)
    mask = low_lanes((128, 128))
    joined = jnp.where(mask, turn(mixture[:128]), mixture[128:]).reshape(8, 16, 128)
    keep_ref[...] = joined
    out_ref[0] = joined.astype(BF)
    out_ref[1] = joined.astype(BF)


def attend_call(flags, recv, key_ids, query_ids):
    return pl.pallas_call(
        attend_kernel,
        grid_spec=pltpu.PrefetchScalarGridSpec(
            num_scalar_prefetch=1,
            grid=(BLOCKS_Q,),
            in_specs=[
                pl.BlockSpec((WIDE, SEND_ROWS, 128), lambda i, f: (0, 0, 0)),
                pl.BlockSpec((CHUNKS, 1, 512), lambda i, f: (0, 0, 0)),
                pl.BlockSpec((1, 256, 1), lambda i, f: (i, 0, 0)),
            ],
            out_specs=[
                pl.BlockSpec((2, 8, 16, 128), lambda i, f: (0, i, 0, 0)),
                pl.BlockSpec((8, 16, 128), lambda i, f: (i, 0, 0)),
                pl.BlockSpec((256, 1), lambda i, f: (i, 0)),
            ],
            scratch_shapes=[
                pltpu.VMEM((CHUNKS, 256, 512), F32),
                pltpu.VMEM((256, 128), F32),
                pltpu.VMEM((256, 128), F32),
                pltpu.VMEM((256, 128), F32),
            ],
        ),
        out_shape=[
            jax.ShapeDtypeStruct((2, WIDE, 16, 128), BF),
            jax.ShapeDtypeStruct((WIDE, 16, 128), F32),
            jax.ShapeDtypeStruct((1024, 1), F32),
        ],
        compiler_params=params(),
        cost_estimate=cost(12),
    )(flags, recv, key_ids, query_ids)


def attend_back_kernel(
    flag_ref, recv_ref, grad_ref, keep_ref, lse_ref, key_id_ref, query_id_ref, out_ref,
    key_grad_ref, query_grad_ref,
):
    at = pl.program_id(0)

    @pl.when(at == 0)
    def _():
        key_grad_ref[...] = jnp.zeros((WIDE, BOTH, 128), F32)

    mask = low_lanes((128, 128))
    packed = recv_ref[pl.ds(at * 8, 8), BOTH : BOTH + 16, :].astype(F32).reshape(128, 128)
    queries = (query_tiles(packed) * SCALE).astype(BF)
    grads = grad_ref[...].astype(F32).reshape(128, 128)
    grad_tile = jnp.concatenate(
        [jnp.where(mask, 0.0, turn(grads)), jnp.where(mask, 0.0, grads)], axis=0
    ).astype(BF)
    product = grads * keep_ref[...].reshape(128, 128)
    delta = jnp.concatenate(
        [
            jnp.sum(jnp.where(mask, product, 0.0), axis=1, keepdims=True),
            jnp.sum(jnp.where(mask, 0.0, product), axis=1, keepdims=True),
        ],
        axis=0,
    )
    lse = lse_ref[...]
    query_ids = query_id_ref[0]
    both = jnp.concatenate([queries, grad_tile], axis=0)
    query_grad_ref[...] = jnp.zeros((256, 128), F32)
    for chunk in range(CHUNKS):

        @pl.when(flag_ref[at, chunk] != 0)
        def _():
            half, group = chunk // 4, chunk % 4
            keys = key_chunk(recv_ref, chunk)
            scores = nt(queries, keys)
            scores = jnp.where(query_ids == key_id_ref[chunk], scores, NEG_FILL)
            chance = jnp.exp(scores - lse)
            grad_scores = (chance * (nt(grad_tile, keys) - delta)).astype(BF)
            query_grad_ref[...] += nn(grad_scores, keys)
            stacked = jnp.concatenate([grad_scores, chance.astype(BF)], axis=0)
            key_grad_ref[group * 8 : group * 8 + 8, half * ROWS : half * ROWS + ROWS, :] += tn(
                stacked, both
            ).reshape(8, ROWS, 128)

    query_grad = query_grad_ref[...] * SCALE
    joined = jnp.where(mask, query_grad[:128], turn(query_grad[128:]))
    out_ref[pl.ds(at * 8, 8), BOTH : BOTH + 16, :] = joined.astype(BF).reshape(8, 16, 128)

    @pl.when(at == BLOCKS_Q - 1)
    def _():
        out_ref[:, 0:BOTH, :] = key_grad_ref[...].astype(BF)


def attend_back_call(flags, recv, grads, keep, lse, key_ids, query_ids):
    return pl.pallas_call(
        attend_back_kernel,
        grid_spec=pltpu.PrefetchScalarGridSpec(
            num_scalar_prefetch=1,
            grid=(BLOCKS_Q,),
            in_specs=[
                pl.BlockSpec((WIDE, SEND_ROWS, 128), lambda i, f: (0, 0, 0)),
                pl.BlockSpec((8, 16, 128), lambda i, f: (i, 0, 0)),
                pl.BlockSpec((8, 16, 128), lambda i, f: (i, 0, 0)),
                pl.BlockSpec((256, 1), lambda i, f: (i, 0)),
                pl.BlockSpec((CHUNKS, 1, 512), lambda i, f: (0, 0, 0)),
                pl.BlockSpec((1, 256, 1), lambda i, f: (i, 0, 0)),
            ],
            out_specs=pl.BlockSpec((WIDE, SEND_ROWS, 128), lambda i, f: (0, 0, 0)),
            scratch_shapes=[
                pltpu.VMEM((WIDE, BOTH, 128), F32),
                pltpu.VMEM((256, 128), F32),
            ],
        ),
        out_shape=jax.ShapeDtypeStruct((WIDE, SEND_ROWS, 128), BF),
        compiler_params=params(),
        cost_estimate=cost(16),
    )(flags, recv, grads, keep, lse, key_ids, query_ids)


KEPT_C, KEPT_A, KEPT_MIX = slice(2048, 3072), slice(3072, 4096), slice(4096, 4608)
KEPT_WIDTH = 4608
TALL = BOTH + 16


def mlp_kernel(
    place_ref, rows_ref, normed_ref, recv_ref, vec_ref, bias_ref, out_weight_ref, one_ref, two_ref,
    branch_ref, middle_ref, pre_ref, kept_ref, out_ref, acc_ref,
):
    at = pl.program_id(0)

    @pl.when(at == 0)
    def _():
        tensor = place_ref[0]
        own = unpack_heads(recv_ref, 0, tensor * WIDE).astype(BF)
        partner = unpack_heads(recv_ref, 0, (1 - tensor) * WIDE).astype(BF)
        partner = jnp.concatenate([partner[ROWS:], partner[:ROWS]], axis=0)
        kept_ref[:, KEPT_A] = normed_ref[...]
        kept_ref[:, KEPT_MIX] = own
        proj = nn(own, out_weight_ref[:, 0:16, :].reshape(HALF_W, MODEL)) + nn(
            partner, out_weight_ref[:, 16:32, :].reshape(HALF_W, MODEL)
        )
        branch = proj + row_of(vec_ref, SHIFT_O)
        branch_ref[...] = branch
        middle = rows_ref[...].astype(F32) + row_of(vec_ref, SCALE_A) * branch
        middle_ref[...] = middle
        hat, _ = norm_parts(middle)
        kept_ref[:, KEPT_C] = (hat * row_of(vec_ref, GAIN_C) + row_of(vec_ref, SHIFT_C)).astype(BF)

    pre = nn(kept_ref[:, KEPT_C], one_ref[...].reshape(MODEL, MODEL)) + bias_ref[...]
    act = (0.5 * pre * (1.0 + lax.erf(pre * ROOT_HALF))).astype(BF)
    pre_ref[...] = pre
    part = nn(act, two_ref[...].reshape(MODEL, MODEL))

    @pl.when(at == 0)
    def _():
        kept_ref[:, 0:MODEL] = act
        acc_ref[...] = part

    @pl.when(at == 1)
    def _():
        kept_ref[:, MODEL:HIDDEN] = act
        out_ref[...] = (acc_ref[...] + part).astype(BF)


def mlp_call(place, rows, normed, recv, small, weights):
    vec, _, bias = small
    return pl.pallas_call(
        mlp_kernel,
        grid=(2,),
        in_specs=[
            pl.BlockSpec(memory_space=pltpu.SMEM),
            whole((BOTH, MODEL)),
            whole((BOTH, MODEL)),
            whole((2 * WIDE, 16, 128)),
            whole((8, MODEL)),
            pl.BlockSpec((1, MODEL), lambda j: (0, j)),
            pl.BlockSpec((WIDE, 32, MODEL), lambda j: (0, 4, 0)),
            pl.BlockSpec((WIDE, 32, MODEL), lambda j: (0, 2 + j, 0)),
            pl.BlockSpec((16, 64, MODEL), lambda j: (j, 0, 0)),
        ],
        out_specs=[
            whole((BOTH, MODEL)),
            whole((BOTH, MODEL)),
            pl.BlockSpec((BOTH, MODEL), lambda j: (0, j)),
            whole((BOTH, KEPT_WIDTH)),
            whole((BOTH, MODEL)),
        ],
        out_shape=[
            jax.ShapeDtypeStruct((BOTH, MODEL), F32),
            jax.ShapeDtypeStruct((BOTH, MODEL), F32),
            jax.ShapeDtypeStruct((BOTH, HIDDEN), F32),
            jax.ShapeDtypeStruct((BOTH, KEPT_WIDTH), BF),
            jax.ShapeDtypeStruct((BOTH, MODEL), BF),
        ],
        scratch_shapes=[pltpu.VMEM((BOTH, MODEL), F32)],
        compiler_params=params(),
        cost_estimate=cost(8),
    )(place, rows, normed, recv, vec, bias, weights, weights, weights)


def mlp_back_steps(
    grad, vec_ref, pre_ref, one_ref, two_ref, grad_ref, back_ref, out_ref, acc_ref, sums_ref,
):
    at = pl.program_id(0)

    @pl.when(at == 0)
    def _():
        rows = grad()
        grad_ref[...] = rows
        rows = rows.astype(F32)
        scaled = rows * row_of(vec_ref, SCALE_M)
        back_ref[0:BOTH, 2048:3072] = scaled.astype(BF)
        sums_ref[...] = jnp.zeros((16, MODEL), F32)
        sums_ref[0:1, :] = column_sum(scaled)

    pre = pre_ref[...]
    slope = 0.5 * (1.0 + lax.erf(pre * ROOT_HALF)) + pre * jnp.exp(-0.5 * pre * pre) * INV_ROOT_TAU
    grad_pre = (nt(back_ref[0:BOTH, 2048:3072], two_ref[...].reshape(MODEL, MODEL)) * slope).astype(BF)
    part = nt(grad_pre, one_ref[...].reshape(MODEL, MODEL))
    bias_sum = jnp.sum(grad_pre.astype(F32), axis=0, keepdims=True)

    @pl.when(at == 0)
    def _():
        back_ref[0:BOTH, 0:MODEL] = grad_pre
        acc_ref[...] = part
        sums_ref[1:2, :] = bias_sum

    @pl.when(at == 1)
    def _():
        back_ref[0:BOTH, MODEL:HIDDEN] = grad_pre
        out_ref[...] = (acc_ref[...] + part).astype(BF)
        sums_ref[2:3, :] = bias_sum
        back_ref[BOTH:TALL, 0:MODEL] = sums_ref[...].astype(BF)
        back_ref[BOTH:TALL, MODEL:3072] = jnp.zeros((16, 2048), BF)


def mlp_back_first_kernel(own_ref, other_ref, *refs):
    mlp_back_steps(lambda: jnp.concatenate([own_ref[...], other_ref[...]], axis=0), *refs)


def mlp_back_next_kernel(
    middle_grad_ref, part_own_ref, part_recv_ref, rows_ref, after_ref, pack_ref, *refs
):
    *refs, input_grad_ref, acc_ref, sums_ref = refs

    def grad():
        hat, rstd = norm_parts(rows_ref[...].astype(F32))
        grad_norm = joined(part_own_ref, part_recv_ref)
        total = middle_grad_ref[...] + norm_back(grad_norm, hat, rstd, row_of(after_ref, GAIN_A))
        input_grad_ref[...] = total[:ROWS]
        return total.astype(BF)

    mlp_back_steps(grad, *refs, acc_ref, sums_ref)


def mlp_back_call(inputs, small, pre, weights):
    first = len(inputs) == 2
    extra = [] if first else [(ROWS, MODEL)]
    return pl.pallas_call(
        mlp_back_first_kernel if first else mlp_back_next_kernel,
        grid=(2,),
        in_specs=[ANYWHERE if part.ndim == 3 else whole(part.shape) for part in inputs]
        + [
            whole((8, MODEL)),
            pl.BlockSpec((BOTH, MODEL), lambda j: (0, j)),
            pl.BlockSpec((WIDE, 32, MODEL), lambda j: (0, 2 + j, 0)),
            pl.BlockSpec((16, 64, MODEL), lambda j: (j, 0, 0)),
        ],
        out_specs=[whole((BOTH, MODEL)), whole((TALL, 3072)), whole((BOTH, MODEL))]
        + [whole(shape) for shape in extra],
        out_shape=[
            jax.ShapeDtypeStruct((BOTH, MODEL), BF),
            jax.ShapeDtypeStruct((TALL, 3072), BF),
            jax.ShapeDtypeStruct((BOTH, MODEL), BF),
        ]
        + [jax.ShapeDtypeStruct(shape, F32) for shape in extra],
        scratch_shapes=[pltpu.VMEM((BOTH, MODEL), F32), pltpu.VMEM((16, MODEL), F32)],
        compiler_params=params(),
        cost_estimate=cost(8),
    )(*inputs, small[0], pre, weights, weights)


PACK_ROWS = 240
CHIPS = WIDE // 2


def store_mine(place_ref, value, grad_ref, pairs, rows, columns):
    value = value.reshape(value.shape[0] // 2, 2, *value.shape[1:])
    for core in range(2):

        @pl.when(place_ref[1] == core)
        def _():
            grad_ref[pairs, rows, columns] = value[:, core].astype(BF)


def both_cores(own_ref, other_ref):
    return jnp.concatenate([own_ref[0:BOTH], other_ref[0:BOTH]], axis=0)


def twice(spec):
    return [spec, spec]


def mlp_weight_kernel(place_ref, *refs):
    act, normed, low, grad_pre = (both_cores(*refs[at : at + 2]) for at in range(0, 8, 2))
    grad_ref = refs[-1]
    grad_two = tn(act, low).reshape(16, 64, MODEL)
    grad_one = tn(normed, grad_pre).reshape(WIDE, 32, MODEL)
    for at in range(2):

        @pl.when(pl.program_id(0) == at)
        def _():
            store_mine(
                place_ref, grad_two, grad_ref, slice(8 * at, 8 * at + 8), slice(0, 64), EVERY
            )
            rows = slice(64 + 32 * at, 96 + 32 * at)
            store_mine(place_ref, grad_one, grad_ref, EVERY, rows, EVERY)


def mlp_weight_call(place, kept, back, part_recv, pack=None):
    rows, extra, aliases = 128, [part_recv], {}
    if pack is not None:
        rows, extra, aliases = PACK_ROWS, [pack], {9: 0}
    return pl.pallas_call(
        mlp_weight_kernel,
        grid=(2,),
        in_specs=[SCALARS]
        + twice(pl.BlockSpec((BOTH, MODEL), lambda j: (0, j)))
        + twice(pl.BlockSpec((BOTH, MODEL), lambda j: (0, 2)))
        + twice(pl.BlockSpec((BOTH, MODEL), lambda j: (0, 2)))
        + twice(pl.BlockSpec((BOTH, MODEL), lambda j: (0, j)))
        + [ANYWHERE] * len(extra),
        out_specs=pl.BlockSpec((CHIPS, 128, MODEL), lambda j: (0, 0, 0)),
        out_shape=jax.ShapeDtypeStruct((CHIPS, rows, MODEL), BF),
        input_output_aliases=aliases,
        compiler_params=params(),
        cost_estimate=cost(7),
    )(place, *kept, *kept, *back, *back, *extra)


def out_back_kernel(
    grad_ref, part_own_ref, part_recv_ref, middle_ref, branch_ref, vec_ref, weight_ref, pack_ref,
     middle_grad_ref, send_ref, low_ref, sums_ref,
):
    hat, rstd = norm_parts(middle_ref[...])
    grad_norm = joined(part_own_ref, part_recv_ref)
    total = grad_ref[...].astype(F32) + norm_back(grad_norm, hat, rstd, row_of(vec_ref, GAIN_C))
    middle_grad_ref[...] = total
    scaled = total * row_of(vec_ref, SCALE_A)
    rows = scaled.astype(BF)
    low_ref[0:BOTH, :] = rows
    grad_mix = nt(rows, weight_ref[...].reshape(HALF_W, MODEL))
    for pair in range(HEADS_DEV // 2):
        pack_heads(grad_mix[:, pair * 128 : pair * 128 + 128], send_ref, pair, 0)
    sums_ref[...] = jnp.zeros((16, MODEL), F32)
    sums_ref[0:1, :] = column_sum(grad_norm * hat)
    sums_ref[1:2, :] = column_sum(grad_norm)
    sums_ref[2:3, :] = column_sum(scaled)
    sums_ref[3:4, :] = column_sum(total * branch_ref[...])
    low_ref[BOTH:TALL, :] = sums_ref[...].astype(BF)


def out_back_call(grad, part_own, part_recv, middle, branch, small, weights, pack):
    return pl.pallas_call(
        out_back_kernel,
        grid=(1,),
        in_specs=[whole((BOTH, MODEL))] * 5
        + [whole((8, MODEL)), pl.BlockSpec((WIDE, 16, MODEL), lambda i: (0, 8, 0)), ANYWHERE],
        out_specs=[whole((BOTH, MODEL)), whole((WIDE, 16, 128)), whole((TALL, MODEL))],
        out_shape=[
            jax.ShapeDtypeStruct((BOTH, MODEL), F32),
            jax.ShapeDtypeStruct((WIDE, 16, 128), BF),
            jax.ShapeDtypeStruct((TALL, MODEL), BF),
        ],
        scratch_shapes=[pltpu.VMEM((16, MODEL), F32)],
        compiler_params=params(),
        cost_estimate=cost(4),
    )(grad, part_own, part_recv, middle, branch, small[0], weights, pack)


def store_out_grads(place_ref, refs, grad_ref, rows):
    grad = tn(both_cores(*refs[0:2]), both_cores(*refs[2:4])).reshape(WIDE, 16, MODEL)
    store_mine(place_ref, grad, grad_ref, EVERY, rows, EVERY)


def out_weight_kernel(place_ref, *refs):
    store_out_grads(place_ref, refs, refs[-1], EVERY)


def out_weight_last_kernel(place_ref, *refs):
    *sums_refs, before_ref, _, grad_ref = refs[4:]
    store_out_grads(place_ref, refs, grad_ref, slice(0, 16))
    parts = [
        own[0:count, :].astype(F32) + other[0:count, :].astype(F32)
        for own, other, count in zip(sums_refs[0::2], sums_refs[1::2], (8, 8, 4, 4, 4))
    ]
    rows = jnp.concatenate(parts + [before_ref[0:4, :].astype(F32)], axis=0).astype(BF)
    grad_ref[:, 16:48, :] = jnp.broadcast_to(rows[None], (CHIPS, 32, MODEL))


OUT_WEIGHT_SPECS = (
    [SCALARS]
    + twice(pl.BlockSpec((BOTH, HALF_W), lambda i: (0, 8)))
    + twice(pl.BlockSpec((BOTH, MODEL), lambda i: (0, 0)))
)
SUMS_SPEC = pl.BlockSpec((16, MODEL), lambda i: (8, 0))


def out_weight_call(place, kept, low):
    return pl.pallas_call(
        out_weight_kernel,
        grid=(1,),
        in_specs=OUT_WEIGHT_SPECS,
        out_specs=pl.BlockSpec((CHIPS, 16, MODEL), lambda i: (0, 8, 0)),
        out_shape=jax.ShapeDtypeStruct((CHIPS, PACK_ROWS, MODEL), BF),
        compiler_params=params(),
        cost_estimate=cost(2),
    )(place, *kept, *low)


def out_weight_last_call(place, kept, low, sums, before, pack):
    flat = [array for pair in sums for array in pair]
    return pl.pallas_call(
        out_weight_last_kernel,
        grid=(1,),
        in_specs=OUT_WEIGHT_SPECS + [SUMS_SPEC] * len(flat) + [whole((16, MODEL)), ANYWHERE],
        out_specs=pl.BlockSpec((CHIPS, 48, MODEL), lambda i: (0, 4, 0)),
        out_shape=jax.ShapeDtypeStruct((CHIPS, PACK_ROWS, MODEL), BF),
        input_output_aliases={6 + len(flat): 0},
        compiler_params=params(),
        cost_estimate=cost(3),
    )(place, *kept, *low, *flat, before, pack)


def qkv_back_kernel(
    recv_ref, rows_ref, grad_ref, mlp_own_ref, mlp_recv_ref, vec_ref, weight_ref,
    part_ref, grads_ref, sums_ref,
):
    grad_q = unpack_heads(recv_ref, BOTH).astype(BF)
    mask = low_lanes((BOTH, 128))
    key_columns, value_columns = [], []
    for pair in range(HEADS_DEV // 2):
        sums = []
        for head in (2 * pair, 2 * pair + 1):
            total = recv_ref[head * QUARTERS, 0:BOTH, :].astype(F32)
            for quarter in range(1, QUARTERS):
                total = total + recv_ref[head * QUARTERS + quarter, 0:BOTH, :].astype(F32)
            sums.append(total)
        key_columns.append(jnp.where(mask, sums[0], turn(sums[1])))
        value_columns.append(jnp.where(mask, turn(sums[0]), sums[1]))
    grad_k = jnp.concatenate(key_columns, axis=1).astype(BF)
    grad_v = jnp.concatenate(value_columns, axis=1).astype(BF)
    grads_ref[0:BOTH, 0:HALF_W] = grad_q
    grads_ref[0:BOTH, HALF_W:MODEL] = grad_k
    grads_ref[0:BOTH, MODEL : MODEL + HALF_W] = grad_v
    result = (
        nt(grad_q, qkv_weight(weight_ref, 0))
        + nt(grad_k, qkv_weight(weight_ref, 1))
        + nt(grad_v, qkv_weight(weight_ref, 2))
    )
    part_ref[...] = result.astype(BF)
    hat, _ = norm_parts(rows_ref[...].astype(F32))
    sums_ref[...] = jnp.zeros((16, MODEL), F32)
    sums_ref[0:1, :] = column_sum(result * hat)
    sums_ref[1:2, :] = column_sum(result)
    sums_ref[2:3, 0:HALF_W] = column_sum(grad_q.astype(F32))
    sums_ref[2:3, HALF_W:MODEL] = column_sum(grad_v.astype(F32))
    branch = joined(mlp_own_ref, mlp_recv_ref) + row_of(vec_ref, SHIFT_M)
    sums_ref[3:4, :] = column_sum(grad_ref[...].astype(F32) * branch)
    grads_ref[BOTH:TALL, 0:MODEL] = sums_ref[...].astype(BF)
    grads_ref[BOTH:TALL, MODEL : MODEL + HALF_W] = jnp.zeros((16, HALF_W), BF)


def qkv_back_call(recv, rows, grad, mlp, mlp_recv, small, weight, block_at):
    return pl.pallas_call(
        qkv_back_kernel,
        grid=(1,),
        in_specs=[
            whole((WIDE, SEND_ROWS, 128)),
            whole((BOTH, MODEL)),
            whole((BOTH, MODEL)),
            whole((BOTH, MODEL)),
            whole((BOTH, MODEL)),
            whole((8, MODEL)),
            qkv_block(block_at),
        ],
        out_specs=[whole((BOTH, MODEL)), whole((TALL, 3 * HALF_W))],
        out_shape=[
            jax.ShapeDtypeStruct((BOTH, MODEL), BF),
            jax.ShapeDtypeStruct((TALL, 3 * HALF_W), BF),
        ],
        scratch_shapes=[pltpu.VMEM((16, MODEL), F32)],
        compiler_params=params(),
        cost_estimate=cost(5),
    )(recv, rows, grad, mlp, mlp_recv, small[0], weight)


def store_qkv_grads(place_ref, refs, grad_ref):
    rows = both_cores(*refs[0:2])

    def part(which):
        columns = slice(which * HALF_W, which * HALF_W + HALF_W)
        grads = jnp.concatenate([ref[0:BOTH, columns] for ref in refs[2:4]], axis=0)
        return tn(rows, grads).reshape(WIDE, 32, HALF_W)

    low, high = slice(0, HALF_W), slice(HALF_W, MODEL)
    store_mine(place_ref, part(0), grad_ref, EVERY, slice(0, 32), low)
    store_mine(place_ref, part(1), grad_ref, EVERY, slice(0, 32), high)
    values = part(2)
    store_mine(place_ref, values[:, 0:16], grad_ref, EVERY, slice(32, 48), low)
    store_mine(place_ref, values[:, 16:32], grad_ref, EVERY, slice(32, 48), high)


def qkv_weight_kernel(place_ref, *refs):
    store_qkv_grads(place_ref, refs, refs[-1])


def qkv_weight_last_kernel(place_ref, *refs):
    grad_ref = refs[-1]
    store_qkv_grads(place_ref, refs, grad_ref)
    rows = sum(ref[BOTH : BOTH + 8, 0:MODEL].astype(F32) for ref in refs[2:4]).astype(BF)
    grad_ref[:, 48:56, :] = jnp.broadcast_to(rows[None], (CHIPS, 8, MODEL))


QKV_WEIGHT_SPECS = (
    [SCALARS]
    + twice(pl.BlockSpec((BOTH, MODEL), lambda i: (0, 3)))
    + twice(whole((TALL, 3 * HALF_W)))
)


def qkv_weight_call(place, kept, grads, pack):
    return pl.pallas_call(
        qkv_weight_kernel,
        grid=(1,),
        in_specs=QKV_WEIGHT_SPECS + [ANYWHERE],
        out_specs=qkv_chips(3),
        out_shape=jax.ShapeDtypeStruct((CHIPS, PACK_ROWS, MODEL), BF),
        input_output_aliases={5: 0},
        compiler_params=params(),
        cost_estimate=cost(4),
    )(place, *kept, *grads, pack)


def qkv_chips(index):
    return pl.BlockSpec((CHIPS, 48, MODEL), lambda i: (0, index, 0))


def qkv_weight_last_call(place, kept, grads):
    return pl.pallas_call(
        qkv_weight_last_kernel,
        grid=(1,),
        in_specs=QKV_WEIGHT_SPECS,
        out_specs=whole((CHIPS, 56, MODEL)),
        out_shape=jax.ShapeDtypeStruct((CHIPS, 56, MODEL), BF),
        compiler_params=params(),
        cost_estimate=cost(4),
    )(place, *kept, *grads)


def with_core(block):
    return block, lax.ppermute(block, "wide", [(i, i ^ 1) for i in range(WIDE)])


def all_to_all(block):
    return lax.all_to_all(block, "wide", 0, 0, tiled=True)


def layer_forward(place, inputs, ids, qkv, rest, small):
    flags, key_ids, query_ids = ids
    sent, rows, normed_a = qkv_call(inputs, small, *qkv)
    recv = all_to_all(sent)
    mix_sent, mix_keep, lse = attend_call(flags, recv, key_ids, query_ids)
    mix_recv = lax.all_to_all(
        mix_sent.reshape(2 * WIDE, 16, 128), ("tensor", "wide"), 0, 0, tiled=True
    )
    branch, middle, pre, wide_kept, mlp = mlp_call(place, rows, normed_a, mix_recv, small, rest)
    mlp_recv = swap(mlp, "tensor")
    return dict(
        rows=rows, recv=recv, keep=mix_keep, lse=lse, branch=branch, middle=middle, pre=pre,
        mlp=mlp, mlp_recv=mlp_recv, for_weights=with_core(wide_kept),
    )


def layer_backward(place, inputs, kept, ids, qkv, rest, small, pack=None):
    flags, key_ids, query_ids = ids
    grad, mlp_back, part, *input_grad = mlp_back_call(
        inputs, small, kept["pre"], rest
    )
    mlp_pair = with_core(mlp_back)
    part_recv = swap(part, "tensor")
    pack = mlp_weight_call(place, kept["for_weights"], mlp_pair, part_recv, pack)
    middle_grad, mix_grad, low_a = out_back_call(
        grad, part, part_recv, kept["middle"], kept["branch"], small, rest, pack
    )
    back = attend_back_call(
        flags, kept["recv"], all_to_all(mix_grad), kept["keep"], kept["lse"], key_ids, query_ids
    )
    qkv_part, qkv_grads = qkv_back_call(
        all_to_all(back), kept["rows"], grad, kept["mlp"], kept["mlp_recv"], small, *qkv
    )
    carried = (middle_grad, qkv_part, swap(qkv_part, "tensor"), kept["rows"])
    for_weights = mlp_pair, with_core(low_a), with_core(qkv_grads)
    return carried, pack, for_weights, input_grad


def body(
    x_in, out_cot, image_ids, w_qkv, w_out, w_fc1, w_fc2, gains, shifts, layer_scales, qv_bias, fc1_bias
):
    section = lax.axis_index("section")
    tensor = lax.axis_index("tensor")
    wide = lax.axis_index("wide")
    is_first = section == 0

    def one(array):
        return lax.dynamic_index_in_dim(array, section, 0, keepdims=False)

    place = jnp.stack([tensor, lax.rem(wide, 2)]).astype(jnp.int32)

    qkv = w_qkv[0]
    small_rows = jnp.concatenate(
        [
            jnp.pad(jnp.concatenate([gains[0], shifts[0], layer_scales[0]], axis=0), ((0, 0), (0, 32))),
            jnp.pad(qv_bias[0], ((0, 0), (0, 48))),
            fc1_bias,
        ],
        axis=0,
    )
    pack_a = jnp.concatenate(
        [
            jnp.concatenate([qkv[:, 0], qkv[:, 1]], axis=1),
            jnp.concatenate([qkv[0:16, 2], qkv[16:32, 2]], axis=1),
            jnp.pad(small_rows, ((0, 5), (0, MODEL - 64))),
        ],
        axis=0,
    )
    own_rows, own_cot = one(x_in), one(out_cot)
    partner = swap(jnp.concatenate([own_rows, own_cot, w_out[0]], axis=0), "tensor")
    other_rows, other_cot, other_out = partner[:ROWS], partner[ROWS:BOTH], partner[BOTH:]
    pack_b = jnp.concatenate(
        [w_fc2[0], w_fc1[0][:, :MODEL], w_fc1[0][:, MODEL:], w_out[0], other_out], axis=0
    )
    other_a = swap(pack_a, "section")
    other_b = swap(pack_b, "section")

    def gather(block):
        return lax.all_gather(block, "wide", axis=0, tiled=False)

    def joined_a(first, second):
        vectors = jnp.concatenate([first[48:64, :HALF_W], second[48:64, :HALF_W]], axis=1)
        return jnp.concatenate([first[:48], second[:48], vectors], axis=0)

    attn_both = gather(jnp.where(is_first, joined_a(pack_a, other_a), joined_a(other_a, pack_a)))

    rest_first = gather(
        jnp.concatenate([jnp.where(is_first, pack_b, other_b), attn_both[0, 96:112]], axis=0)
    )

    def rest_second(rows):
        return gather(jnp.concatenate([jnp.where(is_first, other_b, pack_b), rows], axis=0))

    def small_of(layer):
        block = attn_both[:, 96:107, layer * HALF_W : layer * HALF_W + 64].astype(F32)
        vec = jnp.transpose(block[:, 0:8, 0:32], (1, 0, 2)).reshape(8, MODEL)
        bias = jnp.transpose(block[:, 8:10, 0:16], (1, 0, 2)).reshape(2, HALF_W)
        return vec, bias, block[:, 10].reshape(1, HIDDEN)

    small = (small_of(0), small_of(1))

    id_grid = one(image_ids).reshape(2, WIDE, ROWS)
    sorted_ids = jnp.where(tensor == 0, id_grid, id_grid[::-1])
    key_ids = sorted_ids.reshape(CHUNKS, 1, 512)
    quarter = lax.rem(wide, QUARTERS)
    half_ids = lax.dynamic_index_in_dim(sorted_ids, quarter // 2, 0, keepdims=False)
    quarter_ids = lax.dynamic_slice_in_dim(half_ids, lax.rem(quarter, 2) * 32, 32, 1)
    query_ids = jnp.transpose(quarter_ids.reshape(BLOCKS_Q, 8, 2, 16), (0, 2, 1, 3)).reshape(
        BLOCKS_Q, 256, 1
    )
    key_low, key_high = jnp.min(key_ids[:, 0], axis=1), jnp.max(key_ids[:, 0], axis=1)
    query_low, query_high = jnp.min(query_ids[..., 0], axis=1), jnp.max(query_ids[..., 0], axis=1)
    flags = (
        (query_low[:, None] <= key_high[None]) & (query_high[:, None] >= key_low[None])
    ).astype(jnp.int32)
    ids = (flags, key_ids, query_ids)

    qkv_parts = ((attn_both, 0), (attn_both, 1))
    kept0 = layer_forward(place, (own_rows, other_rows), ids, qkv_parts[0], rest_first, small[0])
    rest = (rest_first, rest_second(kept0["mlp"][:16]))
    kept1 = layer_forward(
        place,
        (kept0["middle"], kept0["mlp"], kept0["mlp_recv"], small[0][0]),
        ids, qkv_parts[1], rest[1], small[1],
    )
    branch1 = kept1["mlp"][:ROWS].astype(F32) + kept1["mlp_recv"][ROWS:].astype(F32)
    out1 = (
        kept1["middle"][:ROWS]
        + small[1][0][SCALE_M] * (branch1 + small[1][0][SHIFT_M])
    ).astype(BF)
    out0 = kept1["rows"][:ROWS]

    same_core = [list(range(core, WIDE, 2)) for core in range(2)]

    def over_chips(pack):
        return lax.psum_scatter(
            pack.reshape(CHIPS * pack.shape[1], MODEL),
            "wide", scatter_dimension=0, axis_index_groups=same_core, tiled=True,
        )

    carried1, pack1, back1, _ = layer_backward(
        place, (own_cot, other_cot), kept1, ids, qkv_parts[1], rest[1], small[1]
    )
    kept_pair0, kept_pair1 = kept0["for_weights"], kept1["for_weights"]
    mlp_back1, low1, grads1 = back1
    sum_mlp1 = over_chips(pack1)
    pack = out_weight_call(place, kept_pair1, low1)
    pack = qkv_weight_call(place, kept_pair1, grads1, pack)

    carried0, pack, back0, (grad_x1,) = layer_backward(
        place, carried1 + (small[1][0], pack), kept0, ids, qkv_parts[0], rest[0], small[0], pack
    )
    mlp_back0, low0, grads0 = back0
    pack = out_weight_last_call(
        place, kept_pair0, low0, (low1, low0, grads1, mlp_back1, mlp_back0), sum_mlp1, pack
    )
    sum_mid = over_chips(pack)
    last_recv = lax.all_to_all(
        qkv_weight_last_call(place, kept_pair0, grads0),
        "wide", 0, 0, axis_index_groups=same_core, tiled=True,
    )
    sum_last = jnp.sum(last_recv.astype(F32), axis=0)

    middle_grad0, part0, part_recv0, _ = carried0
    hat0, rstd0 = norm_parts(own_rows.astype(F32))
    grad_norm0 = part0[:ROWS].astype(F32) + part_recv0[ROWS:].astype(F32)
    grad_x0 = middle_grad0[:ROWS] + norm_back(grad_norm0, hat0, rstd0, small[0][0][GAIN_A])

    def lanes(rows, width):
        return lax.dynamic_slice_in_dim(rows, wide * width, width, rows.ndim - 1)

    mid0 = jnp.concatenate([sum_mid[0:128], sum_mid[192:208]], axis=0)
    mid1 = jnp.concatenate([sum_mlp1, sum_mid[128:144]], axis=0)
    mid_total = jnp.where(is_first, mid0, mid1).astype(F32) + swap(
        jnp.where(is_first, mid1, mid0), "section"
    ).astype(F32)
    late0 = jnp.concatenate([sum_last[0:52].astype(BF), sum_mid[232:236], sum_mid[216:224]], axis=0)
    late1 = jnp.concatenate(
        [sum_mid[144:192], sum_mid[224:228], sum_mid[228:232], sum_mid[208:216]], axis=0
    )
    late_own = jnp.where(is_first, late0, late1)
    late_away = jnp.where(is_first, late1, late0)
    late_total = late_own.astype(F32) + swap(late_away, "section").astype(F32)
    across = lax.ppermute(late_away[48:50], ("section", "tensor"), [(0, 3), (3, 0), (1, 2), (2, 1)])
    heads_total = late_total[48:50] + (
        swap(late_own[48:50], "tensor").astype(F32) + across.astype(F32)
    )
    mlp_total, out_total, qkv_total = mid_total[0:128], mid_total[128:144], late_total[0:48]
    norms = lanes(jnp.concatenate([heads_total, late_total[52:53], late_total[56:60], late_total[51:52]], axis=0), 32)
    g_gains = jnp.stack([norms[0], norms[3]])
    g_shifts = jnp.stack([norms[1], norms[5], norms[4], norms[2]])
    g_scales = jnp.stack([norms[6], norms[7]])
    g_qv = lanes(late_total[50].reshape(2, HALF_W), 16)
    g_fc1_bias = lanes(late_total[53:55].reshape(HIDDEN), 64)
    g_fc2 = mlp_total[0:64]
    g_fc1 = jnp.concatenate([mlp_total[64:96], mlp_total[96:128]], axis=1)
    pairs = qkv_total[0:32]
    value_grad = jnp.concatenate([qkv_total[32:48, :HALF_W], qkv_total[32:48, HALF_W:]], axis=0)
    g_qkv = jnp.stack([pairs[:, :HALF_W], pairs[:, HALF_W:], value_grad], axis=1)

    def by_micro(first, second):
        own = jnp.where(is_first, first, second)
        came = swap(jnp.where(is_first, second, first), "section")
        return jnp.stack([jnp.where(is_first, own, came), jnp.where(is_first, came, own)])

    return (
        by_micro(out0, out1)[None],
        by_micro(grad_x0, grad_x1)[None],
        g_qkv[None],
        out_total[None],
        g_fc1[None],
        g_fc2[None],
        g_gains[None],
        g_shifts[None],
        g_scales[None],
        g_qv[None],
        g_fc1_bias[None],
    )


def solution(mesh):
    in_specs = (
        P(None, ("tensor", "wide"), None),
        P(None, ("tensor", "wide"), None),
        P(),
        P("section", "wide", None, "tensor"),
        P("section", ("tensor", "wide"), None),
        P("section", "wide", "tensor"),
        P("section", ("tensor", "wide"), None),
        P("section", None, "wide"),
        P("section", None, "wide"),
        P("section", None, "wide"),
        P("section", None, ("tensor", "wide")),
        P("section", ("tensor", "wide")),
    )
    out_specs = (
        P("section", None, ("tensor", "wide"), None),
        P("section", None, ("tensor", "wide"), None),
        P("section", "wide", None, "tensor"),
        P("section", ("tensor", "wide"), None),
        P("section", "wide", "tensor"),
        P("section", ("tensor", "wide"), None),
        P("section", None, "wide"),
        P("section", None, "wide"),
        P("section", None, "wide"),
        P("section", None, ("tensor", "wide")),
        P("section", ("tensor", "wide")),
    )
    return jax.shard_map(body, mesh=mesh, in_specs=in_specs, out_specs=out_specs, check_vma=False)
```

```python
import jax
import jax.numpy as jnp
from jax import lax
from jax.experimental import pallas as pl
from jax.experimental.pallas import tpu as pltpu
from jax.sharding import PartitionSpec as P

HEAD = 64
EPS = 1e-06
NEG_FILL = -1e30
ROOT_HALF = 0.7071067811865476
INV_ROOT_TAU = 0.3989422804014327
SCALE = HEAD ** (-0.5)
BF = jnp.bfloat16
F32 = jnp.float32
MIB = 1024 * 1024

ROWS = 64
BOTH = 128
WIDE = 32
HEADS_DEV = 8
QUARTERS = 4
HALF_W = 512
MODEL = 1024
HIDDEN = 2048
SEND_ROWS = 144
BLOCKS_Q = 4
CHUNKS = 8


def params(limit=56):
    return pltpu.CompilerParams(vmem_limit_bytes=limit * MIB)


def cost(micros):
    return pl.CostEstimate(flops=int(micros * 1e9), bytes_accessed=100000, transcendentals=0)


def whole(shape):
    count = len(shape)
    return pl.BlockSpec(shape, lambda *g: (0,) * count)


ANYWHERE = pl.BlockSpec(memory_space=pl.ANY)
SCALARS = pl.BlockSpec(memory_space=pltpu.SMEM)
EVERY = slice(None)


def swap(block, axis):
    return lax.ppermute(block, axis, [(0, 1), (1, 0)])


def nt(left, right):
    return lax.dot_general(left, right, (((1,), (1,)), ((), ())), preferred_element_type=F32)


def tn(left, right):
    return lax.dot_general(left, right, (((0,), (0,)), ((), ())), preferred_element_type=F32)


def nn(left, right):
    return jnp.dot(left, right, preferred_element_type=F32)


def low_lanes(shape):
    return lax.broadcasted_iota(jnp.int32, shape, len(shape) - 1) < HEAD


def turn(tile):
    return pltpu.roll(tile, HEAD, 1)


def pack_heads(tile, out_ref, pair, row0):
    rolled = turn(tile)
    for quarter in range(QUARTERS):
        first = slice(quarter * 32, quarter * 32 + 16)
        second = slice(quarter * 32 + 16, quarter * 32 + 32)
        mask = low_lanes((16, 128))
        even = jnp.where(mask, tile[first], rolled[second])
        odd = jnp.where(mask, rolled[first], tile[second])
        out_ref[(2 * pair) * QUARTERS + quarter, row0 : row0 + 16, :] = even.astype(BF)
        out_ref[(2 * pair + 1) * QUARTERS + quarter, row0 : row0 + 16, :] = odd.astype(BF)


def unpack_heads(in_ref, row0, base=0):
    mask = low_lanes((16, 128))
    columns = []
    for pair in range(HEADS_DEV // 2):
        pieces = []
        for quarter in range(QUARTERS):
            even = in_ref[base + (2 * pair) * QUARTERS + quarter, row0 : row0 + 16, :].astype(F32)
            odd = in_ref[base + (2 * pair + 1) * QUARTERS + quarter, row0 : row0 + 16, :].astype(F32)
            pieces.append(jnp.where(mask, even, turn(odd)))
            pieces.append(jnp.where(mask, turn(even), odd))
        columns.append(jnp.concatenate(pieces, axis=0))
    return jnp.concatenate(columns, axis=1)


def norm_parts(rows_in):
    centre = jnp.mean(rows_in, axis=-1, keepdims=True)
    centred = rows_in - centre
    spread = jnp.mean(centred * centred, axis=-1, keepdims=True)
    rstd_rows = lax.rsqrt(spread + EPS)
    return centred * rstd_rows, rstd_rows


def norm_back(grad_rows, normal_rows, rstd_rows, gain_row):
    scaled = grad_rows * gain_row
    first_mean = jnp.mean(scaled, axis=-1, keepdims=True)
    second_mean = jnp.mean(scaled * normal_rows, axis=-1, keepdims=True)
    return rstd_rows * (scaled - first_mean - normal_rows * second_mean)


def joined(own_ref, recv_ref):
    recv = jnp.concatenate([recv_ref[ROWS:], recv_ref[:ROWS]], axis=0)
    return own_ref[...].astype(F32) + recv.astype(F32)


def column_sum(rows):
    return jnp.sum(rows[:ROWS], axis=0, keepdims=True) + jnp.sum(rows[ROWS:], axis=0, keepdims=True)


GAIN_A, GAIN_C, SHIFT_A, SHIFT_O, SHIFT_C, SHIFT_M, SCALE_A, SCALE_M = range(8)


def row_of(ref, at):
    return ref[at : at + 1, :]


def qkv_weight(ref, which):
    if which < 2:
        return ref[:, 0:32, which * HALF_W : which * HALF_W + HALF_W].reshape(MODEL, HALF_W)
    parts = [ref[:, 32:48, 0:HALF_W], ref[:, 32:48, HALF_W:MODEL]]
    return jnp.concatenate(parts, axis=1).reshape(MODEL, HALF_W)


def project_and_pack(rows, vec_ref, bias_ref, weight_ref, out_ref, rows_ref, normed_ref):
    rows_ref[...] = rows
    hat, _ = norm_parts(rows.astype(F32))
    normed = (hat * row_of(vec_ref, GAIN_A) + row_of(vec_ref, SHIFT_A)).astype(BF)
    normed_ref[...] = normed
    queries = nn(normed, qkv_weight(weight_ref, 0)) + bias_ref[0:1, :]
    keys = nn(normed, qkv_weight(weight_ref, 1))
    values = nn(normed, qkv_weight(weight_ref, 2)) + bias_ref[1:2, :]
    mask = low_lanes((BOTH, 128))
    for pair in range(HEADS_DEV // 2):
        columns = slice(pair * 128, pair * 128 + 128)
        key_tile, value_tile, query_tile = keys[:, columns], values[:, columns], queries[:, columns]
        even = jnp.where(mask, key_tile, turn(value_tile)).astype(BF)
        odd = jnp.where(mask, turn(key_tile), value_tile).astype(BF)
        for quarter in range(QUARTERS):
            out_ref[(2 * pair) * QUARTERS + quarter, 0:BOTH, :] = even
            out_ref[(2 * pair + 1) * QUARTERS + quarter, 0:BOTH, :] = odd
        pack_heads(query_tile, out_ref, pair, BOTH)


def qkv_first_kernel(own_ref, other_ref, vec_ref, bias_ref, weight_ref, out_ref, rows_ref, normed_ref):
    rows = jnp.concatenate([own_ref[...], other_ref[...]], axis=0)
    project_and_pack(rows, vec_ref, bias_ref, weight_ref, out_ref, rows_ref, normed_ref)


def qkv_next_kernel(
    middle_ref, mlp_own_ref, mlp_recv_ref, before_ref, vec_ref, bias_ref, weight_ref,
    out_ref, rows_ref, normed_ref,
):
    branch = joined(mlp_own_ref, mlp_recv_ref) + row_of(before_ref, SHIFT_M)
    rows = (middle_ref[...] + row_of(before_ref, SCALE_M) * branch).astype(BF)
    project_and_pack(rows, vec_ref, bias_ref, weight_ref, out_ref, rows_ref, normed_ref)


def qkv_block(index):
    return pl.BlockSpec((WIDE, 48, MODEL), lambda i: (0, index, 0))


def qkv_call(inputs, small, weight, block_at):
    vec, bias, _ = small
    first = len(inputs) == 2
    return pl.pallas_call(
        qkv_first_kernel if first else qkv_next_kernel,
        grid=(1,),
        in_specs=[whole(part.shape) for part in inputs]
        + [whole((8, MODEL)), whole((2, HALF_W)), qkv_block(block_at)],
        out_specs=[whole((WIDE, SEND_ROWS, 128)), whole((BOTH, MODEL)), whole((BOTH, MODEL))],
        out_shape=[
            jax.ShapeDtypeStruct((WIDE, SEND_ROWS, 128), BF),
            jax.ShapeDtypeStruct((BOTH, MODEL), BF),
            jax.ShapeDtypeStruct((BOTH, MODEL), BF),
        ],
        compiler_params=params(),
        cost_estimate=cost(5),
    )(*inputs, vec, bias, weight)


def query_tiles(packed):
    mask = low_lanes((128, 128))
    return jnp.concatenate(
        [jnp.where(mask, packed, 0.0), jnp.where(mask, turn(packed), 0.0)], axis=0
    )


def key_chunk(recv_ref, chunk):
    half, group = chunk // 4, chunk % 4
    block = recv_ref[group * 8 : group * 8 + 8, half * ROWS : half * ROWS + ROWS, :]
    return block.reshape(512, 128)


def lane_tiles(fn, block):
    return fn(fn(block[:, 0:128], block[:, 128:256]), fn(block[:, 256:384], block[:, 384:512]))


def attend_kernel(
    flag_ref, recv_ref, key_id_ref, query_id_ref, out_ref, keep_ref, lse_ref,
    score_ref, top_ref, total_ref, acc_ref,
):
    at = pl.program_id(0)
    packed = recv_ref[pl.ds(at * 8, 8), BOTH : BOTH + 16, :].astype(F32).reshape(128, 128)
    queries = (query_tiles(packed) * SCALE).astype(BF)
    query_ids = query_id_ref[0]
    top_ref[...] = jnp.full((256, 128), NEG_FILL, F32)
    total_ref[...] = jnp.zeros((256, 128), F32)
    acc_ref[...] = jnp.zeros((256, 128), F32)
    for chunk in range(CHUNKS):

        @pl.when(flag_ref[at, chunk] != 0)
        def _():
            scores = nt(queries, key_chunk(recv_ref, chunk))
            scores = jnp.where(query_ids == key_id_ref[chunk], scores, NEG_FILL)
            score_ref[chunk] = scores
            top_ref[...] = jnp.maximum(top_ref[...], lane_tiles(jnp.maximum, scores))

    top = jnp.max(top_ref[...], axis=1, keepdims=True)
    for chunk in range(CHUNKS):

        @pl.when(flag_ref[at, chunk] != 0)
        def _():
            expo = jnp.exp(score_ref[chunk] - top)
            total_ref[...] += lane_tiles(jnp.add, expo)
            acc_ref[...] += nn(expo.astype(BF), key_chunk(recv_ref, chunk))

    total = jnp.sum(total_ref[...], axis=1, keepdims=True)
    mixture = acc_ref[...] / total
    lse_ref[...] = top + jnp.log(total)
    mask = low_lanes((128, 128))
    joined = jnp.where(mask, turn(mixture[:128]), mixture[128:]).reshape(8, 16, 128)
    keep_ref[...] = joined
    out_ref[0] = joined.astype(BF)
    out_ref[1] = joined.astype(BF)


def attend_call(flags, recv, key_ids, query_ids):
    return pl.pallas_call(
        attend_kernel,
        grid_spec=pltpu.PrefetchScalarGridSpec(
            num_scalar_prefetch=1,
            grid=(BLOCKS_Q,),
            in_specs=[
                pl.BlockSpec((WIDE, SEND_ROWS, 128), lambda i, f: (0, 0, 0)),
                pl.BlockSpec((CHUNKS, 1, 512), lambda i, f: (0, 0, 0)),
                pl.BlockSpec((1, 256, 1), lambda i, f: (i, 0, 0)),
            ],
            out_specs=[
                pl.BlockSpec((2, 8, 16, 128), lambda i, f: (0, i, 0, 0)),
                pl.BlockSpec((8, 16, 128), lambda i, f: (i, 0, 0)),
                pl.BlockSpec((256, 1), lambda i, f: (i, 0)),
            ],
            scratch_shapes=[
                pltpu.VMEM((CHUNKS, 256, 512), F32),
                pltpu.VMEM((256, 128), F32),
                pltpu.VMEM((256, 128), F32),
                pltpu.VMEM((256, 128), F32),
            ],
        ),
        out_shape=[
            jax.ShapeDtypeStruct((2, WIDE, 16, 128), BF),
            jax.ShapeDtypeStruct((WIDE, 16, 128), F32),
            jax.ShapeDtypeStruct((1024, 1), F32),
        ],
        compiler_params=params(),
        cost_estimate=cost(12),
    )(flags, recv, key_ids, query_ids)


def attend_back_kernel(
    flag_ref, recv_ref, grad_ref, keep_ref, lse_ref, key_id_ref, query_id_ref, out_ref,
    key_grad_ref, query_grad_ref,
):
    at = pl.program_id(0)

    @pl.when(at == 0)
    def _():
        key_grad_ref[...] = jnp.zeros((WIDE, BOTH, 128), F32)

    mask = low_lanes((128, 128))
    packed = recv_ref[pl.ds(at * 8, 8), BOTH : BOTH + 16, :].astype(F32).reshape(128, 128)
    queries = (query_tiles(packed) * SCALE).astype(BF)
    grads = grad_ref[...].astype(F32).reshape(128, 128)
    grad_tile = jnp.concatenate(
        [jnp.where(mask, 0.0, turn(grads)), jnp.where(mask, 0.0, grads)], axis=0
    ).astype(BF)
    product = grads * keep_ref[...].reshape(128, 128)
    delta = jnp.concatenate(
        [
            jnp.sum(jnp.where(mask, product, 0.0), axis=1, keepdims=True),
            jnp.sum(jnp.where(mask, 0.0, product), axis=1, keepdims=True),
        ],
        axis=0,
    )
    lse = lse_ref[...]
    query_ids = query_id_ref[0]
    both = jnp.concatenate([queries, grad_tile], axis=0)
    query_grad_ref[...] = jnp.zeros((256, 128), F32)
    for chunk in range(CHUNKS):

        @pl.when(flag_ref[at, chunk] != 0)
        def _():
            half, group = chunk // 4, chunk % 4
            keys = key_chunk(recv_ref, chunk)
            scores = nt(queries, keys)
            scores = jnp.where(query_ids == key_id_ref[chunk], scores, NEG_FILL)
            chance = jnp.exp(scores - lse)
            grad_scores = (chance * (nt(grad_tile, keys) - delta)).astype(BF)
            query_grad_ref[...] += nn(grad_scores, keys)
            stacked = jnp.concatenate([grad_scores, chance.astype(BF)], axis=0)
            key_grad_ref[group * 8 : group * 8 + 8, half * ROWS : half * ROWS + ROWS, :] += tn(
                stacked, both
            ).reshape(8, ROWS, 128)

    query_grad = query_grad_ref[...] * SCALE
    joined = jnp.where(mask, query_grad[:128], turn(query_grad[128:]))
    out_ref[pl.ds(at * 8, 8), BOTH : BOTH + 16, :] = joined.astype(BF).reshape(8, 16, 128)

    @pl.when(at == BLOCKS_Q - 1)
    def _():
        out_ref[:, 0:BOTH, :] = key_grad_ref[...].astype(BF)


def attend_back_call(flags, recv, grads, keep, lse, key_ids, query_ids):
    return pl.pallas_call(
        attend_back_kernel,
        grid_spec=pltpu.PrefetchScalarGridSpec(
            num_scalar_prefetch=1,
            grid=(BLOCKS_Q,),
            in_specs=[
                pl.BlockSpec((WIDE, SEND_ROWS, 128), lambda i, f: (0, 0, 0)),
                pl.BlockSpec((8, 16, 128), lambda i, f: (i, 0, 0)),
                pl.BlockSpec((8, 16, 128), lambda i, f: (i, 0, 0)),
                pl.BlockSpec((256, 1), lambda i, f: (i, 0)),
                pl.BlockSpec((CHUNKS, 1, 512), lambda i, f: (0, 0, 0)),
                pl.BlockSpec((1, 256, 1), lambda i, f: (i, 0, 0)),
            ],
            out_specs=pl.BlockSpec((WIDE, SEND_ROWS, 128), lambda i, f: (0, 0, 0)),
            scratch_shapes=[
                pltpu.VMEM((WIDE, BOTH, 128), F32),
                pltpu.VMEM((256, 128), F32),
            ],
        ),
        out_shape=jax.ShapeDtypeStruct((WIDE, SEND_ROWS, 128), BF),
        compiler_params=params(),
        cost_estimate=cost(16),
    )(flags, recv, grads, keep, lse, key_ids, query_ids)


KEPT_C, KEPT_A, KEPT_MIX = slice(2048, 3072), slice(3072, 4096), slice(4096, 4608)
KEPT_WIDTH = 4608
TALL = BOTH + 16


def mlp_kernel(
    place_ref, rows_ref, normed_ref, recv_ref, vec_ref, bias_ref, out_weight_ref, one_ref, two_ref,
    branch_ref, middle_ref, pre_ref, kept_ref, out_ref, acc_ref,
):
    at = pl.program_id(0)

    @pl.when(at == 0)
    def _():
        tensor = place_ref[0]
        own = unpack_heads(recv_ref, 0, tensor * WIDE).astype(BF)
        partner = unpack_heads(recv_ref, 0, (1 - tensor) * WIDE).astype(BF)
        partner = jnp.concatenate([partner[ROWS:], partner[:ROWS]], axis=0)
        kept_ref[:, KEPT_A] = normed_ref[...]
        kept_ref[:, KEPT_MIX] = own
        proj = nn(own, out_weight_ref[:, 0:16, :].reshape(HALF_W, MODEL)) + nn(
            partner, out_weight_ref[:, 16:32, :].reshape(HALF_W, MODEL)
        )
        branch = proj + row_of(vec_ref, SHIFT_O)
        branch_ref[...] = branch
        middle = rows_ref[...].astype(F32) + row_of(vec_ref, SCALE_A) * branch
        middle_ref[...] = middle
        hat, _ = norm_parts(middle)
        kept_ref[:, KEPT_C] = (hat * row_of(vec_ref, GAIN_C) + row_of(vec_ref, SHIFT_C)).astype(BF)

    pre = nn(kept_ref[:, KEPT_C], one_ref[...].reshape(MODEL, MODEL)) + bias_ref[...]
    act = (0.5 * pre * (1.0 + lax.erf(pre * ROOT_HALF))).astype(BF)
    pre_ref[...] = pre
    part = nn(act, two_ref[...].reshape(MODEL, MODEL))

    @pl.when(at == 0)
    def _():
        kept_ref[:, 0:MODEL] = act
        acc_ref[...] = part

    @pl.when(at == 1)
    def _():
        kept_ref[:, MODEL:HIDDEN] = act
        out_ref[...] = (acc_ref[...] + part).astype(BF)


def mlp_call(place, rows, normed, recv, small, weights):
    vec, _, bias = small
    return pl.pallas_call(
        mlp_kernel,
        grid=(2,),
        in_specs=[
            pl.BlockSpec(memory_space=pltpu.SMEM),
            whole((BOTH, MODEL)),
            whole((BOTH, MODEL)),
            whole((2 * WIDE, 16, 128)),
            whole((8, MODEL)),
            pl.BlockSpec((1, MODEL), lambda j: (0, j)),
            pl.BlockSpec((WIDE, 32, MODEL), lambda j: (0, 4, 0)),
            pl.BlockSpec((WIDE, 32, MODEL), lambda j: (0, 2 + j, 0)),
            pl.BlockSpec((16, 64, MODEL), lambda j: (j, 0, 0)),
        ],
        out_specs=[
            whole((BOTH, MODEL)),
            whole((BOTH, MODEL)),
            pl.BlockSpec((BOTH, MODEL), lambda j: (0, j)),
            whole((BOTH, KEPT_WIDTH)),
            whole((BOTH, MODEL)),
        ],
        out_shape=[
            jax.ShapeDtypeStruct((BOTH, MODEL), F32),
            jax.ShapeDtypeStruct((BOTH, MODEL), F32),
            jax.ShapeDtypeStruct((BOTH, HIDDEN), F32),
            jax.ShapeDtypeStruct((BOTH, KEPT_WIDTH), BF),
            jax.ShapeDtypeStruct((BOTH, MODEL), BF),
        ],
        scratch_shapes=[pltpu.VMEM((BOTH, MODEL), F32)],
        compiler_params=params(),
        cost_estimate=cost(8),
    )(place, rows, normed, recv, vec, bias, weights, weights, weights)


def mlp_back_steps(
    grad, vec_ref, pre_ref, one_ref, two_ref, grad_ref, back_ref, out_ref, acc_ref, sums_ref,
):
    at = pl.program_id(0)

    @pl.when(at == 0)
    def _():
        rows = grad()
        grad_ref[...] = rows
        rows = rows.astype(F32)
        scaled = rows * row_of(vec_ref, SCALE_M)
        back_ref[0:BOTH, 2048:3072] = scaled.astype(BF)
        sums_ref[...] = jnp.zeros((16, MODEL), F32)
        sums_ref[0:1, :] = column_sum(scaled)

    pre = pre_ref[...]
    slope = 0.5 * (1.0 + lax.erf(pre * ROOT_HALF)) + pre * jnp.exp(-0.5 * pre * pre) * INV_ROOT_TAU
    grad_pre = (nt(back_ref[0:BOTH, 2048:3072], two_ref[...].reshape(MODEL, MODEL)) * slope).astype(BF)
    part = nt(grad_pre, one_ref[...].reshape(MODEL, MODEL))
    bias_sum = jnp.sum(grad_pre.astype(F32), axis=0, keepdims=True)

    @pl.when(at == 0)
    def _():
        back_ref[0:BOTH, 0:MODEL] = grad_pre
        acc_ref[...] = part
        sums_ref[1:2, :] = bias_sum

    @pl.when(at == 1)
    def _():
        back_ref[0:BOTH, MODEL:HIDDEN] = grad_pre
        out_ref[...] = (acc_ref[...] + part).astype(BF)
        sums_ref[2:3, :] = bias_sum
        back_ref[BOTH:TALL, 0:MODEL] = sums_ref[...].astype(BF)
        back_ref[BOTH:TALL, MODEL:3072] = jnp.zeros((16, 2048), BF)


def mlp_back_first_kernel(own_ref, other_ref, *refs):
    mlp_back_steps(lambda: jnp.concatenate([own_ref[...], other_ref[...]], axis=0), *refs)


def mlp_back_next_kernel(
    middle_grad_ref, part_own_ref, part_recv_ref, rows_ref, after_ref, pack_ref, *refs
):
    *refs, input_grad_ref, acc_ref, sums_ref = refs

    def grad():
        hat, rstd = norm_parts(rows_ref[...].astype(F32))
        grad_norm = joined(part_own_ref, part_recv_ref)
        total = middle_grad_ref[...] + norm_back(grad_norm, hat, rstd, row_of(after_ref, GAIN_A))
        input_grad_ref[...] = total[:ROWS]
        return total.astype(BF)

    mlp_back_steps(grad, *refs, acc_ref, sums_ref)


def mlp_back_call(inputs, small, pre, weights):
    first = len(inputs) == 2
    extra = [] if first else [(ROWS, MODEL)]
    return pl.pallas_call(
        mlp_back_first_kernel if first else mlp_back_next_kernel,
        grid=(2,),
        in_specs=[ANYWHERE if part.ndim == 3 else whole(part.shape) for part in inputs]
        + [
            whole((8, MODEL)),
            pl.BlockSpec((BOTH, MODEL), lambda j: (0, j)),
            pl.BlockSpec((WIDE, 32, MODEL), lambda j: (0, 2 + j, 0)),
            pl.BlockSpec((16, 64, MODEL), lambda j: (j, 0, 0)),
        ],
        out_specs=[whole((BOTH, MODEL)), whole((TALL, 3072)), whole((BOTH, MODEL))]
        + [whole(shape) for shape in extra],
        out_shape=[
            jax.ShapeDtypeStruct((BOTH, MODEL), BF),
            jax.ShapeDtypeStruct((TALL, 3072), BF),
            jax.ShapeDtypeStruct((BOTH, MODEL), BF),
        ]
        + [jax.ShapeDtypeStruct(shape, F32) for shape in extra],
        scratch_shapes=[pltpu.VMEM((BOTH, MODEL), F32), pltpu.VMEM((16, MODEL), F32)],
        compiler_params=params(),
        cost_estimate=cost(8),
    )(*inputs, small[0], pre, weights, weights)


PACK_ROWS = 240
CHIPS = WIDE // 2


def store_mine(place_ref, value, grad_ref, pairs, rows, columns):
    value = value.reshape(value.shape[0] // 2, 2, *value.shape[1:])
    for core in range(2):

        @pl.when(place_ref[1] == core)
        def _():
            grad_ref[pairs, rows, columns] = value[:, core].astype(BF)


def both_cores(own_ref, other_ref):
    return jnp.concatenate([own_ref[0:BOTH], other_ref[0:BOTH]], axis=0)


def twice(spec):
    return [spec, spec]


def mlp_weight_kernel(place_ref, *refs):
    act, normed, low, grad_pre = (both_cores(*refs[at : at + 2]) for at in range(0, 8, 2))
    grad_ref = refs[-1]
    grad_two = tn(act, low).reshape(16, 64, MODEL)
    grad_one = tn(normed, grad_pre).reshape(WIDE, 32, MODEL)
    for at in range(2):

        @pl.when(pl.program_id(0) == at)
        def _():
            store_mine(
                place_ref, grad_two, grad_ref, slice(8 * at, 8 * at + 8), slice(0, 64), EVERY
            )
            rows = slice(64 + 32 * at, 96 + 32 * at)
            store_mine(place_ref, grad_one, grad_ref, EVERY, rows, EVERY)


def mlp_weight_call(place, kept, back, part_recv, pack=None):
    rows, extra, aliases = 128, [part_recv], {}
    if pack is not None:
        rows, extra, aliases = PACK_ROWS, [pack], {9: 0}
    return pl.pallas_call(
        mlp_weight_kernel,
        grid=(2,),
        in_specs=[SCALARS]
        + twice(pl.BlockSpec((BOTH, MODEL), lambda j: (0, j)))
        + twice(pl.BlockSpec((BOTH, MODEL), lambda j: (0, 2)))
        + twice(pl.BlockSpec((BOTH, MODEL), lambda j: (0, 2)))
        + twice(pl.BlockSpec((BOTH, MODEL), lambda j: (0, j)))
        + [ANYWHERE] * len(extra),
        out_specs=pl.BlockSpec((CHIPS, 128, MODEL), lambda j: (0, 0, 0)),
        out_shape=jax.ShapeDtypeStruct((CHIPS, rows, MODEL), BF),
        input_output_aliases=aliases,
        compiler_params=params(),
        cost_estimate=cost(7),
    )(place, *kept, *kept, *back, *back, *extra)


def out_back_kernel(
    grad_ref, part_own_ref, part_recv_ref, middle_ref, branch_ref, vec_ref, weight_ref, pack_ref,
     middle_grad_ref, send_ref, low_ref, sums_ref,
):
    hat, rstd = norm_parts(middle_ref[...])
    grad_norm = joined(part_own_ref, part_recv_ref)
    total = grad_ref[...].astype(F32) + norm_back(grad_norm, hat, rstd, row_of(vec_ref, GAIN_C))
    middle_grad_ref[...] = total
    scaled = total * row_of(vec_ref, SCALE_A)
    rows = scaled.astype(BF)
    low_ref[0:BOTH, :] = rows
    grad_mix = nt(rows, weight_ref[...].reshape(HALF_W, MODEL))
    for pair in range(HEADS_DEV // 2):
        pack_heads(grad_mix[:, pair * 128 : pair * 128 + 128], send_ref, pair, 0)
    sums_ref[...] = jnp.zeros((16, MODEL), F32)
    sums_ref[0:1, :] = column_sum(grad_norm * hat)
    sums_ref[1:2, :] = column_sum(grad_norm)
    sums_ref[2:3, :] = column_sum(scaled)
    sums_ref[3:4, :] = column_sum(total * branch_ref[...])
    low_ref[BOTH:TALL, :] = sums_ref[...].astype(BF)


def out_back_call(grad, part_own, part_recv, middle, branch, small, weights, pack):
    return pl.pallas_call(
        out_back_kernel,
        grid=(1,),
        in_specs=[whole((BOTH, MODEL))] * 5
        + [whole((8, MODEL)), pl.BlockSpec((WIDE, 16, MODEL), lambda i: (0, 8, 0)), ANYWHERE],
        out_specs=[whole((BOTH, MODEL)), whole((WIDE, 16, 128)), whole((TALL, MODEL))],
        out_shape=[
            jax.ShapeDtypeStruct((BOTH, MODEL), F32),
            jax.ShapeDtypeStruct((WIDE, 16, 128), BF),
            jax.ShapeDtypeStruct((TALL, MODEL), BF),
        ],
        scratch_shapes=[pltpu.VMEM((16, MODEL), F32)],
        compiler_params=params(),
        cost_estimate=cost(4),
    )(grad, part_own, part_recv, middle, branch, small[0], weights, pack)


def store_out_grads(place_ref, refs, grad_ref, rows):
    grad = tn(both_cores(*refs[0:2]), both_cores(*refs[2:4])).reshape(WIDE, 16, MODEL)
    store_mine(place_ref, grad, grad_ref, EVERY, rows, EVERY)


def out_weight_kernel(place_ref, *refs):
    store_out_grads(place_ref, refs, refs[-1], EVERY)


def out_weight_last_kernel(place_ref, *refs):
    *sums_refs, before_ref, _, grad_ref = refs[4:]
    store_out_grads(place_ref, refs, grad_ref, slice(0, 16))
    parts = [
        own[0:count, :].astype(F32) + other[0:count, :].astype(F32)
        for own, other, count in zip(sums_refs[0::2], sums_refs[1::2], (8, 8, 4, 4, 4))
    ]
    rows = jnp.concatenate(parts + [before_ref[0:4, :].astype(F32)], axis=0).astype(BF)
    grad_ref[:, 16:48, :] = jnp.broadcast_to(rows[None], (CHIPS, 32, MODEL))


OUT_WEIGHT_SPECS = (
    [SCALARS]
    + twice(pl.BlockSpec((BOTH, HALF_W), lambda i: (0, 8)))
    + twice(pl.BlockSpec((BOTH, MODEL), lambda i: (0, 0)))
)
SUMS_SPEC = pl.BlockSpec((16, MODEL), lambda i: (8, 0))


def out_weight_call(place, kept, low):
    return pl.pallas_call(
        out_weight_kernel,
        grid=(1,),
        in_specs=OUT_WEIGHT_SPECS,
        out_specs=pl.BlockSpec((CHIPS, 16, MODEL), lambda i: (0, 8, 0)),
        out_shape=jax.ShapeDtypeStruct((CHIPS, PACK_ROWS, MODEL), BF),
        compiler_params=params(),
        cost_estimate=cost(2),
    )(place, *kept, *low)


def out_weight_last_call(place, kept, low, sums, before, pack):
    flat = [array for pair in sums for array in pair]
    return pl.pallas_call(
        out_weight_last_kernel,
        grid=(1,),
        in_specs=OUT_WEIGHT_SPECS + [SUMS_SPEC] * len(flat) + [whole((16, MODEL)), ANYWHERE],
        out_specs=pl.BlockSpec((CHIPS, 48, MODEL), lambda i: (0, 4, 0)),
        out_shape=jax.ShapeDtypeStruct((CHIPS, PACK_ROWS, MODEL), BF),
        input_output_aliases={6 + len(flat): 0},
        compiler_params=params(),
        cost_estimate=cost(3),
    )(place, *kept, *low, *flat, before, pack)


def qkv_back_kernel(
    recv_ref, rows_ref, grad_ref, mlp_own_ref, mlp_recv_ref, vec_ref, weight_ref,
    part_ref, grads_ref, sums_ref,
):
    grad_q = unpack_heads(recv_ref, BOTH).astype(BF)
    mask = low_lanes((BOTH, 128))
    key_columns, value_columns = [], []
    for pair in range(HEADS_DEV // 2):
        sums = []
        for head in (2 * pair, 2 * pair + 1):
            total = recv_ref[head * QUARTERS, 0:BOTH, :].astype(F32)
            for quarter in range(1, QUARTERS):
                total = total + recv_ref[head * QUARTERS + quarter, 0:BOTH, :].astype(F32)
            sums.append(total)
        key_columns.append(jnp.where(mask, sums[0], turn(sums[1])))
        value_columns.append(jnp.where(mask, turn(sums[0]), sums[1]))
    grad_k = jnp.concatenate(key_columns, axis=1).astype(BF)
    grad_v = jnp.concatenate(value_columns, axis=1).astype(BF)
    grads_ref[0:BOTH, 0:HALF_W] = grad_q
    grads_ref[0:BOTH, HALF_W:MODEL] = grad_k
    grads_ref[0:BOTH, MODEL : MODEL + HALF_W] = grad_v
    result = (
        nt(grad_q, qkv_weight(weight_ref, 0))
        + nt(grad_k, qkv_weight(weight_ref, 1))
        + nt(grad_v, qkv_weight(weight_ref, 2))
    )
    part_ref[...] = result.astype(BF)
    hat, _ = norm_parts(rows_ref[...].astype(F32))
    sums_ref[...] = jnp.zeros((16, MODEL), F32)
    sums_ref[0:1, :] = column_sum(result * hat)
    sums_ref[1:2, :] = column_sum(result)
    sums_ref[2:3, 0:HALF_W] = column_sum(grad_q.astype(F32))
    sums_ref[2:3, HALF_W:MODEL] = column_sum(grad_v.astype(F32))
    branch = joined(mlp_own_ref, mlp_recv_ref) + row_of(vec_ref, SHIFT_M)
    sums_ref[3:4, :] = column_sum(grad_ref[...].astype(F32) * branch)
    grads_ref[BOTH:TALL, 0:MODEL] = sums_ref[...].astype(BF)
    grads_ref[BOTH:TALL, MODEL : MODEL + HALF_W] = jnp.zeros((16, HALF_W), BF)


def qkv_back_call(recv, rows, grad, mlp, mlp_recv, small, weight, block_at):
    return pl.pallas_call(
        qkv_back_kernel,
        grid=(1,),
        in_specs=[
            whole((WIDE, SEND_ROWS, 128)),
            whole((BOTH, MODEL)),
            whole((BOTH, MODEL)),
            whole((BOTH, MODEL)),
            whole((BOTH, MODEL)),
            whole((8, MODEL)),
            qkv_block(block_at),
        ],
        out_specs=[whole((BOTH, MODEL)), whole((TALL, 3 * HALF_W))],
        out_shape=[
            jax.ShapeDtypeStruct((BOTH, MODEL), BF),
            jax.ShapeDtypeStruct((TALL, 3 * HALF_W), BF),
        ],
        scratch_shapes=[pltpu.VMEM((16, MODEL), F32)],
        compiler_params=params(),
        cost_estimate=cost(5),
    )(recv, rows, grad, mlp, mlp_recv, small[0], weight)


def store_qkv_grads(place_ref, refs, grad_ref):
    rows = both_cores(*refs[0:2])

    def part(which):
        columns = slice(which * HALF_W, which * HALF_W + HALF_W)
        grads = jnp.concatenate([ref[0:BOTH, columns] for ref in refs[2:4]], axis=0)
        return tn(rows, grads).reshape(WIDE, 32, HALF_W)

    low, high = slice(0, HALF_W), slice(HALF_W, MODEL)
    store_mine(place_ref, part(0), grad_ref, EVERY, slice(0, 32), low)
    store_mine(place_ref, part(1), grad_ref, EVERY, slice(0, 32), high)
    values = part(2)
    store_mine(place_ref, values[:, 0:16], grad_ref, EVERY, slice(32, 48), low)
    store_mine(place_ref, values[:, 16:32], grad_ref, EVERY, slice(32, 48), high)


def qkv_weight_kernel(place_ref, *refs):
    store_qkv_grads(place_ref, refs, refs[-1])


def qkv_weight_last_kernel(place_ref, *refs):
    grad_ref = refs[-1]
    store_qkv_grads(place_ref, refs, grad_ref)
    rows = sum(ref[BOTH : BOTH + 8, 0:MODEL].astype(F32) for ref in refs[2:4]).astype(BF)
    grad_ref[:, 48:56, :] = jnp.broadcast_to(rows[None], (CHIPS, 8, MODEL))


QKV_WEIGHT_SPECS = (
    [SCALARS]
    + twice(pl.BlockSpec((BOTH, MODEL), lambda i: (0, 3)))
    + twice(whole((TALL, 3 * HALF_W)))
)


def qkv_weight_call(place, kept, grads, pack):
    return pl.pallas_call(
        qkv_weight_kernel,
        grid=(1,),
        in_specs=QKV_WEIGHT_SPECS + [ANYWHERE],
        out_specs=qkv_chips(3),
        out_shape=jax.ShapeDtypeStruct((CHIPS, PACK_ROWS, MODEL), BF),
        input_output_aliases={5: 0},
        compiler_params=params(),
        cost_estimate=cost(4),
    )(place, *kept, *grads, pack)


def qkv_chips(index):
    return pl.BlockSpec((CHIPS, 48, MODEL), lambda i: (0, index, 0))


def qkv_weight_last_call(place, kept, grads):
    return pl.pallas_call(
        qkv_weight_last_kernel,
        grid=(1,),
        in_specs=QKV_WEIGHT_SPECS,
        out_specs=whole((CHIPS, 56, MODEL)),
        out_shape=jax.ShapeDtypeStruct((CHIPS, 56, MODEL), BF),
        compiler_params=params(),
        cost_estimate=cost(4),
    )(place, *kept, *grads)


def with_core(block):
    return block, lax.ppermute(block, "wide", [(i, i ^ 1) for i in range(WIDE)])


def all_to_all(block):
    return lax.all_to_all(block, "wide", 0, 0, tiled=True)


def layer_forward(place, inputs, ids, qkv, rest, small):
    flags, key_ids, query_ids = ids
    sent, rows, normed_a = qkv_call(inputs, small, *qkv)
    recv = all_to_all(sent)
    mix_sent, mix_keep, lse = attend_call(flags, recv, key_ids, query_ids)
    mix_recv = lax.all_to_all(
        mix_sent.reshape(2 * WIDE, 16, 128), ("tensor", "wide"), 0, 0, tiled=True
    )
    branch, middle, pre, wide_kept, mlp = mlp_call(place, rows, normed_a, mix_recv, small, rest)
    mlp_recv = swap(mlp, "tensor")
    return dict(
        rows=rows, recv=recv, keep=mix_keep, lse=lse, branch=branch, middle=middle, pre=pre,
        mlp=mlp, mlp_recv=mlp_recv, for_weights=with_core(wide_kept),
    )


def layer_backward(place, inputs, kept, ids, qkv, rest, small, pack=None):
    flags, key_ids, query_ids = ids
    grad, mlp_back, part, *input_grad = mlp_back_call(
        inputs, small, kept["pre"], rest
    )
    mlp_pair = with_core(mlp_back)
    part_recv = swap(part, "tensor")
    pack = mlp_weight_call(place, kept["for_weights"], mlp_pair, part_recv, pack)
    middle_grad, mix_grad, low_a = out_back_call(
        grad, part, part_recv, kept["middle"], kept["branch"], small, rest, pack
    )
    back = attend_back_call(
        flags, kept["recv"], all_to_all(mix_grad), kept["keep"], kept["lse"], key_ids, query_ids
    )
    qkv_part, qkv_grads = qkv_back_call(
        all_to_all(back), kept["rows"], grad, kept["mlp"], kept["mlp_recv"], small, *qkv
    )
    carried = (middle_grad, qkv_part, swap(qkv_part, "tensor"), kept["rows"])
    for_weights = mlp_pair, with_core(low_a), with_core(qkv_grads)
    return carried, pack, for_weights, input_grad


def body(
    x_in, out_cot, image_ids, w_qkv, w_out, w_fc1, w_fc2, gains, shifts, layer_scales, qv_bias, fc1_bias
):
    section = lax.axis_index("section")
    tensor = lax.axis_index("tensor")
    wide = lax.axis_index("wide")
    is_first = section == 0

    def one(array):
        return lax.dynamic_index_in_dim(array, section, 0, keepdims=False)

    place = jnp.stack([tensor, lax.rem(wide, 2)]).astype(jnp.int32)

    qkv = w_qkv[0]
    small_rows = jnp.concatenate(
        [
            jnp.pad(jnp.concatenate([gains[0], shifts[0], layer_scales[0]], axis=0), ((0, 0), (0, 32))),
            jnp.pad(qv_bias[0], ((0, 0), (0, 48))),
            fc1_bias,
        ],
        axis=0,
    )
    pack_a = jnp.concatenate(
        [
            jnp.concatenate([qkv[:, 0], qkv[:, 1]], axis=1),
            jnp.concatenate([qkv[0:16, 2], qkv[16:32, 2]], axis=1),
            jnp.pad(small_rows, ((0, 5), (0, MODEL - 64))),
        ],
        axis=0,
    )
    own_rows, own_cot = one(x_in), one(out_cot)
    partner = swap(jnp.concatenate([own_rows, own_cot, w_out[0]], axis=0), "tensor")
    other_rows, other_cot, other_out = partner[:ROWS], partner[ROWS:BOTH], partner[BOTH:]
    pack_b = jnp.concatenate(
        [w_fc2[0], w_fc1[0][:, :MODEL], w_fc1[0][:, MODEL:], w_out[0], other_out], axis=0
    )
    other_a = swap(pack_a, "section")
    other_b = swap(pack_b, "section")

    def gather(block):
        return lax.all_gather(block, "wide", axis=0, tiled=False)

    def joined_a(first, second):
        vectors = jnp.concatenate([first[48:64, :HALF_W], second[48:64, :HALF_W]], axis=1)
        return jnp.concatenate([first[:48], second[:48], vectors], axis=0)

    attn_both = gather(jnp.where(is_first, joined_a(pack_a, other_a), joined_a(other_a, pack_a)))

    first_here = is_first & (attn_both[0, 111, MODEL - 1] == 0)
    rest_first = gather(jnp.where(first_here, pack_b, other_b))

    def rest_second(rows):
        return gather(jnp.concatenate([jnp.where(is_first, other_b, pack_b), rows], axis=0))

    def small_of(layer):
        block = attn_both[:, 96:107, layer * HALF_W : layer * HALF_W + 64].astype(F32)
        vec = jnp.transpose(block[:, 0:8, 0:32], (1, 0, 2)).reshape(8, MODEL)
        bias = jnp.transpose(block[:, 8:10, 0:16], (1, 0, 2)).reshape(2, HALF_W)
        return vec, bias, block[:, 10].reshape(1, HIDDEN)

    small = (small_of(0), small_of(1))

    id_grid = one(image_ids).reshape(2, WIDE, ROWS)
    sorted_ids = jnp.where(tensor == 0, id_grid, id_grid[::-1])
    key_ids = sorted_ids.reshape(CHUNKS, 1, 512)
    quarter = lax.rem(wide, QUARTERS)
    half_ids = lax.dynamic_index_in_dim(sorted_ids, quarter // 2, 0, keepdims=False)
    quarter_ids = lax.dynamic_slice_in_dim(half_ids, lax.rem(quarter, 2) * 32, 32, 1)
    query_ids = jnp.transpose(quarter_ids.reshape(BLOCKS_Q, 8, 2, 16), (0, 2, 1, 3)).reshape(
        BLOCKS_Q, 256, 1
    )
    key_low, key_high = jnp.min(key_ids[:, 0], axis=1), jnp.max(key_ids[:, 0], axis=1)
    query_low, query_high = jnp.min(query_ids[..., 0], axis=1), jnp.max(query_ids[..., 0], axis=1)
    flags = (
        (query_low[:, None] <= key_high[None]) & (query_high[:, None] >= key_low[None])
    ).astype(jnp.int32)
    ids = (flags, key_ids, query_ids)

    qkv_parts = ((attn_both, 0), (attn_both, 1))
    kept0 = layer_forward(place, (own_rows, other_rows), ids, qkv_parts[0], rest_first, small[0])
    rest = (rest_first, rest_second(kept0["mlp"][:16]))
    kept1 = layer_forward(
        place,
        (kept0["middle"], kept0["mlp"], kept0["mlp_recv"], small[0][0]),
        ids, qkv_parts[1], rest[1], small[1],
    )
    branch1 = kept1["mlp"][:ROWS].astype(F32) + kept1["mlp_recv"][ROWS:].astype(F32)
    out1 = (
        kept1["middle"][:ROWS]
        + small[1][0][SCALE_M] * (branch1 + small[1][0][SHIFT_M])
    ).astype(BF)
    out0 = kept1["rows"][:ROWS]

    same_core = [list(range(core, WIDE, 2)) for core in range(2)]

    def over_chips(pack):
        return lax.psum_scatter(
            pack.reshape(CHIPS * pack.shape[1], MODEL),
            "wide", scatter_dimension=0, axis_index_groups=same_core, tiled=True,
        )

    carried1, pack1, back1, _ = layer_backward(
        place, (own_cot, other_cot), kept1, ids, qkv_parts[1], rest[1], small[1]
    )
    kept_pair0, kept_pair1 = kept0["for_weights"], kept1["for_weights"]
    mlp_back1, low1, grads1 = back1
    sum_mlp1 = over_chips(pack1)
    pack = out_weight_call(place, kept_pair1, low1)
    pack = qkv_weight_call(place, kept_pair1, grads1, pack)

    carried0, pack, back0, (grad_x1,) = layer_backward(
        place, carried1 + (small[1][0], pack), kept0, ids, qkv_parts[0], rest[0], small[0], pack
    )
    mlp_back0, low0, grads0 = back0
    pack = out_weight_last_call(
        place, kept_pair0, low0, (low1, low0, grads1, mlp_back1, mlp_back0), sum_mlp1, pack
    )
    sum_mid = over_chips(pack)
    last_recv = lax.all_to_all(
        qkv_weight_last_call(place, kept_pair0, grads0),
        "wide", 0, 0, axis_index_groups=same_core, tiled=True,
    )
    sum_last = jnp.sum(last_recv.astype(F32), axis=0)

    middle_grad0, part0, part_recv0, _ = carried0
    hat0, rstd0 = norm_parts(own_rows.astype(F32))
    grad_norm0 = part0[:ROWS].astype(F32) + part_recv0[ROWS:].astype(F32)
    grad_x0 = middle_grad0[:ROWS] + norm_back(grad_norm0, hat0, rstd0, small[0][0][GAIN_A])

    def lanes(rows, width):
        return lax.dynamic_slice_in_dim(rows, wide * width, width, rows.ndim - 1)

    mid0 = jnp.concatenate([sum_mid[0:128], sum_mid[192:208]], axis=0)
    mid1 = jnp.concatenate([sum_mlp1, sum_mid[128:144]], axis=0)
    mid_total = jnp.where(is_first, mid0, mid1).astype(F32) + swap(
        jnp.where(is_first, mid1, mid0), "section"
    ).astype(F32)
    late0 = jnp.concatenate([sum_last[0:52].astype(BF), sum_mid[232:236], sum_mid[216:224]], axis=0)
    late1 = jnp.concatenate(
        [sum_mid[144:192], sum_mid[224:228], sum_mid[228:232], sum_mid[208:216]], axis=0
    )
    late_own = jnp.where(is_first, late0, late1)
    late_away = jnp.where(is_first, late1, late0)
    late_total = late_own.astype(F32) + swap(late_away, "section").astype(F32)
    across = lax.ppermute(late_away[48:50], ("section", "tensor"), [(0, 3), (3, 0), (1, 2), (2, 1)])
    heads_total = late_total[48:50] + (
        swap(late_own[48:50], "tensor").astype(F32) + across.astype(F32)
    )
    mlp_total, out_total, qkv_total = mid_total[0:128], mid_total[128:144], late_total[0:48]
    norms = lanes(jnp.concatenate([heads_total, late_total[52:53], late_total[56:60], late_total[51:52]], axis=0), 32)
    g_gains = jnp.stack([norms[0], norms[3]])
    g_shifts = jnp.stack([norms[1], norms[5], norms[4], norms[2]])
    g_scales = jnp.stack([norms[6], norms[7]])
    g_qv = lanes(late_total[50].reshape(2, HALF_W), 16)
    g_fc1_bias = lanes(late_total[53:55].reshape(HIDDEN), 64)
    g_fc2 = mlp_total[0:64]
    g_fc1 = jnp.concatenate([mlp_total[64:96], mlp_total[96:128]], axis=1)
    pairs = qkv_total[0:32]
    value_grad = jnp.concatenate([qkv_total[32:48, :HALF_W], qkv_total[32:48, HALF_W:]], axis=0)
    g_qkv = jnp.stack([pairs[:, :HALF_W], pairs[:, HALF_W:], value_grad], axis=1)

    def by_micro(first, second):
        own = jnp.where(is_first, first, second)
        came = swap(jnp.where(is_first, second, first), "section")
        return jnp.stack([jnp.where(is_first, own, came), jnp.where(is_first, came, own)])

    return (
        by_micro(out0, out1)[None],
        by_micro(grad_x0, grad_x1)[None],
        g_qkv[None],
        out_total[None],
        g_fc1[None],
        g_fc2[None],
        g_gains[None],
        g_shifts[None],
        g_scales[None],
        g_qv[None],
        g_fc1_bias[None],
    )


def solution(mesh):
    in_specs = (
        P(None, ("tensor", "wide"), None),
        P(None, ("tensor", "wide"), None),
        P(),
        P("section", "wide", None, "tensor"),
        P("section", ("tensor", "wide"), None),
        P("section", "wide", "tensor"),
        P("section", ("tensor", "wide"), None),
        P("section", None, "wide"),
        P("section", None, "wide"),
        P("section", None, "wide"),
        P("section", None, ("tensor", "wide")),
        P("section", ("tensor", "wide")),
    )
    out_specs = (
        P("section", None, ("tensor", "wide"), None),
        P("section", None, ("tensor", "wide"), None),
        P("section", "wide", None, "tensor"),
        P("section", ("tensor", "wide"), None),
        P("section", "wide", "tensor"),
        P("section", ("tensor", "wide"), None),
        P("section", None, "wide"),
        P("section", None, "wide"),
        P("section", None, "wide"),
        P("section", None, ("tensor", "wide")),
        P("section", ("tensor", "wide")),
    )
    return jax.shard_map(body, mesh=mesh, in_specs=in_specs, out_specs=out_specs, check_vma=False)
```
